32 devices in a mesh: tm: 16 (over z, y, x), head: 2 (over core).
Axes of the slice: x: 2, y: 2, z: 4, core: 2. Of those that a mesh axis runs over, the one named last changes fastest.
Arguments:
- query: bfloat16 [8192, 5120], P('tm', 'head'), may hold values from -100 to 100
- key: bfloat16 [8192, 5120], P('tm', 'head'), may hold values from -100 to 100
- value: bfloat16 [8192, 5120], P('tm', 'head'), may hold values from -6 to 6
- q_gain: float32 [5120], P('head'), may hold values from 0.1 to 1.9
- k_gain: float32 [5120], P('head'), may hold values from 0.1 to 1.9
- far_frames: int32 [128, 12], replicated, may hold values from -1 to 15, as said below
- far_pick: int32 [16, 16], replicated, may hold values from 0 to 7
Outputs:
- attended: bfloat16 [8192, 5120], P('tm', 'head')
The draws below stay inside these ranges and needn't reach their ends.
Inputs may be any that keep to these rules, and one draw needn't show every extreme that they name: `far_frames`: for query block r of frame f, entry j - 1 (j = 1 to 6) is a frame f - d and entry 5 + j a frame f + d, with 2**j <= d < 2**(j+1), or -1 where no frame of the video lies at such a distance on that side. In the first query block of each frame every such entry is the farthest frame that the band allows on that side.
All inputs are finite; a program needn't handle non-finite values.
Results may differ from the reference program's by a relative error of at most 0.012.
The reference program's roundings to bfloat16 on the way count: a program that leaves them out, or rounds other values in their place, can miss the bound.
Values may be sent and summed in bfloat16 or wider, within the bound.
No kernel may reach another device: no remote copies, remote signals or barrier semaphores. Data moves between devices by JAX's collectives and lax.ppermute only.
A program may use at most 128 MiB of HBM per device.

```python
import jax
import jax.numpy as jnp
from jax import lax

HEADS = 40
HEAD_DIM = 128
D = 5120
TOK_FRAME = 512
BLOCK = 64
NFAR = 12
FRAMES = 16
TOKENS = 8192


def spread_rows(key):
    row_key, col_key, base_key = jax.random.split(key, 3)
    row_scale = jnp.exp(jax.random.uniform(row_key, (TOKENS, 1), jnp.float32, 0.0, 2.3))
    col_scale = jnp.exp(jax.random.uniform(col_key, (1, D), jnp.float32, 0.0, 2.3))
    base = jax.random.truncated_normal(base_key, -3.0, 3.0, (TOKENS, D), jnp.float32)
    return base * row_scale * col_scale / 3.0


def draw_query(key, part):
    key = jax.random.fold_in(key, 1)
    values = spread_rows(key)
    return values.astype(jnp.bfloat16)


def draw_key(key, part):
    key = jax.random.fold_in(key, 2)
    values = spread_rows(key)
    return values.astype(jnp.bfloat16)


def draw_far_frames(key, part):
    key = jax.random.fold_in(key, 3)
    block_total = TOKENS // BLOCK
    per_frame = TOK_FRAME // BLOCK
    frame = jnp.arange(block_total, dtype=jnp.int32) // per_frame
    first_block = (jnp.arange(block_total, dtype=jnp.int32) % per_frame == 0)[:, None]
    raw = jax.random.randint(key, (block_total, NFAR), 0, 2 ** 20, jnp.int32)
    half_slots = NFAR // 2
    slot = jnp.arange(NFAR, dtype=jnp.int32)
    band = slot % half_slots + 1
    side = jnp.where(slot < half_slots, -1, 1)
    lowest = jnp.left_shift(1, band)[None, :]
    highest = 2 * lowest - 1
    reach = jnp.where(side[None, :] < 0, frame[:, None], FRAMES - 1 - frame[:, None])
    upper = jnp.minimum(highest, reach)
    width_band = upper - lowest + 1
    distance = lowest + raw % jnp.maximum(width_band, 1)
    distance = jnp.where(first_block, upper, distance)
    target = frame[:, None] + side[None, :] * distance
    return jnp.where(width_band > 0, target, -1).astype(jnp.int32)


def draw_far_pick(key, part):
    key = jax.random.fold_in(key, 5)
    return jax.random.randint(key, (FRAMES, FRAMES), 0, TOK_FRAME // BLOCK, jnp.int32)


def levels(rng, shape, shards, low, high):
    loudness = 1.0
    for position, blocks in shards:
        heights = jax.random.uniform(jax.random.fold_in(jax.random.fold_in(rng, 6), position), (blocks,), jnp.float32, low / len(shards), high / len(shards))
        loudness = loudness * jnp.repeat(jnp.exp(heights), shape[position] // blocks).reshape((-1,) + (1,) * (len(shape) - 1 - position))
    return loudness


def centred(own_key, extent, scale, most, cuts=(), kind=jnp.bfloat16):
    drawn = jax.random.normal(own_key, extent, jnp.float32) * scale
    if len(cuts) > 0:
        drawn = levels(own_key, extent, cuts, -0.22, 0.18) * drawn
    return jnp.clip(drawn, min=-most, max=most).astype(kind)


def setup_inputs(seed: int = 0) -> dict:
    keys = jax.random.split(jax.random.key(seed), 8)
    return {
        "query": draw_query(jax.random.fold_in(keys[7], 71), 0),
        "key": draw_key(jax.random.fold_in(keys[7], 71), 0),
        "value": centred(keys[2], (TOKENS, D), 1.0, 6.0, ((0, 16), (1, 2))),
        "q_gain": jnp.clip(1.0 + 0.18 * jax.random.normal(keys[3], (D,), jnp.float32), 0.1, 1.9),
        "k_gain": jnp.clip(1.0 + 0.18 * jax.random.normal(keys[4], (D,), jnp.float32), 0.1, 1.9),
        "far_frames": draw_far_frames(jax.random.fold_in(keys[7], 71), 0),
        "far_pick": draw_far_pick(jax.random.fold_in(keys[7], 71), 0),
    }


epsilon = 1e-06
masked = -1e+30

def normalize(values, gain):
    squares = lax.optimization_barrier(jnp.sum(jnp.square(values.astype(jnp.float32)), axis=1))
    scaled = values.astype(jnp.float32) * lax.rsqrt(squares / D + epsilon)[:, None] * gain[None, :]
    return scaled.astype(jnp.bfloat16)

def reference(query, key, value, q_gain, k_gain, far_frames, far_pick):
    q_norm = normalize(query, q_gain)
    k_norm = normalize(key, k_gain)
    frame_count = TOKENS // TOK_FRAME
    block_count = TOK_FRAME // BLOCK
    key_pad = jnp.pad(k_norm, ((TOK_FRAME, TOK_FRAME), (0, 0)))
    value_pad = jnp.pad(value, ((TOK_FRAME, TOK_FRAME), (0, 0)))
    score_scale = HEAD_DIM ** (-0.5)

    def one_frame(frame):
        q_rows = lax.dynamic_slice_in_dim(q_norm, frame * TOK_FRAME, TOK_FRAME, 0).astype(jnp.float32)
        q_rows = q_rows.reshape(TOK_FRAME, HEADS, HEAD_DIM)
        near_key = lax.dynamic_slice_in_dim(key_pad, frame * TOK_FRAME, 3 * TOK_FRAME, 0).astype(jnp.float32)
        near_key = near_key.reshape(3 * TOK_FRAME, HEADS, HEAD_DIM)
        near_value = lax.dynamic_slice_in_dim(value_pad, frame * TOK_FRAME, 3 * TOK_FRAME, 0).astype(jnp.float32)
        near_value = near_value.reshape(3 * TOK_FRAME, HEADS, HEAD_DIM)
        key_frame = frame - 1 + jnp.arange(3 * TOK_FRAME) // TOK_FRAME
        near_ok = (key_frame >= 0) & (key_frame < frame_count)
        lists = lax.dynamic_slice_in_dim(far_frames, frame * block_count, block_count, 0)
        list_ok = lists >= 0
        sources = jnp.maximum(lists, 0).astype(jnp.int32)
        pick_row = lax.dynamic_index_in_dim(far_pick, frame, 0, keepdims=False)
        picked = jnp.take(pick_row, sources)
        offsets = (sources * TOK_FRAME + picked * BLOCK)[:, :, None] + jnp.arange(BLOCK)[None, None, :]
        offsets = offsets.reshape(block_count, NFAR * BLOCK).astype(jnp.int32)
        far_key = jnp.take(k_norm, offsets, axis=0).astype(jnp.float32)
        far_key = far_key.reshape(block_count, NFAR * BLOCK, HEADS, HEAD_DIM)
        far_value = jnp.take(value, offsets, axis=0).astype(jnp.float32)
        far_value = far_value.reshape(block_count, NFAR * BLOCK, HEADS, HEAD_DIM)
        far_ok = jnp.repeat(list_ok, BLOCK, axis=1)
        near_score = jnp.einsum('qhd,khd->hqk', q_rows, near_key) * score_scale
        near_score = jnp.where(near_ok[None, None, :], near_score, masked)
        near_score = near_score.reshape(HEADS, block_count, BLOCK, 3 * TOK_FRAME)
        q_blocks = q_rows.reshape(block_count, BLOCK, HEADS, HEAD_DIM)
        far_score = jnp.einsum('bqhd,bkhd->hbqk', q_blocks, far_key) * score_scale
        far_score = jnp.where(far_ok[None, :, None, :], far_score, masked)
        row_peak = jnp.maximum(near_score.max(-1), far_score.max(-1))[..., None]
        near_prob = jnp.exp(near_score - row_peak)
        far_prob = jnp.exp(far_score - row_peak)
        prob_sum = near_prob.sum(-1) + far_prob.sum(-1)
        near_weight = lax.optimization_barrier(near_prob.astype(jnp.bfloat16)).astype(jnp.float32)
        far_weight = lax.optimization_barrier(far_prob.astype(jnp.bfloat16)).astype(jnp.float32)
        near_out = jnp.einsum('hbqk,khd->bqhd', near_weight, near_value)
        far_out = jnp.einsum('hbqk,bkhd->bqhd', far_weight, far_value)
        divisor = jnp.transpose(prob_sum, (1, 2, 0))[..., None]
        result = ((near_out + far_out) / divisor).astype(jnp.bfloat16)
        return result.reshape(TOK_FRAME, D)
    return lax.map(one_frame, jnp.arange(frame_count)).reshape(TOKENS, D)
```

```python
import functools
import math

import jax
import jax.numpy as jnp
from jax import lax
from jax.experimental import pallas as pl
from jax.experimental.pallas import tpu as pltpu
from jax.sharding import PartitionSpec as P

HEAD_DIM = 128
BLOCK = 64
NFAR = 12
EPSILON = 1e-06
MASKED = -1e30
VMEM_LIMIT = 56 * 1024 * 1024


class Plan:
    def __init__(self, frames, rows, heads):
        self.frames, self.rows = frames, rows
        self.group = 4 if heads % 4 == 0 and frames % 4 == 0 else 1
        self.planes = frames // self.group
        self.blocks = rows // BLOCK
        self.heads = heads // self.group
        self.chunks = [1] + [2] * ((self.heads - 1) // 2) + [1] * ((self.heads - 1) % 2)
        bands = sum(2**band <= frames - 1 for band in range(1, NFAR // 2 + 1))
        self.slots = [*range(bands), *range(NFAR // 2, NFAR // 2 + bands)]
        self.by_shift = 2 <= self.planes <= 8
        if self.by_shift:
            self.shifts = [s for d in range(1, self.planes) for s in (d, -d)]
        else:
            self.shifts = [1, -1]
        square = self.group * self.group
        side = self.group * (self.group - 1) if self.by_shift else 0
        self.near0 = side + self.blocks
        self.region = {1: (0, side + self.blocks)}
        after = self.near0 + self.group * self.blocks
        self.region[-1] = (after, self.blocks + side)
        after += self.blocks + side
        if self.by_shift:
            for s in self.shifts[2:]:
                self.region[s] = (after, square)
                after += square
        else:
            self.region[0] = (after, self.planes * square)
            after += self.planes * square
        self.total = after

    def line(self, shift):
        step = shift * self.group
        return [(i, i + step) for i in range(self.frames) if 0 <= i + step < self.frames]

    def sharers(self):
        g = self.group
        return [[p * g + i for i in range(g)] for p in range(self.planes)]

    def lines(self):
        g = self.group
        return [[p * g + i for p in range(self.planes)] for i in range(g)]


def norm_body(plan, q_ref, k_ref, v_ref, q_rs, k_rs, q_gain, k_gain, q_out, *kv_out):
    q = q_ref[...].astype(jnp.float32) * q_rs[...] * q_gain[...]
    q_out[0] = q.astype(jnp.bfloat16)
    k = (k_ref[...].astype(jnp.float32) * k_rs[...] * k_gain[...]).astype(jnp.bfloat16)
    start = 0
    for width, out in zip(plan.chunks, kv_out):
        stop = start + width * HEAD_DIM
        out[0, 0] = k[:, start:stop]
        out[0, 1] = v_ref[:, start:stop]
        start = stop


def normalize(plan, query, key, value, q_rs, k_rs, q_gain, k_gain):
    rows, width = query.shape
    part = width // plan.group
    tile = pl.BlockSpec((rows, part), lambda g: (0, g))
    column = pl.BlockSpec((rows, 1), lambda g: (0, 0))
    gain = pl.BlockSpec((1, part), lambda g: (0, g))
    shapes = [jax.ShapeDtypeStruct((plan.group, rows, part), jnp.bfloat16)]
    specs = [pl.BlockSpec((1, rows, part), lambda g: (g, 0, 0))]
    for heads in plan.chunks:
        wide = heads * HEAD_DIM
        shapes.append(jax.ShapeDtypeStruct((plan.group, 2, rows, wide), jnp.bfloat16))
        specs.append(pl.BlockSpec((1, 2, rows, wide), lambda g: (g, 0, 0, 0)))
    return pl.pallas_call(
        functools.partial(norm_body, plan),
        grid=(plan.group,),
        in_specs=[tile, tile, tile, column, column, gain, gain],
        out_specs=specs,
        out_shape=shapes,
        compiler_params=pltpu.CompilerParams(vmem_limit_bytes=VMEM_LIMIT),
        name="norm",
    )(query, key, value, q_rs, k_rs, q_gain, k_gain)


def pack_body(plan, plane_ref, pick_ref, kv_ref, *refs):
    outs, sem = refs[:-1], refs[-1]
    plane = plane_ref[0]
    group, rows = plan.group, plan.rows

    def block(dest, f, g):
        return pick_ref[(dest * group + f) * plan.frames + plane * group + g]

    def copies(index):
        made = []

        def add(g, src, dst, size):
            made.append(
                pltpu.make_async_copy(
                    kv_ref.at[g, :, pl.ds(pl.multiple_of(src, BLOCK), size), :],
                    outs[index].at[:, pl.ds(dst, size), :],
                    sem.at[index, len(made)],
                )
            )

        if not plan.by_shift:
            for dest in range(plan.planes):
                for f in range(group):
                    for g in range(group):
                        slot = (dest * group + f) * group + g
                        add(g, block(dest, f, g) * BLOCK, slot * BLOCK, BLOCK)
            return made
        shift = plan.shifts[index]
        dest = jnp.clip(plane + shift, 0, plan.planes - 1)
        skip = {1: group - 1, -1: 0}.get(shift)
        slot = 0
        if shift == -1:
            add(0, 0, 0, rows)
            slot = plan.blocks
        for f in range(group):
            for g in range(group):
                if g != skip:
                    add(g, block(dest, f, g) * BLOCK, slot * BLOCK, BLOCK)
                    slot += 1
        if shift == 1:
            add(group - 1, 0, slot * BLOCK, rows)
        return made

    def for_each(act):
        for index in range(len(outs)):
            if plan.by_shift:
                dest = plane + plan.shifts[index]

                @pl.when((dest >= 0) & (dest < plan.planes))
                def _(index=index):
                    for copy in copies(index):
                        act(copy)
            else:
                for copy in copies(index):
                    act(copy)

    for_each(lambda copy: copy.start())
    for_each(lambda copy: copy.wait())


def pack(plan, plane, picks, kv):
    width = kv.shape[-1]
    if plan.by_shift:
        sizes = [plan.region[s][1] for s in plan.shifts]
    else:
        sizes = [plan.region[0][1]]
    return pl.pallas_call(
        functools.partial(pack_body, plan),
        in_specs=[
            pl.BlockSpec(memory_space=pltpu.SMEM),
            pl.BlockSpec(memory_space=pltpu.SMEM),
            pl.BlockSpec(memory_space=pl.ANY),
        ],
        out_specs=[pl.BlockSpec(memory_space=pl.ANY)] * len(sizes),
        out_shape=[jax.ShapeDtypeStruct((2, n * BLOCK, width), kv.dtype) for n in sizes],
        scratch_shapes=[pltpu.SemaphoreType.DMA((len(sizes), max(sizes)))],
        compiler_params=pltpu.CompilerParams(vmem_limit_bytes=VMEM_LIMIT),
        name="pack",
    )(plane, picks, kv)


def attend_body(plan, offset, heads, order, plane_ref, pos_ref, q_ref, kv_ref, *refs):
    recvs = refs[: len(order)]
    out_ref, qbuf, kvbuf, fark, farv, sem = refs[len(order) :]
    group, rows, nfar = plan.group, plan.rows, len(plan.slots)
    plane = plane_ref[0]
    scale = math.log2(math.e) / math.sqrt(HEAD_DIM)
    tile = min(rows, 256)
    per_tile = tile // BLOCK

    def copies(h, slot):
        start = pl.multiple_of(h * HEAD_DIM, HEAD_DIM)
        cols = pl.ds(start, HEAD_DIM)
        q_cols = pl.ds(pl.multiple_of(start + offset * HEAD_DIM, HEAD_DIM), HEAD_DIM)
        made = [pltpu.make_async_copy(q_ref.at[:, :, q_cols], qbuf.at[slot], sem.at[slot, 0])]
        for g in range(group):
            place = pl.ds((plan.near0 + g * plan.blocks) * BLOCK, rows)
            made.append(
                pltpu.make_async_copy(
                    kv_ref.at[g, :, :, cols], kvbuf.at[slot, :, place, :], sem.at[slot, 1 + g]
                )
            )
        for index, name in enumerate(order):
            first, count = plan.region[name]
            place = pl.ds(first * BLOCK, count * BLOCK)
            made.append(
                pltpu.make_async_copy(
                    recvs[index].at[:, :, cols],
                    kvbuf.at[slot, :, place, :],
                    sem.at[slot, 1 + group + index],
                )
            )
        return made

    for copy in copies(0, 0):
        copy.start()

    lanes = lax.broadcasted_iota(jnp.int32, (1, nfar * BLOCK), 1) // BLOCK
    contract = (((1,), (1,)), ((), ()))

    def one_frame(h, slot, f):
        first = pl.multiple_of((plan.near0 + (f - 1) * plan.blocks) * BLOCK, BLOCK)
        frame = plane * group + f
        for t in range(rows // tile):
            q = qbuf[slot, f, t * tile : (t + 1) * tile, :]
            scores = []
            for part, ok in enumerate((frame > 0, None, frame < plan.frames - 1)):
                k = kvbuf[slot, 0, pl.ds(first + part * rows, rows), :]
                s = lax.dot_general(q, k, contract, preferred_element_type=jnp.float32)
                scores.append(s if ok is None else jnp.where(ok, s, MASKED))
            far = []
            for i in range(per_tile):
                row = f * plan.blocks + t * per_tile + i
                ok = lanes < 0
                for n in range(nfar):
                    at = pos_ref[row * nfar + n]
                    src = pl.ds(pl.multiple_of(jnp.maximum(at, 0) * BLOCK, BLOCK), BLOCK)
                    fark[t * per_tile + i, n * BLOCK : (n + 1) * BLOCK, :] = kvbuf[slot, 0, src, :]
                    farv[t * per_tile + i, n * BLOCK : (n + 1) * BLOCK, :] = kvbuf[slot, 1, src, :]
                    ok = ok | ((lanes == n) & (at >= 0))
                s = lax.dot_general(
                    q[i * BLOCK : (i + 1) * BLOCK],
                    fark[t * per_tile + i],
                    contract,
                    preferred_element_type=jnp.float32,
                )
                far.append(jnp.where(ok, s, MASKED))
            far = jnp.concatenate(far, axis=0)
            peak = jnp.max(far, axis=1, keepdims=True)
            for s in scores:
                peak = jnp.maximum(peak, jnp.max(s, axis=1, keepdims=True))
            total, out = 0.0, 0.0
            for part, s in enumerate(scores):
                p = jnp.exp2((s - peak) * scale)
                total += jnp.sum(p, axis=1, keepdims=True)
                v = kvbuf[slot, 1, pl.ds(first + part * rows, rows), :]
                out += jnp.dot(p.astype(jnp.bfloat16), v, preferred_element_type=jnp.float32)
            p = jnp.exp2((far - peak) * scale)
            total += jnp.sum(p, axis=1, keepdims=True)
            p = p.astype(jnp.bfloat16)
            far_out = [
                jnp.dot(
                    p[i * BLOCK : (i + 1) * BLOCK],
                    farv[t * per_tile + i],
                    preferred_element_type=jnp.float32,
                )
                for i in range(per_tile)
            ]
            out = (out + jnp.concatenate(far_out, axis=0)) / total
            cols = pl.ds(pl.multiple_of(h * HEAD_DIM, HEAD_DIM), HEAD_DIM)
            out_ref[f, t * tile : (t + 1) * tile, cols] = out.astype(jnp.bfloat16)

    def one_head(h, carry):
        slot = h % 2
        for copy in copies(h, slot):
            copy.wait()

        @pl.when(h + 1 < heads)
        def _():
            for copy in copies(h + 1, 1 - slot):
                copy.start()

        lax.fori_loop(0, group, lambda f, c: (one_frame(h, slot, f), c)[1], 0)
        return carry

    lax.fori_loop(0, heads, one_head, 0)


def attend(plan, offset, heads, plane, pos, q, kv, recv):
    order = list(recv)
    nfar = len(plan.slots)
    any_spec = pl.BlockSpec(memory_space=pl.ANY)
    smem = pl.BlockSpec(memory_space=pltpu.SMEM)
    return pl.pallas_call(
        functools.partial(attend_body, plan, offset, heads, order),
        in_specs=[smem, smem, any_spec, any_spec] + [any_spec] * len(order),
        out_specs=pl.BlockSpec(memory_space=pltpu.VMEM),
        out_shape=jax.ShapeDtypeStruct((plan.group, plan.rows, heads * HEAD_DIM), jnp.bfloat16),
        scratch_shapes=[
            pltpu.VMEM((2, plan.group, plan.rows, HEAD_DIM), jnp.bfloat16),
            pltpu.VMEM((2, 2, plan.total * BLOCK, HEAD_DIM), jnp.bfloat16),
            pltpu.VMEM((plan.blocks, nfar * BLOCK, HEAD_DIM), jnp.bfloat16),
            pltpu.VMEM((plan.blocks, nfar * BLOCK, HEAD_DIM), jnp.bfloat16),
            pltpu.SemaphoreType.DMA((2, 1 + plan.group + len(order))),
        ],
        compiler_params=pltpu.CompilerParams(vmem_limit_bytes=VMEM_LIMIT),
        name="attend",
    )(plane, pos, q, kv, *recv.values())


def far_positions(plan, plane, far_frames, far_pick):
    group, blocks = plan.group, plan.blocks
    own = group * blocks
    lists = lax.dynamic_slice_in_dim(far_frames, plane * own, own, 0)
    lists = jnp.concatenate([lists[:, s : s + 1] for s in plan.slots], axis=1)
    g = jnp.maximum(lists, 0)
    rows = lax.dynamic_slice_in_dim(far_pick, plane * group, group, 0)
    rows = jnp.repeat(rows, blocks, axis=0)
    hit = g[:, :, None] == jnp.arange(plan.frames)
    pick = jnp.sum(jnp.where(hit, rows[:, None, :], 0), axis=2)
    f = (jnp.arange(own) // blocks)[:, None]
    source, lane = g // group, g % group
    if plan.by_shift:
        pos = jnp.zeros_like(g)
        for s in plan.shifts:
            base = plan.region[s][0]
            if s == 1:
                at = base + f * (group - 1) + lane
            elif s == -1:
                at = base + blocks + f * (group - 1) + lane - 1
            else:
                at = base + f * group + lane
            pos = jnp.where(plane - source == s, at, pos)
    else:
        pos = plan.region[0][0] + (source * group + f) * group + lane
    away = g - plane * group
    near = (away >= -1) & (away <= group)
    pos = jnp.where(near, plan.near0 + away * blocks + pick, pos)
    return jnp.where(lists >= 0, pos, -1).astype(jnp.int32).reshape(-1)


def local(query, key, value, q_gain, k_gain, far_frames, far_pick):
    rows, width = query.shape
    full_width = width * lax.axis_size("head")
    plan = Plan(lax.axis_size("tm"), rows, width // HEAD_DIM)
    plane = lax.axis_index("tm") // plan.group
    plane_arg = plane.astype(jnp.int32).reshape(1)
    sums = jnp.stack(
        [jnp.sum(jnp.square(x.astype(jnp.float32)), axis=1) for x in (query, key)]
    )
    rs = lax.rsqrt(lax.psum(sums, "head") / full_width + EPSILON)[:, :, None]
    q, *kvs = normalize(
        plan, query, key, value, rs[0], rs[1], q_gain[None, :], k_gain[None, :]
    )
    picks = far_pick.reshape(-1)
    pos = far_positions(plan, plane, far_frames, far_pick)

    def share(x):
        if plan.group == 1:
            return x
        return lax.all_to_all(
            x, "tm", 0, 0, axis_index_groups=plan.sharers(), tiled=True
        )

    def exchange(kv):
        sent = pack(plan, plane_arg, picks, kv)
        if plan.by_shift:
            return {
                s: lax.ppermute(x, "tm", plan.line(s)) for s, x in zip(plan.shifts, sent)
            }
        far = sent[0].reshape(2, plan.planes, -1, kv.shape[-1])
        far = lax.all_to_all(
            far, "tm", 1, 1, axis_index_groups=plan.lines(), tiled=True
        )
        return {
            1: lax.ppermute(kv[plan.group - 1], "tm", plan.line(1)),
            -1: lax.ppermute(kv[0], "tm", plan.line(-1)),
            0: far.reshape(sent[0].shape),
        }

    kvs = [share(kvs[0])] + kvs[1:]
    recvs = [exchange(kvs[0])]
    for c in range(1, len(kvs)):
        kvs[c] = share(kvs[c])
        recvs.append(exchange(kvs[c]))
    q = share(q)
    outs, offset = [], 0
    for heads, kv, recv in zip(plan.chunks, kvs, recvs):
        out = attend(plan, offset, heads, plane_arg, pos, q, kv, recv)
        outs.append(share(out))
        offset += heads
    merged = jnp.concatenate(outs, axis=2)
    return jnp.transpose(merged, (1, 0, 2)).reshape(rows, width)


def solution(mesh):
    placed = (P("tm", "head"), P("tm", "head"), P("tm", "head"), P("head"), P("head"), P(), P())
    return jax.shard_map(
        local, mesh=mesh, in_specs=placed, out_specs=P("tm", "head"), check_vma=False
    )
```

```python
import functools
import math

import jax
import jax.numpy as jnp
from jax import lax
from jax.experimental import pallas as pl
from jax.experimental.pallas import tpu as pltpu
from jax.sharding import PartitionSpec as P

HEAD_DIM = 128
BLOCK = 64
NFAR = 12
EPSILON = 1e-06
MASKED = -1e30
VMEM_LIMIT = 56 * 1024 * 1024


class Plan:
    def __init__(self, frames, rows, heads):
        self.frames, self.rows = frames, rows
        self.group = 4 if heads % 4 == 0 and frames % 4 == 0 else 1
        self.planes = frames // self.group
        self.blocks = rows // BLOCK
        self.heads = heads // self.group
        self.key_parts = [n for n in (1, self.heads - 1) if n]
        self.value_parts = [n for n in (min(2, self.heads), self.heads - 2) if n > 0]
        bands = sum(2**band <= frames - 1 for band in range(1, NFAR // 2 + 1))
        self.slots = [*range(bands), *range(NFAR // 2, NFAR // 2 + bands)]
        square = self.group * self.group
        self.near0 = self.blocks
        after = self.blocks * (self.group + 2)
        self.matched = 2 <= self.planes <= 8
        self.links, self.base, self.far = [], {}, {}
        if self.matched:
            for d in range(1, self.planes):
                for odd in (0, 1):
                    if any((p // d) % 2 == odd for p in range(self.planes - d)):
                        link = (d, odd)
                        self.links.append(link)
                        self.base[link] = after
                        self.far[link] = square - self.group if d == 1 else square
                        after += self.far[link]
        else:
            self.base[None] = after
            after += self.planes * square
        self.total = after

    def size(self, link):
        return self.far[link] + (self.blocks if link[0] == 1 else 0)

    def above(self, link, plane):
        d, odd = link
        return (plane // d) % 2 == odd

    def pairs(self, link):
        d, _ = link
        step = d * self.group
        made = []
        for i in range(self.frames - step):
            if self.above(link, i // self.group):
                made += [(i, i + step), (i + step, i)]
        return made

    def halo(self, step):
        return [(i, i + step) for i in range(self.frames) if 0 <= i + step < self.frames]

    def sharers(self):
        g = self.group
        return [[p * g + i for i in range(g)] for p in range(self.planes)]

    def lines(self):
        g = self.group
        return [[p * g + i for p in range(self.planes)] for i in range(g)]


def norm_body(n_after, q_ref, k_ref, q_rs, k_rs, q_gain, k_gain, *refs):
    q_out, *k_out = refs[n_after:]
    q = q_ref[...].astype(jnp.float32) * q_rs[...] * q_gain[...]
    q_out[0] = q.astype(jnp.bfloat16)
    k = (k_ref[...].astype(jnp.float32) * k_rs[...] * k_gain[...]).astype(jnp.bfloat16)
    split_columns(k, k_out)


def split_columns(x, outs):
    start = 0
    for out in outs:
        stop = start + out.shape[-1]
        out[0] = x[:, start:stop]
        start = stop


def split_body(x_ref, *outs):
    split_columns(x_ref[...], outs)


def shares(plan, widths):
    shapes, specs = [], []
    for heads in widths:
        wide = heads * HEAD_DIM
        shapes.append(jax.ShapeDtypeStruct((plan.group, plan.rows, wide), jnp.bfloat16))
        specs.append(pl.BlockSpec((1, plan.rows, wide), lambda g: (g, 0, 0)))
    return shapes, specs


def split(plan, x, widths):
    shapes, specs = shares(plan, widths)
    return pl.pallas_call(
        split_body,
        grid=(plan.group,),
        in_specs=[pl.BlockSpec((plan.rows, plan.heads * HEAD_DIM), lambda g: (0, g))],
        out_specs=specs,
        out_shape=shapes,
        compiler_params=pltpu.CompilerParams(vmem_limit_bytes=VMEM_LIMIT),
        name="split",
    )(x)


def normalize(plan, query, key, q_rs, k_rs, q_gain, k_gain, after):
    part = plan.heads * HEAD_DIM
    tile = pl.BlockSpec((plan.rows, part), lambda g: (0, g))
    column = pl.BlockSpec((plan.rows, 1), lambda g: (0, 0))
    gain = pl.BlockSpec((1, part), lambda g: (0, g))
    shapes, specs = shares(plan, [plan.heads] + plan.key_parts)
    return pl.pallas_call(
        functools.partial(norm_body, len(after)),
        grid=(plan.group,),
        in_specs=[tile, tile, column, column, gain, gain]
        + [pl.BlockSpec(memory_space=pl.ANY)] * len(after),
        out_specs=specs,
        out_shape=shapes,
        compiler_params=pltpu.CompilerParams(vmem_limit_bytes=VMEM_LIMIT),
        name="norm",
    )(query, key, q_rs, k_rs, q_gain, k_gain, *after)


def pack_body(plan, n_after, plane_ref, pick_ref, x_ref, *refs):
    outs, sem = refs[n_after:-1], refs[-1]
    plane = plane_ref[0]
    group, rows = plan.group, plan.rows

    def block(dest, f, g):
        return pick_ref[(dest * group + f) * plan.frames + plane * group + g]

    def copies(index):
        made = []

        def add(g, src, dst, size):
            made.append(
                pltpu.make_async_copy(
                    x_ref.at[g, pl.ds(pl.multiple_of(src, BLOCK), size), :],
                    outs[index].at[pl.ds(dst, size), :],
                    sem.at[index, len(made)],
                )
            )

        if not plan.matched:
            for dest in range(plan.planes):
                for f in range(group):
                    for g in range(group):
                        slot = (dest * group + f) * group + g
                        add(g, block(dest, f, g) * BLOCK, slot * BLOCK, BLOCK)
            return made
        link = plan.links[index]
        dest, up = partner(link)
        dest = jnp.clip(dest, 0, plan.planes - 1)
        near = link[0] == 1
        slot = 0
        for f in range(group):
            for g in range(group - near):
                if near:
                    g += jnp.where(up, 0, 1)
                add(g, block(dest, f, g) * BLOCK, slot * BLOCK, BLOCK)
                slot += 1
        if near:
            add(jnp.where(up, group - 1, 0), 0, slot * BLOCK, rows)
        return made

    def partner(link):
        up = plan.above(link, plane)
        return plane + jnp.where(up, link[0], -link[0]), up

    def for_each(act):
        for index in range(len(outs)):
            if plan.matched:
                dest, _ = partner(plan.links[index])

                @pl.when((dest >= 0) & (dest < plan.planes))
                def _(index=index):
                    for copy in copies(index):
                        act(copy)
            else:
                for copy in copies(index):
                    act(copy)

    for_each(lambda copy: copy.start())
    for_each(lambda copy: copy.wait())


def pack(plan, plane, picks, x, first, heads, after):
    width = heads * HEAD_DIM
    if plan.matched:
        sizes = [plan.size(link) for link in plan.links]
    else:
        sizes = [plan.planes * plan.group * plan.group]
    smem = pl.BlockSpec(memory_space=pltpu.SMEM)
    any_spec = pl.BlockSpec(memory_space=pl.ANY)
    return pl.pallas_call(
        functools.partial(pack_body, plan, len(after)),
        grid=(1,),
        in_specs=[
            smem,
            smem,
            pl.BlockSpec((plan.group, plan.rows, width), lambda i: (0, 0, first // heads)),
        ]
        + [any_spec] * len(after),
        out_specs=[any_spec] * len(sizes),
        out_shape=[jax.ShapeDtypeStruct((n * BLOCK, width), x.dtype) for n in sizes],
        scratch_shapes=[pltpu.SemaphoreType.DMA((len(sizes), max(sizes)))],
        compiler_params=pltpu.CompilerParams(vmem_limit_bytes=VMEM_LIMIT),
        name="pack",
    )(plane, picks, x, *after)


def attend_body(plan, order, at_q, at_k, at_v, plane_ref, pos_ref, q_ref, k_ref, v_ref, *refs):
    k_recvs = refs[: len(order)]
    v_recvs = refs[len(order) : 2 * len(order)]
    out_ref, qbuf, kbuf, vbuf, fark, farv, sem = refs[2 * len(order) :]
    group, rows, nfar = plan.group, plan.rows, len(plan.slots)
    plane = plane_ref[0]
    scale = math.log2(math.e) / math.sqrt(HEAD_DIM)
    tile = min(rows, 256)
    per_tile = tile // BLOCK

    def head(at):
        return slice(at * HEAD_DIM, (at + 1) * HEAD_DIM)

    copies = []

    def add(src, dst):
        copies.append(pltpu.make_async_copy(src, dst, sem.at[len(copies)]))

    add(q_ref.at[:, :, head(at_q)], qbuf)
    sources = ((k_ref, at_k[0], k_recvs, at_k[1], kbuf), (v_ref, at_v[0], v_recvs, at_v[1], vbuf))
    for ref, at, recvs, recv_at, buf in sources:

        def receive(index, src, first, count):
            first = first * BLOCK
            if not isinstance(first, int):
                first = pl.multiple_of(first, BLOCK)
            add(
                recvs[index].at[src * BLOCK : (src + count) * BLOCK, head(recv_at)],
                buf.at[pl.ds(first, count * BLOCK), :],
            )

        for g in range(group):
            place = pl.ds((plan.near0 + g * plan.blocks) * BLOCK, rows)
            add(ref.at[g, :, head(at)], buf.at[place, :])
        after = plan.near0 + group * plan.blocks
        for index, name in enumerate(order):
            if name in plan.links:
                count = plan.far[name]
                if count:
                    receive(index, 0, plan.base[name], count)
                if name[0] == 1:
                    up = plan.above(name, plane)
                    receive(index, count, jnp.where(up, after, 0), plan.blocks)
            elif name is None:
                receive(index, 0, plan.base[None], plan.total - plan.base[None])
            else:
                receive(index, 0, 0 if name == "before" else after, plan.blocks)
    for copy in copies:
        copy.start()
    for copy in copies:
        copy.wait()

    lanes = lax.broadcasted_iota(jnp.int32, (1, nfar * BLOCK), 1) // BLOCK
    contract = (((1,), (1,)), ((), ()))

    def one_frame(f, carry):
        first = pl.multiple_of((plan.near0 + (f - 1) * plan.blocks) * BLOCK, BLOCK)
        frame = plane * group + f
        for t in range(rows // tile):
            q = qbuf[f, t * tile : (t + 1) * tile, :]
            scores = []
            for part, ok in enumerate((frame > 0, None, frame < plan.frames - 1)):
                k = kbuf[pl.ds(first + part * rows, rows), :]
                s = lax.dot_general(q, k, contract, preferred_element_type=jnp.float32)
                scores.append(s if ok is None else jnp.where(ok, s, MASKED))
            far = []
            for i in range(per_tile):
                block = t * per_tile + i
                ok = lanes < 0
                for n in range(nfar):
                    at = pos_ref[(f * plan.blocks + block) * nfar + n]
                    src = pl.ds(pl.multiple_of(jnp.maximum(at, 0) * BLOCK, BLOCK), BLOCK)
                    fark[block, n * BLOCK : (n + 1) * BLOCK, :] = kbuf[src, :]
                    farv[block, n * BLOCK : (n + 1) * BLOCK, :] = vbuf[src, :]
                    ok = ok | ((lanes == n) & (at >= 0))
                s = lax.dot_general(
                    q[i * BLOCK : (i + 1) * BLOCK],
                    fark[block],
                    contract,
                    preferred_element_type=jnp.float32,
                )
                far.append(jnp.where(ok, s, MASKED))
            far = jnp.concatenate(far, axis=0)
            peak = jnp.max(far, axis=1, keepdims=True)
            for s in scores:
                peak = jnp.maximum(peak, jnp.max(s, axis=1, keepdims=True))
            total, out = 0.0, 0.0
            for part, s in enumerate(scores):
                p = jnp.exp2((s - peak) * scale)
                total += jnp.sum(p, axis=1, keepdims=True)
                v = vbuf[pl.ds(first + part * rows, rows), :]
                out += jnp.dot(p.astype(jnp.bfloat16), v, preferred_element_type=jnp.float32)
            p = jnp.exp2((far - peak) * scale)
            total += jnp.sum(p, axis=1, keepdims=True)
            p = p.astype(jnp.bfloat16)
            far_out = [
                jnp.dot(
                    p[i * BLOCK : (i + 1) * BLOCK],
                    farv[t * per_tile + i],
                    preferred_element_type=jnp.float32,
                )
                for i in range(per_tile)
            ]
            out = (out + jnp.concatenate(far_out, axis=0)) / total
            out_ref[f, t * tile : (t + 1) * tile, :] = out.astype(jnp.bfloat16)
        return carry

    lax.fori_loop(0, group, one_frame, 0)


def attend(plan, plane, pos, q, at_q, k, at_k, k_recv, v, at_v, v_recv):
    order = list(k_recv)
    nfar = len(plan.slots)
    any_spec = pl.BlockSpec(memory_space=pl.ANY)
    smem = pl.BlockSpec(memory_space=pltpu.SMEM)
    rows = plan.total * BLOCK
    return pl.pallas_call(
        functools.partial(attend_body, plan, order, at_q, at_k, at_v),
        in_specs=[smem, smem] + [any_spec] * (3 + 2 * len(order)),
        out_specs=pl.BlockSpec(memory_space=pltpu.VMEM),
        out_shape=jax.ShapeDtypeStruct((plan.group, plan.rows, HEAD_DIM), jnp.bfloat16),
        scratch_shapes=[
            pltpu.VMEM((plan.group, plan.rows, HEAD_DIM), jnp.bfloat16),
            pltpu.VMEM((rows, HEAD_DIM), jnp.bfloat16),
            pltpu.VMEM((rows, HEAD_DIM), jnp.bfloat16),
            pltpu.VMEM((plan.blocks, nfar * BLOCK, HEAD_DIM), jnp.bfloat16),
            pltpu.VMEM((plan.blocks, nfar * BLOCK, HEAD_DIM), jnp.bfloat16),
            pltpu.SemaphoreType.DMA((1 + 2 * (plan.group + 2 + len(order)),)),
        ],
        compiler_params=pltpu.CompilerParams(vmem_limit_bytes=VMEM_LIMIT),
        name="attend",
    )(plane, pos, q, k, v, *k_recv.values(), *v_recv.values())


def merge_body(x_ref, *refs):
    refs[-1][...] = x_ref[0]


def merge(plan, x, head, out):
    width = plan.group * plan.heads * HEAD_DIM
    return pl.pallas_call(
        merge_body,
        grid=(plan.group,),
        in_specs=[pl.BlockSpec((1, plan.rows, HEAD_DIM), lambda g: (g, 0, 0))]
        + [pl.BlockSpec(memory_space=pl.ANY)] * len(out),
        out_specs=pl.BlockSpec((plan.rows, HEAD_DIM), lambda g: (0, g * plan.heads + head)),
        out_shape=jax.ShapeDtypeStruct((plan.rows, width), x.dtype),
        input_output_aliases={1: 0} if out else {},
        compiler_params=pltpu.CompilerParams(vmem_limit_bytes=VMEM_LIMIT),
        name="merge",
    )(x, *out)


def far_positions(plan, plane, far_frames, far_pick):
    group, blocks = plan.group, plan.blocks
    own = group * blocks
    lists = lax.dynamic_slice_in_dim(far_frames, plane * own, own, 0)
    lists = jnp.concatenate([lists[:, s : s + 1] for s in plan.slots], axis=1)
    g = jnp.maximum(lists, 0)
    rows = lax.dynamic_slice_in_dim(far_pick, plane * group, group, 0)
    rows = jnp.repeat(rows, blocks, axis=0)
    hit = g[:, :, None] == jnp.arange(plan.frames)
    pick = jnp.sum(jnp.where(hit, rows[:, None, :], 0), axis=2)
    f = (jnp.arange(own) // blocks)[:, None]
    source, lane = g // group, g % group
    if plan.matched:
        pos = jnp.zeros_like(g)
        for link in plan.links:
            if link[0] == 1:
                at = f * (group - 1) + lane - jnp.where(source > plane, 1, 0)
            else:
                at = f * group + lane
            low = jnp.minimum(source, plane)
            hit = (jnp.abs(source - plane) == link[0]) & plan.above(link, low)
            pos = jnp.where(hit, plan.base[link] + at, pos)
    else:
        pos = plan.base[None] + (source * group + f) * group + lane
    away = g - plane * group
    near = (away >= -1) & (away <= group)
    pos = jnp.where(near, plan.near0 + away * blocks + pick, pos)
    return jnp.where(lists >= 0, pos, -1).astype(jnp.int32).reshape(-1)


def local(query, key, value, q_gain, k_gain, far_frames, far_pick):
    rows, width = query.shape
    full_width = width * lax.axis_size("head")
    plan = Plan(lax.axis_size("tm"), rows, width // HEAD_DIM)
    plane = lax.axis_index("tm") // plan.group
    plane_arg = plane.astype(jnp.int32).reshape(1)
    picks = far_pick.reshape(-1)

    def share(x):
        if plan.group == 1:
            return x
        return lax.all_to_all(x, "tm", 0, 0, axis_index_groups=plan.sharers(), tiled=True)

    def exchange(x, first, heads, after):
        sent = pack(plan, plane_arg, picks, x, first, heads, after)
        packed.append(sent)
        if plan.matched:
            return {n: lax.ppermute(y, "tm", plan.pairs(n)) for n, y in zip(plan.links, sent)}
        far = sent[0].reshape(plan.planes, -1, heads * HEAD_DIM)
        far = lax.all_to_all(far, "tm", 0, 0, axis_index_groups=plan.lines(), tiled=True)
        x = x[:, :, first * HEAD_DIM : (first + heads) * HEAD_DIM]
        return {
            "before": lax.ppermute(x[plan.group - 1], "tm", plan.halo(1)),
            "after": lax.ppermute(x[0], "tm", plan.halo(-1)),
            None: far.reshape(sent[0].shape),
        }

    packed, arrived = [], []

    def send(x, first, heads):
        after = list(arrived[-2].values()) if len(arrived) > 1 else []
        arrived.append(exchange(x, first, heads, after))
        return arrived[-1]

    vs = [share(x) for x in split(plan, value, plan.value_parts)]
    v_recvs = [send(vs[0], 0, plan.value_parts[0])]
    sums = jnp.stack([jnp.sum(jnp.square(x.astype(jnp.float32)), axis=1) for x in (query, key)])
    rs = lax.rsqrt(lax.psum(sums, "head") / full_width + EPSILON)[:, :, None]
    q, *ks = normalize(
        plan, query, key, rs[0], rs[1], q_gain[None, :], k_gain[None, :], packed[0][:1]
    )
    ks = [share(x) for x in ks]
    q = share(q)
    pos = far_positions(plan, plane, far_frames, far_pick)

    out, head = [], 0
    for part, (v, v_heads) in enumerate(zip(vs, plan.value_parts)):
        if part:
            v_recvs.append(send(v, 0, v_heads))
        for at_v in range(v_heads):
            late = head >= plan.key_parts[0]
            k, at_k = ks[late], head - late * plan.key_parts[0]
            k_recv = send(k, at_k, 1)
            x = attend(
                plan, plane_arg, pos, q, head, k, (at_k, 0), k_recv, v, (at_v, at_v), v_recvs[part]
            )
            out = [merge(plan, share(x), head, out)]
            head += 1
    return out[0]


def solution(mesh):
    placed = (P("tm", "head"), P("tm", "head"), P("tm", "head"), P("head"), P("head"), P(), P())
    return jax.shard_map(
        local, mesh=mesh, in_specs=placed, out_specs=P("tm", "head"), check_vma=False
    )
```

```python
import functools
import math

import jax
import jax.numpy as jnp
from jax import lax
from jax.experimental import pallas as pl
from jax.experimental.pallas import tpu as pltpu
from jax.sharding import PartitionSpec as P

HEAD_DIM = 128
BLOCK = 64
NFAR = 12
EPSILON = 1e-06
MASKED = -1e30
VMEM_LIMIT = 56 * 1024 * 1024


class Plan:
    def __init__(self, frames, rows, heads):
        self.frames, self.rows = frames, rows
        self.group = 4 if heads % 4 == 0 and frames % 4 == 0 else 1
        self.planes = frames // self.group
        self.blocks = rows // BLOCK
        self.heads = heads // self.group
        self.early = min(2, self.heads)
        bands = sum(2**band <= frames - 1 for band in range(1, NFAR // 2 + 1))
        self.slots = [*range(bands), *range(NFAR // 2, NFAR // 2 + bands)]
        square = self.group * self.group
        self.near0 = self.blocks
        after = self.blocks * (self.group + 2)
        self.matched = 2 <= self.planes <= 8
        self.links, self.base, self.far = [], {}, {}
        if self.matched:
            for d in range(1, self.planes):
                for odd in (0, 1):
                    if any((p // d) % 2 == odd for p in range(self.planes - d)):
                        link = (d, odd)
                        self.links.append(link)
                        self.base[link] = after
                        self.far[link] = square - self.group if d == 1 else square
                        after += self.far[link]
        else:
            self.base[None] = after
            after += self.planes * square
        self.total = after

    def size(self, link):
        return self.far[link] + (self.blocks if link[0] == 1 else 0)

    def above(self, link, plane):
        d, odd = link
        return (plane // d) % 2 == odd

    def pairs(self, link):
        d, _ = link
        step = d * self.group
        made = []
        for i in range(self.frames - step):
            if self.above(link, i // self.group):
                made += [(i, i + step), (i + step, i)]
        return made

    def halo(self, step):
        return [(i, i + step) for i in range(self.frames) if 0 <= i + step < self.frames]

    def sharers(self):
        g = self.group
        return [[p * g + i for i in range(g)] for p in range(self.planes)]

    def lines(self):
        g = self.group
        return [[p * g + i for p in range(self.planes)] for i in range(g)]


def params():
    return dict(
        compiler_params=pltpu.CompilerParams(vmem_limit_bytes=VMEM_LIMIT),
        cost_estimate=pl.CostEstimate(flops=1, bytes_accessed=1, transcendentals=0),
    )


def select_body(first, n_after, x_ref, *refs):
    out = refs[-1]
    cols = slice(first * HEAD_DIM, first * HEAD_DIM + out.shape[-1])
    x = x_ref[:, cols]
    if len(refs) > n_after + 1:
        rs, gain = refs[0], refs[1]
        x = x.astype(jnp.float32) * rs[...] * gain[:, cols]
    out[0] = x.astype(out.dtype)


def select(plan, x, first, heads, after, rs=None, gain=None):
    part = plan.heads * HEAD_DIM
    wide = heads * HEAD_DIM
    specs = [pl.BlockSpec((plan.rows, part), lambda g: (0, g))]
    extra = []
    if rs is not None:
        extra = [rs[:, None], gain[None, :]]
        specs.append(pl.BlockSpec((plan.rows, 1), lambda g: (0, 0)))
        specs.append(pl.BlockSpec((1, part), lambda g: (0, g)))
    return pl.pallas_call(
        functools.partial(select_body, first, len(after)),
        grid=(plan.group,),
        in_specs=specs + [pl.BlockSpec(memory_space=pl.ANY)] * len(after),
        out_specs=pl.BlockSpec((1, plan.rows, wide), lambda g: (g, 0, 0)),
        out_shape=jax.ShapeDtypeStruct((plan.group, plan.rows, wide), x.dtype),
        name="select",
        **params(),
    )(x, *extra, *after)


def pack_body(plan, n_after, plane_ref, pick_ref, x_ref, *refs):
    outs, sem = refs[n_after:-1], refs[-1]
    plane = plane_ref[0]
    group, rows = plan.group, plan.rows

    def block(dest, f, g):
        return pick_ref[(dest * group + f) * plan.frames + plane * group + g]

    def copies(index):
        made = []

        def add(g, src, dst, size):
            made.append(
                pltpu.make_async_copy(
                    x_ref.at[g, pl.ds(pl.multiple_of(src, BLOCK), size), :],
                    outs[index].at[pl.ds(dst, size), :],
                    sem.at[index, len(made)],
                )
            )

        if not plan.matched:
            for dest in range(plan.planes):
                for f in range(group):
                    for g in range(group):
                        slot = (dest * group + f) * group + g
                        add(g, block(dest, f, g) * BLOCK, slot * BLOCK, BLOCK)
            return made
        link = plan.links[index]
        dest, up = partner(link)
        dest = jnp.clip(dest, 0, plan.planes - 1)
        near = link[0] == 1
        slot = 0
        for f in range(group):
            for g in range(group - near):
                if near:
                    g += jnp.where(up, 0, 1)
                add(g, block(dest, f, g) * BLOCK, slot * BLOCK, BLOCK)
                slot += 1
        if near:
            add(jnp.where(up, group - 1, 0), 0, slot * BLOCK, rows)
        return made

    def partner(link):
        up = plan.above(link, plane)
        return plane + jnp.where(up, link[0], -link[0]), up

    def for_each(act):
        for index in range(len(outs)):
            if plan.matched:
                dest, _ = partner(plan.links[index])

                @pl.when((dest >= 0) & (dest < plan.planes))
                def _(index=index):
                    for copy in copies(index):
                        act(copy)
            else:
                for copy in copies(index):
                    act(copy)

    for_each(lambda copy: copy.start())
    for_each(lambda copy: copy.wait())


def pack(plan, plane, picks, x, first, heads, after):
    width = heads * HEAD_DIM
    if plan.matched:
        sizes = [plan.size(link) for link in plan.links]
    else:
        sizes = [plan.planes * plan.group * plan.group]
    smem = pl.BlockSpec(memory_space=pltpu.SMEM)
    any_spec = pl.BlockSpec(memory_space=pl.ANY)
    return pl.pallas_call(
        functools.partial(pack_body, plan, len(after)),
        grid=(1,),
        in_specs=[
            smem,
            smem,
            pl.BlockSpec((plan.group, plan.rows, width), lambda i: (0, 0, first // heads)),
        ]
        + [any_spec] * len(after),
        out_specs=[any_spec] * len(sizes),
        out_shape=[jax.ShapeDtypeStruct((n * BLOCK, width), x.dtype) for n in sizes],
        scratch_shapes=[pltpu.SemaphoreType.DMA((len(sizes), max(sizes)))],
        name="pack",
        **params(),
    )(plane, picks, x, *after)


def attend_body(plan, order, heads, n_after, at_q, at_k, at_v, *refs):
    plane_ref, pos_ref, q_ref, k_ref, v_ref = refs[:5]
    refs = refs[5:]
    k_recvs = refs[: len(order)]
    v_recvs = refs[len(order) : 2 * len(order)]
    out_ref, qbuf, kbuf, vbuf, fark, farv, sem = refs[2 * len(order) + n_after :]
    group, rows, nfar = plan.group, plan.rows, len(plan.slots)
    plane = plane_ref[0]
    scale = math.log2(math.e) / math.sqrt(HEAD_DIM)
    tile = min(rows, 256)
    per_tile = tile // BLOCK
    lanes = lax.broadcasted_iota(jnp.int32, (1, nfar * BLOCK), 1) // BLOCK
    contract = (((1,), (1,)), ((), ()))

    def head(at):
        return slice(at * HEAD_DIM, (at + 1) * HEAD_DIM)

    def copies(h):
        made, slot = [], h % 2

        def add(src, dst):
            made.append(pltpu.make_async_copy(src, dst, sem.at[slot, len(made)]))

        add(q_ref.at[:, :, head(at_q + h)], qbuf.at[slot])
        for ref, at, recvs, recv_at, buf in (
            (k_ref, at_k + h, k_recvs, h, kbuf),
            (v_ref, at_v + h, v_recvs, at_v + h, vbuf),
        ):

            def receive(index, src, first, count):
                first = first * BLOCK
                if not isinstance(first, int):
                    first = pl.multiple_of(first, BLOCK)
                add(
                    recvs[index].at[src * BLOCK : (src + count) * BLOCK, head(recv_at)],
                    buf.at[slot, pl.ds(first, count * BLOCK), :],
                )

            for g in range(group):
                place = pl.ds((plan.near0 + g * plan.blocks) * BLOCK, rows)
                add(ref.at[g, :, head(at)], buf.at[slot, place, :])
            after = plan.near0 + group * plan.blocks
            for index, name in enumerate(order):
                if name in plan.links:
                    count = plan.far[name]
                    if count:
                        receive(index, 0, plan.base[name], count)
                    if name[0] == 1:
                        up = plan.above(name, plane)
                        receive(index, count, jnp.where(up, after, 0), plan.blocks)
                elif name is None:
                    receive(index, 0, plan.base[None], plan.total - plan.base[None])
                else:
                    receive(index, 0, 0 if name == "before" else after, plan.blocks)
        return made

    def one_frame(f, h):
        slot = h % 2
        first = pl.multiple_of((plan.near0 + (f - 1) * plan.blocks) * BLOCK, BLOCK)
        frame = plane * group + f
        for t in range(rows // tile):
            q = qbuf[slot, f, t * tile : (t + 1) * tile, :]
            scores = []
            for part, ok in enumerate((frame > 0, None, frame < plan.frames - 1)):
                k = kbuf[slot, pl.ds(first + part * rows, rows), :]
                s = lax.dot_general(q, k, contract, preferred_element_type=jnp.float32)
                scores.append(s if ok is None else jnp.where(ok, s, MASKED))
            far = []
            for i in range(per_tile):
                block = t * per_tile + i
                ok = lanes < 0
                for n in range(nfar):
                    at = pos_ref[(f * plan.blocks + block) * nfar + n]
                    src = pl.ds(pl.multiple_of(jnp.maximum(at, 0) * BLOCK, BLOCK), BLOCK)
                    fark[block, n * BLOCK : (n + 1) * BLOCK, :] = kbuf[slot, src, :]
                    farv[block, n * BLOCK : (n + 1) * BLOCK, :] = vbuf[slot, src, :]
                    ok = ok | ((lanes == n) & (at >= 0))
                s = lax.dot_general(
                    q[i * BLOCK : (i + 1) * BLOCK],
                    fark[block],
                    contract,
                    preferred_element_type=jnp.float32,
                )
                far.append(jnp.where(ok, s, MASKED))
            far = jnp.concatenate(far, axis=0)
            peak = jnp.max(far, axis=1, keepdims=True)
            for s in scores:
                peak = jnp.maximum(peak, jnp.max(s, axis=1, keepdims=True))
            total, out = 0.0, 0.0
            for part, s in enumerate(scores):
                p = jnp.exp2((s - peak) * scale)
                total += jnp.sum(p, axis=1, keepdims=True)
                v = vbuf[slot, pl.ds(first + part * rows, rows), :]
                out += jnp.dot(p.astype(jnp.bfloat16), v, preferred_element_type=jnp.float32)
            p = jnp.exp2((far - peak) * scale)
            total += jnp.sum(p, axis=1, keepdims=True)
            p = p.astype(jnp.bfloat16)
            far_out = [
                jnp.dot(
                    p[i * BLOCK : (i + 1) * BLOCK],
                    farv[t * per_tile + i],
                    preferred_element_type=jnp.float32,
                )
                for i in range(per_tile)
            ]
            out = (out + jnp.concatenate(far_out, axis=0)) / total
            out_ref[f, t * tile : (t + 1) * tile, head(h)] = out.astype(jnp.bfloat16)

    for copy in copies(0):
        copy.start()
    for h in range(heads):
        if h + 1 < heads:
            for copy in copies(h + 1):
                copy.start()
        for copy in copies(h):
            copy.wait()
        lax.fori_loop(0, group, lambda f, c, h=h: (one_frame(f, h), c)[1], 0)


def attend(plan, plane, pos, heads, q, at_q, k, at_k, k_recv, v, at_v, v_recv, after):
    order = list(k_recv)
    nfar = len(plan.slots)
    any_spec = pl.BlockSpec(memory_space=pl.ANY)
    smem = pl.BlockSpec(memory_space=pltpu.SMEM)
    rows = plan.total * BLOCK
    return pl.pallas_call(
        functools.partial(attend_body, plan, order, heads, len(after), at_q, at_k, at_v),
        in_specs=[smem, smem] + [any_spec] * (3 + 2 * len(order) + len(after)),
        out_specs=pl.BlockSpec(memory_space=pltpu.VMEM),
        out_shape=jax.ShapeDtypeStruct((plan.group, plan.rows, heads * HEAD_DIM), jnp.bfloat16),
        scratch_shapes=[
            pltpu.VMEM((2, plan.group, plan.rows, HEAD_DIM), jnp.bfloat16),
            pltpu.VMEM((2, rows, HEAD_DIM), jnp.bfloat16),
            pltpu.VMEM((2, rows, HEAD_DIM), jnp.bfloat16),
            pltpu.VMEM((plan.blocks, nfar * BLOCK, HEAD_DIM), jnp.bfloat16),
            pltpu.VMEM((plan.blocks, nfar * BLOCK, HEAD_DIM), jnp.bfloat16),
            pltpu.SemaphoreType.DMA((2, 1 + 2 * (plan.group + 2 + len(order)))),
        ],
        name="attend",
        **params(),
    )(plane, pos, q, k, v, *k_recv.values(), *v_recv.values(), *after)


def merge_body(plan, first, x_ref, *refs):
    out, sem = refs[-2:]
    copies = []
    for g in range(plan.group):
        start = (g * plan.heads + first) * HEAD_DIM
        dst = out.at[:, start : start + x_ref.shape[-1]]
        copies.append(pltpu.make_async_copy(x_ref.at[g], dst, sem.at[g]))
    for copy in copies:
        copy.start()
    for copy in copies:
        copy.wait()


def merge(plan, x, first, out):
    width = plan.group * plan.heads * HEAD_DIM
    any_spec = pl.BlockSpec(memory_space=pl.ANY)
    return pl.pallas_call(
        functools.partial(merge_body, plan, first),
        in_specs=[pl.BlockSpec(memory_space=pltpu.VMEM)] + [any_spec] * len(out),
        out_specs=any_spec,
        out_shape=jax.ShapeDtypeStruct((plan.rows, width), x.dtype),
        input_output_aliases={1: 0} if out else {},
        scratch_shapes=[pltpu.SemaphoreType.DMA((plan.group,))],
        name="merge",
        **params(),
    )(x, *out)


def far_positions(plan, plane, far_frames, far_pick):
    group, blocks = plan.group, plan.blocks
    own = group * blocks
    lists = lax.dynamic_slice_in_dim(far_frames, plane * own, own, 0)
    lists = jnp.concatenate([lists[:, s : s + 1] for s in plan.slots], axis=1)
    g = jnp.maximum(lists, 0)
    rows = lax.dynamic_slice_in_dim(far_pick, plane * group, group, 0)
    rows = jnp.repeat(rows, blocks, axis=0)
    hit = g[:, :, None] == jnp.arange(plan.frames)
    pick = jnp.sum(jnp.where(hit, rows[:, None, :], 0), axis=2)
    f = (jnp.arange(own) // blocks)[:, None]
    source, lane = g // group, g % group
    if plan.matched:
        pos = jnp.zeros_like(g)
        for link in plan.links:
            if link[0] == 1:
                at = f * (group - 1) + lane - jnp.where(source > plane, 1, 0)
            else:
                at = f * group + lane
            low = jnp.minimum(source, plane)
            hit = (jnp.abs(source - plane) == link[0]) & plan.above(link, low)
            pos = jnp.where(hit, plan.base[link] + at, pos)
    else:
        pos = plan.base[None] + (source * group + f) * group + lane
    away = g - plane * group
    near = (away >= -1) & (away <= group)
    pos = jnp.where(near, plan.near0 + away * blocks + pick, pos)
    return jnp.where(lists >= 0, pos, -1).astype(jnp.int32).reshape(-1)


def local(query, key, value, q_gain, k_gain, far_frames, far_pick):
    rows, width = query.shape
    full_width = width * lax.axis_size("head")
    plan = Plan(lax.axis_size("tm"), rows, width // HEAD_DIM)
    plane = lax.axis_index("tm") // plan.group
    plane_arg = plane.astype(jnp.int32).reshape(1)
    picks = far_pick.reshape(-1)

    def share(x):
        if plan.group == 1:
            return x
        return lax.all_to_all(x, "tm", 0, 0, axis_index_groups=plan.sharers(), tiled=True)

    def exchange(x, first, heads, after):
        sent = pack(plan, plane_arg, picks, x, first, heads, after)
        packed.append(sent[:1])
        if plan.matched:
            return {n: lax.ppermute(y, "tm", plan.pairs(n)) for n, y in zip(plan.links, sent)}
        far = sent[0].reshape(plan.planes, -1, heads * HEAD_DIM)
        far = lax.all_to_all(far, "tm", 0, 0, axis_index_groups=plan.lines(), tiled=True)
        x = x[:, :, first * HEAD_DIM : (first + heads) * HEAD_DIM]
        return {
            "before": lax.ppermute(x[plan.group - 1], "tm", plan.halo(1)),
            "after": lax.ppermute(x[0], "tm", plan.halo(-1)),
            None: far.reshape(sent[0].shape),
        }

    packed = []
    early, late = plan.early, plan.heads - plan.early
    v0 = share(select(plan, value, 0, early, []))
    v0_recv = exchange(v0, 0, early, [])
    sums = jnp.stack([jnp.sum(jnp.square(x.astype(jnp.float32)), axis=1) for x in (query, key)])
    q_rs, k_rs = lax.rsqrt(lax.psum(sums, "head") / full_width + EPSILON)
    k0 = share(select(plan, key, 0, early, packed[0], k_rs, k_gain))
    k0_recv = exchange(k0, 0, early, [])
    q = share(select(plan, query, 0, plan.heads, packed[1], q_rs, q_gain))
    pos = far_positions(plan, plane, far_frames, far_pick)
    if late:
        v1 = share(select(plan, value, early, late, packed[1]))
        v1_recv = exchange(v1, 0, late, [q])
        k1 = share(select(plan, key, early, late, packed[2], k_rs, k_gain))
        k1_recv = [exchange(k1, 0, 1, [])]
    x = attend(plan, plane_arg, pos, early, q, 0, k0, 0, k0_recv, v0, 0, v0_recv, [])
    out = merge(plan, share(x), 0, [])
    for h in range(late):
        if h + 1 < late:
            k1_recv.append(exchange(k1, h + 1, 1, [out]))
        x = attend(
            plan, plane_arg, pos, 1, q, early + h, k1, h, k1_recv[h], v1, h, v1_recv,
            packed[-1] if h + 1 < late else [out],
        )
        if h + 2 < late:
            out = merge(plan, share(x), early + h, [out])
        else:
            last = last + [x] if h + 1 == late and late > 1 else [x]
    if late:
        first = plan.heads - len(last)
        for h, x in enumerate(last):
            out = merge(plan, share(x), first + h, [out])
    return out


def solution(mesh):
    placed = (P("tm", "head"), P("tm", "head"), P("tm", "head"), P("head"), P("head"), P(), P())
    return jax.shard_map(
        local, mesh=mesh, in_specs=placed, out_specs=P("tm", "head"), check_vma=False
    )
```

```python
import functools
import math

import jax
import jax.numpy as jnp
from jax import lax
from jax.experimental import pallas as pl
from jax.experimental.pallas import tpu as pltpu
from jax.sharding import PartitionSpec as P

HEAD_DIM = 128
BLOCK = 64
NFAR = 12
EPSILON = 1e-06
MASKED = -1e30
VMEM_LIMIT = 56 * 1024 * 1024


class Plan:
    def __init__(self, frames, rows, heads):
        self.frames, self.rows = frames, rows
        self.group = 4 if heads % 4 == 0 and frames % 4 == 0 else 1
        self.planes = frames // self.group
        self.blocks = rows // BLOCK
        self.heads = heads // self.group
        bands = sum(2**band <= frames - 1 for band in range(1, NFAR // 2 + 1))
        self.slots = [*range(bands), *range(NFAR // 2, NFAR // 2 + bands)]
        square = self.group * self.group
        self.near0 = self.blocks
        after = self.blocks * (self.group + 2)
        self.matched = 2 <= self.planes <= 8
        self.links, self.base, self.far = [], {}, {}
        if self.matched:
            for d in range(1, self.planes):
                for odd in (0, 1):
                    if any((p // d) % 2 == odd for p in range(self.planes - d)):
                        link = (d, odd)
                        self.links.append(link)
                        self.base[link] = after
                        self.far[link] = square - self.group if d == 1 else square
                        after += self.far[link]
        else:
            self.base[None] = after
            after += self.planes * square
        self.total = after

    def size(self, link):
        return self.far[link] + (self.blocks if link[0] == 1 else 0)

    def above(self, link, plane):
        d, odd = link
        return (plane // d) % 2 == odd

    def pairs(self, link):
        d, _ = link
        step = d * self.group
        made = []
        for i in range(self.frames - step):
            if self.above(link, i // self.group):
                made += [(i, i + step), (i + step, i)]
        return made

    def halo(self, step):
        return [(i, i + step) for i in range(self.frames) if 0 <= i + step < self.frames]

    def sharers(self):
        g = self.group
        return [[p * g + i for i in range(g)] for p in range(self.planes)]

    def lines(self):
        g = self.group
        return [[p * g + i for p in range(self.planes)] for i in range(g)]


def params():
    return dict(
        compiler_params=pltpu.CompilerParams(vmem_limit_bytes=VMEM_LIMIT),
        cost_estimate=pl.CostEstimate(flops=1, bytes_accessed=1, transcendentals=0),
    )


def select_body(scaled, n_after, *refs):
    out = refs[-1]
    refs = list(refs[: len(refs) - 1 - n_after])
    for item, with_scale in enumerate(scaled):
        x = refs.pop(0)[...]
        if with_scale:
            rs, gain = refs.pop(0), refs.pop(0)
            x = x.astype(jnp.float32) * rs[...] * gain[...]
        out[0, item] = x.astype(out.dtype)


def select(plan, items, after):
    args, specs = [], []
    for x, head, rs, gain in items:

        def at(g, head=head):
            return 0, g * plan.heads + head

        args.append(x)
        specs.append(pl.BlockSpec((plan.rows, HEAD_DIM), at))
        if rs is not None:
            args += [rs, gain]
            specs.append(pl.BlockSpec((plan.rows, 1), lambda g: (0, 0)))
            specs.append(pl.BlockSpec((1, HEAD_DIM), at))
    shape = (plan.group, len(items), plan.rows, HEAD_DIM)
    return pl.pallas_call(
        functools.partial(select_body, [rs is not None for _, _, rs, _ in items], len(after)),
        grid=(plan.group,),
        in_specs=specs + [pl.BlockSpec(memory_space=pl.ANY)] * len(after),
        out_specs=pl.BlockSpec((1,) + shape[1:], lambda g: (g, 0, 0, 0)),
        out_shape=jax.ShapeDtypeStruct(shape, jnp.bfloat16),
        name="select",
        **params(),
    )(*args, *after)


def pack_body(plan, n_after, plane_ref, pick_ref, x_ref, *refs):
    outs, sem = refs[n_after:-1], refs[-1]
    plane = plane_ref[0]
    group, rows = plan.group, plan.rows

    def block(dest, f, g):
        return pick_ref[(dest * group + f) * plan.frames + plane * group + g]

    def copies(index):
        made = []

        def add(g, src, dst, size):
            made.append(
                pltpu.make_async_copy(
                    x_ref.at[g, :, pl.ds(pl.multiple_of(src, BLOCK), size), :],
                    outs[index].at[:, pl.ds(dst, size), :],
                    sem.at[index, len(made)],
                )
            )

        if not plan.matched:
            for dest in range(plan.planes):
                for f in range(group):
                    for g in range(group):
                        slot = (dest * group + f) * group + g
                        add(g, block(dest, f, g) * BLOCK, slot * BLOCK, BLOCK)
            return made
        link = plan.links[index]
        dest, up = partner(link)
        dest = jnp.clip(dest, 0, plan.planes - 1)
        near = link[0] == 1
        slot = 0
        for f in range(group):
            for g in range(group - near):
                if near:
                    g += jnp.where(up, 0, 1)
                add(g, block(dest, f, g) * BLOCK, slot * BLOCK, BLOCK)
                slot += 1
        if near:
            add(jnp.where(up, group - 1, 0), 0, slot * BLOCK, rows)
        return made

    def partner(link):
        up = plan.above(link, plane)
        return plane + jnp.where(up, link[0], -link[0]), up

    def for_each(act):
        for index in range(len(outs)):
            if plan.matched:
                dest, _ = partner(plan.links[index])

                @pl.when((dest >= 0) & (dest < plan.planes))
                def _(index=index):
                    for copy in copies(index):
                        act(copy)
            else:
                for copy in copies(index):
                    act(copy)

    for_each(lambda copy: copy.start())
    for_each(lambda copy: copy.wait())


def pack(plan, plane, picks, x, pair, after):
    if plan.matched:
        sizes = [plan.size(link) for link in plan.links]
    else:
        sizes = [plan.planes * plan.group * plan.group]
    smem = pl.BlockSpec(memory_space=pltpu.SMEM)
    any_spec = pl.BlockSpec(memory_space=pl.ANY)
    return pl.pallas_call(
        functools.partial(pack_body, plan, len(after)),
        grid=(1,),
        in_specs=[
            smem,
            smem,
            pl.BlockSpec((plan.group, 2, plan.rows, HEAD_DIM), lambda i: (0, pair, 0, 0)),
        ]
        + [any_spec] * len(after),
        out_specs=[any_spec] * len(sizes),
        out_shape=[jax.ShapeDtypeStruct((2, n * BLOCK, HEAD_DIM), x.dtype) for n in sizes],
        scratch_shapes=[pltpu.SemaphoreType.DMA((len(sizes), max(sizes)))],
        name="pack",
        **params(),
    )(plane, picks, x, *after)


def attend_body(plan, order, heads, at_out, n_out, *refs):
    plane_ref, pos_ref = refs[:2]
    step = 2 + len(order)
    inputs = [refs[2 + h * step : 2 + (h + 1) * step] for h in range(len(heads))]
    out_ref, qbuf, kvbuf, obuf, fark, farv, sem, out_sem = refs[2 + len(heads) * step + n_out :]
    group, rows, nfar = plan.group, plan.rows, len(plan.slots)
    plane = plane_ref[0]
    scale = math.log2(math.e) / math.sqrt(HEAD_DIM)
    tile = min(rows, 256)
    per_tile = tile // BLOCK
    lanes = lax.broadcasted_iota(jnp.int32, (1, nfar * BLOCK), 1) // BLOCK
    contract = (((1,), (1,)), ((), ()))

    def copies(h):
        made, slot = [], h % 2
        q_ref, kv_ref, *recvs = inputs[h]
        at_q, at_k = heads[h]

        def add(src, dst):
            made.append(pltpu.make_async_copy(src, dst, sem.at[slot, len(made)]))

        def receive(index, src, first, count):
            first = first * BLOCK
            if not isinstance(first, int):
                first = pl.multiple_of(first, BLOCK)
            add(
                recvs[index].at[:, src * BLOCK : (src + count) * BLOCK, :],
                kvbuf.at[slot, :, pl.ds(first, count * BLOCK), :],
            )

        add(q_ref.at[:, at_q], qbuf.at[slot])
        for g in range(group):
            place = pl.ds((plan.near0 + g * plan.blocks) * BLOCK, rows)
            add(kv_ref.at[g, at_k : at_k + 2], kvbuf.at[slot, :, place, :])
        after = plan.near0 + group * plan.blocks
        for index, name in enumerate(order):
            if name in plan.links:
                count = plan.far[name]
                if count:
                    receive(index, 0, plan.base[name], count)
                if name[0] == 1:
                    up = plan.above(name, plane)
                    receive(index, count, jnp.where(up, after, 0), plan.blocks)
            elif name is None:
                receive(index, 0, plan.base[None], plan.total - plan.base[None])
            else:
                receive(index, 0, 0 if name == "before" else after, plan.blocks)
        return made

    def one_frame(f, h):
        slot = h % 2
        first = pl.multiple_of((plan.near0 + (f - 1) * plan.blocks) * BLOCK, BLOCK)
        frame = plane * group + f
        for t in range(rows // tile):
            q = qbuf[slot, f, t * tile : (t + 1) * tile, :]
            scores = []
            for part, ok in enumerate((frame > 0, None, frame < plan.frames - 1)):
                k = kvbuf[slot, 0, pl.ds(first + part * rows, rows), :]
                s = lax.dot_general(q, k, contract, preferred_element_type=jnp.float32)
                scores.append(s if ok is None else jnp.where(ok, s, MASKED))
            far = []
            for i in range(per_tile):
                block = t * per_tile + i
                ok = lanes < 0
                for n in range(nfar):
                    at = pos_ref[(f * plan.blocks + block) * nfar + n]
                    src = pl.ds(pl.multiple_of(jnp.maximum(at, 0) * BLOCK, BLOCK), BLOCK)
                    fark[block, n * BLOCK : (n + 1) * BLOCK, :] = kvbuf[slot, 0, src, :]
                    farv[block, n * BLOCK : (n + 1) * BLOCK, :] = kvbuf[slot, 1, src, :]
                    ok = ok | ((lanes == n) & (at >= 0))
                s = lax.dot_general(
                    q[i * BLOCK : (i + 1) * BLOCK],
                    fark[block],
                    contract,
                    preferred_element_type=jnp.float32,
                )
                far.append(jnp.where(ok, s, MASKED))
            far = jnp.concatenate(far, axis=0)
            peak = jnp.max(far, axis=1, keepdims=True)
            for s in scores:
                peak = jnp.maximum(peak, jnp.max(s, axis=1, keepdims=True))
            total, out = 0.0, 0.0
            for part, s in enumerate(scores):
                p = jnp.exp2((s - peak) * scale)
                total += jnp.sum(p, axis=1, keepdims=True)
                v = kvbuf[slot, 1, pl.ds(first + part * rows, rows), :]
                out += jnp.dot(p.astype(jnp.bfloat16), v, preferred_element_type=jnp.float32)
            p = jnp.exp2((far - peak) * scale)
            total += jnp.sum(p, axis=1, keepdims=True)
            p = p.astype(jnp.bfloat16)
            far_out = [
                jnp.dot(
                    p[i * BLOCK : (i + 1) * BLOCK],
                    farv[t * per_tile + i],
                    preferred_element_type=jnp.float32,
                )
                for i in range(per_tile)
            ]
            out = (out + jnp.concatenate(far_out, axis=0)) / total
            obuf[f, h, t * tile : (t + 1) * tile, :] = out.astype(jnp.bfloat16)

    for copy in copies(0):
        copy.start()
    for h in range(len(heads)):
        if h + 1 < len(heads):
            for copy in copies(h + 1):
                copy.start()
        for copy in copies(h):
            copy.wait()
        lax.fori_loop(0, group, lambda f, c, h=h: (one_frame(f, h), c)[1], 0)
    done = pltpu.make_async_copy(obuf, out_ref.at[:, at_out : at_out + len(heads)], out_sem)
    done.start()
    done.wait()


def attend(plan, plane, pos, heads, at_out, of, out):
    order = list(heads[0][4])
    nfar, count = len(plan.slots), len(heads)
    any_spec = pl.BlockSpec(memory_space=pl.ANY)
    smem = pl.BlockSpec(memory_space=pltpu.SMEM)
    args = [y for q, _, kv, _, recv in heads for y in (q, kv, *recv.values())]
    items = [(at_q, at_k) for _, at_q, _, at_k, _ in heads]
    shape = (plan.group, of, plan.rows, HEAD_DIM)
    return pl.pallas_call(
        functools.partial(attend_body, plan, order, items, at_out, len(out)),
        in_specs=[smem, smem] + [any_spec] * (len(args) + len(out)),
        out_specs=any_spec,
        out_shape=jax.ShapeDtypeStruct(shape, jnp.bfloat16),
        input_output_aliases={2 + len(args): 0} if out else {},
        scratch_shapes=[
            pltpu.VMEM((2, plan.group, plan.rows, HEAD_DIM), jnp.bfloat16),
            pltpu.VMEM((2, 2, plan.total * BLOCK, HEAD_DIM), jnp.bfloat16),
            pltpu.VMEM((plan.group, count, plan.rows, HEAD_DIM), jnp.bfloat16),
            pltpu.VMEM((plan.blocks, nfar * BLOCK, HEAD_DIM), jnp.bfloat16),
            pltpu.VMEM((plan.blocks, nfar * BLOCK, HEAD_DIM), jnp.bfloat16),
            pltpu.SemaphoreType.DMA((2, 1 + plan.group + 2 + len(order))),
            pltpu.SemaphoreType.DMA,
        ],
        name="attend",
        **params(),
    )(plane, pos, *args, *out)


def merge_body(plan, first, x_ref, *refs):
    out, sem = refs[-2:]
    copies = []
    for g in range(plan.group):
        for h in range(x_ref.shape[1]):
            start = (g * plan.heads + first + h) * HEAD_DIM
            dst = out.at[:, start : start + HEAD_DIM]
            copies.append(pltpu.make_async_copy(x_ref.at[g, h], dst, sem.at[len(copies)]))
    for copy in copies:
        copy.start()
    for copy in copies:
        copy.wait()


def merge(plan, x, first, out):
    width = plan.group * plan.heads * HEAD_DIM
    any_spec = pl.BlockSpec(memory_space=pl.ANY)
    return pl.pallas_call(
        functools.partial(merge_body, plan, first),
        in_specs=[pl.BlockSpec(memory_space=pltpu.VMEM)] + [any_spec] * len(out),
        out_specs=any_spec,
        out_shape=jax.ShapeDtypeStruct((plan.rows, width), x.dtype),
        input_output_aliases={1: 0} if out else {},
        scratch_shapes=[pltpu.SemaphoreType.DMA((plan.group * x.shape[1],))],
        name="merge",
        **params(),
    )(x, *out)


def far_positions(plan, plane, far_frames, far_pick):
    group, blocks = plan.group, plan.blocks
    own = group * blocks
    lists = lax.dynamic_slice_in_dim(far_frames, plane * own, own, 0)
    lists = jnp.concatenate([lists[:, s : s + 1] for s in plan.slots], axis=1)
    g = jnp.maximum(lists, 0)
    rows = lax.dynamic_slice_in_dim(far_pick, plane * group, group, 0)
    rows = jnp.repeat(rows, blocks, axis=0)
    hit = g[:, :, None] == jnp.arange(plan.frames)
    pick = jnp.sum(jnp.where(hit, rows[:, None, :], 0), axis=2)
    f = (jnp.arange(own) // blocks)[:, None]
    source, lane = g // group, g % group
    if plan.matched:
        pos = jnp.zeros_like(g)
        for link in plan.links:
            if link[0] == 1:
                at = f * (group - 1) + lane - jnp.where(source > plane, 1, 0)
            else:
                at = f * group + lane
            low = jnp.minimum(source, plane)
            hit = (jnp.abs(source - plane) == link[0]) & plan.above(link, low)
            pos = jnp.where(hit, plan.base[link] + at, pos)
    else:
        pos = plan.base[None] + (source * group + f) * group + lane
    away = g - plane * group
    near = (away >= -1) & (away <= group)
    pos = jnp.where(near, plan.near0 + away * blocks + pick, pos)
    return jnp.where(lists >= 0, pos, -1).astype(jnp.int32).reshape(-1)


def local(query, key, value, q_gain, k_gain, far_frames, far_pick):
    rows, width = query.shape
    full_width = width * lax.axis_size("head")
    plan = Plan(lax.axis_size("tm"), rows, width // HEAD_DIM)
    plane = lax.axis_index("tm") // plan.group
    plane_arg = plane.astype(jnp.int32).reshape(1)
    picks = far_pick.reshape(-1)

    def share(x):
        if plan.group == 1:
            return x
        return lax.all_to_all(x, "tm", 0, 0, axis_index_groups=plan.sharers(), tiled=True)

    def exchange(x, pair, after):
        sent = pack(plan, plane_arg, picks, x, pair, after)
        packed.append(sent[:1])
        if plan.matched:
            return {n: lax.ppermute(y, "tm", plan.pairs(n)) for n, y in zip(plan.links, sent)}
        far = sent[0].reshape(2, plan.planes, -1, HEAD_DIM)
        far = lax.all_to_all(far, "tm", 1, 1, axis_index_groups=plan.lines(), tiled=True)
        x = x[:, 2 * pair : 2 * pair + 2]
        return {
            "before": lax.ppermute(x[plan.group - 1], "tm", plan.halo(1)),
            "after": lax.ppermute(x[0], "tm", plan.halo(-1)),
            None: far.reshape(sent[0].shape),
        }

    sums = jnp.stack([jnp.sum(jnp.square(x.astype(jnp.float32)), axis=1) for x in (query, key)])
    q_rs, k_rs = lax.rsqrt(lax.psum(sums, "head") / full_width + EPSILON)[:, :, None]
    q_gain, k_gain = q_gain[None, :], k_gain[None, :]

    def pair(h):
        return [(key, h, k_rs, k_gain), (value, h, None, None)]

    heads = plan.heads
    packed, recvs = [], []
    queries = [(query, h, q_rs, q_gain) for h in range(heads)]
    first = share(select(plan, pair(0), []))
    second = share(select(plan, (pair(1) if heads > 1 else []) + queries, []))
    recvs.append(exchange(first, 0, []))
    where = [(first, 0)]
    if heads > 1:
        recvs.append(exchange(second, 0, []))
        where.append((second, 0))
    if heads > 2:
        late = [item for h in range(2, heads) for item in pair(h)]
        third = share(select(plan, late, packed[1]))
        where += [(third, 2 * h) for h in range(heads - 2)]
    pos = far_positions(plan, plane, far_frames, far_pick)
    first_q = second.shape[1] - heads

    def run(chosen, at_out, of, out):
        args = [(second, first_q + h, *where[h], recvs[h]) for h in chosen]
        return attend(plan, plane_arg, pos, args, at_out, of, out)

    early = min(2, heads)
    for h in range(2, heads - 1):
        recvs.append(exchange(third, h - 2, []))
    out = merge(plan, share(run(range(early), 0, early, [])), 0, [])
    if heads > 2:
        recvs.append(exchange(third, heads - 3, [out]))
        held = []
        for h in range(2, heads):
            held = [run([h], h - 2, heads - 2, held)]
        out = merge(plan, share(held[0]), 2, [out])
    return out


def solution(mesh):
    placed = (P("tm", "head"), P("tm", "head"), P("tm", "head"), P("head"), P("head"), P(), P())
    return jax.shard_map(
        local, mesh=mesh, in_specs=placed, out_specs=P("tm", "head"), check_vma=False
    )
```

```python
import functools
import math

import jax
import jax.numpy as jnp
from jax import lax
from jax.experimental import pallas as pl
from jax.experimental.pallas import tpu as pltpu
from jax.sharding import PartitionSpec as P

HEAD_DIM = 128
BLOCK = 64
NFAR = 12
EPSILON = 1e-06
MASKED = -1e30
VMEM_LIMIT = 56 * 1024 * 1024


class Plan:
    def __init__(self, frames, rows, heads):
        self.frames, self.rows = frames, rows
        self.group = 4 if heads % 4 == 0 and frames % 4 == 0 else 1
        self.planes = frames // self.group
        self.blocks = rows // BLOCK
        self.heads = heads // self.group
        bands = sum(2**band <= frames - 1 for band in range(1, NFAR // 2 + 1))
        self.slots = [*range(bands), *range(NFAR // 2, NFAR // 2 + bands)]
        square = self.group * self.group
        self.near0 = self.blocks
        after = self.blocks * (self.group + 2)
        self.matched = 2 <= self.planes <= 8
        self.links, self.base, self.far = [], {}, {}
        if self.matched:
            for d in range(1, self.planes):
                for odd in (0, 1):
                    if any((p // d) % 2 == odd for p in range(self.planes - d)):
                        link = (d, odd)
                        self.links.append(link)
                        self.base[link] = after
                        self.far[link] = square - self.group if d == 1 else square
                        after += self.far[link]
        else:
            self.base[None] = after
            after += self.planes * square
        self.total = after

    def size(self, link):
        return self.far[link] + (self.blocks if link[0] == 1 else 0)

    def above(self, link, plane):
        d, odd = link
        return (plane // d) % 2 == odd

    def pairs(self, link):
        d, _ = link
        step = d * self.group
        made = []
        for i in range(self.frames - step):
            if self.above(link, i // self.group):
                made += [(i, i + step), (i + step, i)]
        return made

    def halo(self, step):
        return [(i, i + step) for i in range(self.frames) if 0 <= i + step < self.frames]

    def sharers(self):
        g = self.group
        return [[p * g + i for i in range(g)] for p in range(self.planes)]

    def lines(self):
        g = self.group
        return [[p * g + i for p in range(self.planes)] for i in range(g)]


def params():
    return dict(
        compiler_params=pltpu.CompilerParams(vmem_limit_bytes=VMEM_LIMIT),
        cost_estimate=pl.CostEstimate(flops=1, bytes_accessed=1, transcendentals=0),
    )


def select_body(scaled, n_after, *refs):
    out = refs[-1]
    refs = list(refs[: len(refs) - 1 - n_after])
    for item, with_scale in enumerate(scaled):
        x = refs.pop(0)[...]
        if with_scale:
            rs, gain = refs.pop(0), refs.pop(0)
            x = x.astype(jnp.float32) * rs[...] * gain[...]
        out[0, item] = x.astype(out.dtype)


def select(plan, items, after):
    args, specs = [], []
    for x, head, rs, gain in items:

        def at(g, head=head):
            return 0, g * plan.heads + head

        args.append(x)
        specs.append(pl.BlockSpec((plan.rows, HEAD_DIM), at))
        if rs is not None:
            args += [rs, gain]
            specs.append(pl.BlockSpec((plan.rows, 1), lambda g: (0, 0)))
            specs.append(pl.BlockSpec((1, HEAD_DIM), at))
    shape = (plan.group, len(items), plan.rows, HEAD_DIM)
    return pl.pallas_call(
        functools.partial(select_body, [rs is not None for _, _, rs, _ in items], len(after)),
        grid=(plan.group,),
        in_specs=specs + [pl.BlockSpec(memory_space=pl.ANY)] * len(after),
        out_specs=pl.BlockSpec((1,) + shape[1:], lambda g: (g, 0, 0, 0)),
        out_shape=jax.ShapeDtypeStruct(shape, jnp.bfloat16),
        name="select",
        **params(),
    )(*args, *after)


def pack_body(plan, n_after, plane_ref, pick_ref, x_ref, *refs):
    outs, sem = refs[n_after:-1], refs[-1]
    plane = plane_ref[0]
    group, rows = plan.group, plan.rows

    def block(dest, f, g):
        return pick_ref[(dest * group + f) * plan.frames + plane * group + g]

    def copies(index):
        made = []

        def add(g, src, dst, size):
            made.append(
                pltpu.make_async_copy(
                    x_ref.at[g, :, pl.ds(pl.multiple_of(src, BLOCK), size), :],
                    outs[index].at[:, pl.ds(dst, size), :],
                    sem.at[index, len(made)],
                )
            )

        if not plan.matched:
            for dest in range(plan.planes):
                for f in range(group):
                    for g in range(group):
                        slot = (dest * group + f) * group + g
                        add(g, block(dest, f, g) * BLOCK, slot * BLOCK, BLOCK)
            return made
        link = plan.links[index]
        dest, up = partner(link)
        dest = jnp.clip(dest, 0, plan.planes - 1)
        near = link[0] == 1
        slot = 0
        for f in range(group):
            for g in range(group - near):
                if near:
                    g += jnp.where(up, 0, 1)
                add(g, block(dest, f, g) * BLOCK, slot * BLOCK, BLOCK)
                slot += 1
        if near:
            add(jnp.where(up, group - 1, 0), 0, slot * BLOCK, rows)
        return made

    def partner(link):
        up = plan.above(link, plane)
        return plane + jnp.where(up, link[0], -link[0]), up

    def for_each(act):
        for index in range(len(outs)):
            if plan.matched:
                dest, _ = partner(plan.links[index])

                @pl.when((dest >= 0) & (dest < plan.planes))
                def _(index=index):
                    for copy in copies(index):
                        act(copy)
            else:
                for copy in copies(index):
                    act(copy)

    for_each(lambda copy: copy.start())
    for_each(lambda copy: copy.wait())


def pack(plan, plane, picks, x, pair, after):
    if plan.matched:
        sizes = [plan.size(link) for link in plan.links]
    else:
        sizes = [plan.planes * plan.group * plan.group]
    smem = pl.BlockSpec(memory_space=pltpu.SMEM)
    any_spec = pl.BlockSpec(memory_space=pl.ANY)
    return pl.pallas_call(
        functools.partial(pack_body, plan, len(after)),
        grid=(1,),
        in_specs=[
            smem,
            smem,
            pl.BlockSpec((plan.group, 2, plan.rows, HEAD_DIM), lambda i: (0, pair, 0, 0)),
        ]
        + [any_spec] * len(after),
        out_specs=[any_spec] * len(sizes),
        out_shape=[jax.ShapeDtypeStruct((2, n * BLOCK, HEAD_DIM), x.dtype) for n in sizes],
        scratch_shapes=[pltpu.SemaphoreType.DMA((len(sizes), max(sizes)))],
        name="pack",
        **params(),
    )(plane, picks, x, *after)


def attend_body(plan, order, heads, at_out, n_out, *refs):
    plane_ref, pos_ref = refs[:2]
    step = 2 + len(order)
    inputs = [refs[2 + h * step : 2 + (h + 1) * step] for h in range(len(heads))]
    out_ref, qbuf, kvbuf, obuf, fark, farv, sem, out_sem = refs[2 + len(heads) * step + n_out :]
    group, rows, nfar = plan.group, plan.rows, len(plan.slots)
    plane = plane_ref[0]
    scale = math.log2(math.e) / math.sqrt(HEAD_DIM)
    tile = min(rows, 256)
    per_tile = tile // BLOCK
    lanes = lax.broadcasted_iota(jnp.int32, (1, nfar * BLOCK), 1) // BLOCK
    contract = (((1,), (1,)), ((), ()))

    def copies(h):
        made, slot = [], h % 2
        q_ref, kv_ref, *recvs = inputs[h]
        at_q, at_k = heads[h]

        def add(src, dst):
            made.append(pltpu.make_async_copy(src, dst, sem.at[slot, len(made)]))

        def receive(index, src, first, count):
            first = first * BLOCK
            if not isinstance(first, int):
                first = pl.multiple_of(first, BLOCK)
            add(
                recvs[index].at[:, src * BLOCK : (src + count) * BLOCK, :],
                kvbuf.at[slot, :, pl.ds(first, count * BLOCK), :],
            )

        add(q_ref.at[:, at_q], qbuf.at[slot])
        for g in range(group):
            place = pl.ds((plan.near0 + g * plan.blocks) * BLOCK, rows)
            add(kv_ref.at[g, at_k : at_k + 2], kvbuf.at[slot, :, place, :])
        after = plan.near0 + group * plan.blocks
        for index, name in enumerate(order):
            if name in plan.links:
                count = plan.far[name]
                if count:
                    receive(index, 0, plan.base[name], count)
                if name[0] == 1:
                    up = plan.above(name, plane)
                    receive(index, count, jnp.where(up, after, 0), plan.blocks)
            elif name is None:
                receive(index, 0, plan.base[None], plan.total - plan.base[None])
            else:
                receive(index, 0, 0 if name == "before" else after, plan.blocks)
        return made

    def one_frame(f, h):
        slot = h % 2
        first = pl.multiple_of((plan.near0 + (f - 1) * plan.blocks) * BLOCK, BLOCK)
        frame = plane * group + f
        for t in range(rows // tile):
            q = qbuf[slot, f, t * tile : (t + 1) * tile, :]
            scores = []
            for part, ok in enumerate((frame > 0, None, frame < plan.frames - 1)):
                k = kvbuf[slot, 0, pl.ds(first + part * rows, rows), :]
                s = lax.dot_general(q, k, contract, preferred_element_type=jnp.float32)
                scores.append(s if ok is None else jnp.where(ok, s, MASKED))
            far = []
            for i in range(per_tile):
                block = t * per_tile + i
                ok = lanes < 0
                for n in range(nfar):
                    at = pos_ref[(f * plan.blocks + block) * nfar + n]
                    src = pl.ds(pl.multiple_of(jnp.maximum(at, 0) * BLOCK, BLOCK), BLOCK)
                    fark[block, n * BLOCK : (n + 1) * BLOCK, :] = kvbuf[slot, 0, src, :]
                    farv[block, n * BLOCK : (n + 1) * BLOCK, :] = kvbuf[slot, 1, src, :]
                    ok = ok | ((lanes == n) & (at >= 0))
                s = lax.dot_general(
                    q[i * BLOCK : (i + 1) * BLOCK],
                    fark[block],
                    contract,
                    preferred_element_type=jnp.float32,
                )
                far.append(jnp.where(ok, s, MASKED))
            far = jnp.concatenate(far, axis=0)
            peak = jnp.max(far, axis=1, keepdims=True)
            for s in scores:
                peak = jnp.maximum(peak, jnp.max(s, axis=1, keepdims=True))
            total, out = 0.0, 0.0
            for part, s in enumerate(scores):
                p = jnp.exp2((s - peak) * scale)
                total += jnp.sum(p, axis=1, keepdims=True)
                v = kvbuf[slot, 1, pl.ds(first + part * rows, rows), :]
                out += jnp.dot(p.astype(jnp.bfloat16), v, preferred_element_type=jnp.float32)
            p = jnp.exp2((far - peak) * scale)
            total += jnp.sum(p, axis=1, keepdims=True)
            p = p.astype(jnp.bfloat16)
            far_out = [
                jnp.dot(
                    p[i * BLOCK : (i + 1) * BLOCK],
                    farv[t * per_tile + i],
                    preferred_element_type=jnp.float32,
                )
                for i in range(per_tile)
            ]
            out = (out + jnp.concatenate(far_out, axis=0)) / total
            obuf[f, h, t * tile : (t + 1) * tile, :] = out.astype(jnp.bfloat16)

    for copy in copies(0):
        copy.start()
    for h in range(len(heads)):
        if h + 1 < len(heads):
            for copy in copies(h + 1):
                copy.start()
        for copy in copies(h):
            copy.wait()
        lax.fori_loop(0, group, lambda f, c, h=h: (one_frame(f, h), c)[1], 0)
    done = pltpu.make_async_copy(obuf, out_ref.at[:, at_out : at_out + len(heads)], out_sem)
    done.start()
    done.wait()


def attend(plan, plane, pos, heads, at_out, of, out):
    order = list(heads[0][4])
    nfar, count = len(plan.slots), len(heads)
    any_spec = pl.BlockSpec(memory_space=pl.ANY)
    smem = pl.BlockSpec(memory_space=pltpu.SMEM)
    args = [y for q, _, kv, _, recv in heads for y in (q, kv, *recv.values())]
    items = [(at_q, at_k) for _, at_q, _, at_k, _ in heads]
    shape = (plan.group, of, plan.rows, HEAD_DIM)
    return pl.pallas_call(
        functools.partial(attend_body, plan, order, items, at_out, len(out)),
        in_specs=[smem, smem] + [any_spec] * (len(args) + len(out)),
        out_specs=any_spec,
        out_shape=jax.ShapeDtypeStruct(shape, jnp.bfloat16),
        input_output_aliases={2 + len(args): 0} if out else {},
        scratch_shapes=[
            pltpu.VMEM((2, plan.group, plan.rows, HEAD_DIM), jnp.bfloat16),
            pltpu.VMEM((2, 2, plan.total * BLOCK, HEAD_DIM), jnp.bfloat16),
            pltpu.VMEM((plan.group, count, plan.rows, HEAD_DIM), jnp.bfloat16),
            pltpu.VMEM((plan.blocks, nfar * BLOCK, HEAD_DIM), jnp.bfloat16),
            pltpu.VMEM((plan.blocks, nfar * BLOCK, HEAD_DIM), jnp.bfloat16),
            pltpu.SemaphoreType.DMA((2, 1 + plan.group + 2 + len(order))),
            pltpu.SemaphoreType.DMA,
        ],
        name="attend",
        **params(),
    )(plane, pos, *args, *out)


def merge_body(plan, first, x_ref, *refs):
    out, sem = refs[-2:]
    copies = []
    for g in range(plan.group):
        for h in range(x_ref.shape[1]):
            start = (g * plan.heads + first + h) * HEAD_DIM
            dst = out.at[:, start : start + HEAD_DIM]
            copies.append(pltpu.make_async_copy(x_ref.at[g, h], dst, sem.at[len(copies)]))
    for copy in copies:
        copy.start()
    for copy in copies:
        copy.wait()


def merge(plan, x, first, out):
    width = plan.group * plan.heads * HEAD_DIM
    any_spec = pl.BlockSpec(memory_space=pl.ANY)
    return pl.pallas_call(
        functools.partial(merge_body, plan, first),
        in_specs=[pl.BlockSpec(memory_space=pltpu.VMEM)] + [any_spec] * len(out),
        out_specs=any_spec,
        out_shape=jax.ShapeDtypeStruct((plan.rows, width), x.dtype),
        input_output_aliases={1: 0} if out else {},
        scratch_shapes=[pltpu.SemaphoreType.DMA((plan.group * x.shape[1],))],
        name="merge",
        **params(),
    )(x, *out)


def far_positions(plan, plane, far_frames, far_pick):
    group, blocks = plan.group, plan.blocks
    own = group * blocks
    lists = lax.dynamic_slice_in_dim(far_frames, plane * own, own, 0)
    lists = jnp.concatenate([lists[:, s : s + 1] for s in plan.slots], axis=1)
    g = jnp.maximum(lists, 0)
    rows = lax.dynamic_slice_in_dim(far_pick, plane * group, group, 0)
    rows = jnp.repeat(rows, blocks, axis=0)
    hit = g[:, :, None] == jnp.arange(plan.frames)
    pick = jnp.sum(jnp.where(hit, rows[:, None, :], 0), axis=2)
    f = (jnp.arange(own) // blocks)[:, None]
    source, lane = g // group, g % group
    if plan.matched:
        pos = jnp.zeros_like(g)
        for link in plan.links:
            if link[0] == 1:
                at = f * (group - 1) + lane - jnp.where(source > plane, 1, 0)
            else:
                at = f * group + lane
            low = jnp.minimum(source, plane)
            hit = (jnp.abs(source - plane) == link[0]) & plan.above(link, low)
            pos = jnp.where(hit, plan.base[link] + at, pos)
    else:
        pos = plan.base[None] + (source * group + f) * group + lane
    away = g - plane * group
    near = (away >= -1) & (away <= group)
    pos = jnp.where(near, plan.near0 + away * blocks + pick, pos)
    return jnp.where(lists >= 0, pos, -1).astype(jnp.int32).reshape(-1)


def local(query, key, value, q_gain, k_gain, far_frames, far_pick):
    rows, width = query.shape
    full_width = width * lax.axis_size("head")
    plan = Plan(lax.axis_size("tm"), rows, width // HEAD_DIM)
    plane = lax.axis_index("tm") // plan.group
    plane_arg = plane.astype(jnp.int32).reshape(1)
    picks = far_pick.reshape(-1)

    def share(x):
        if plan.group == 1:
            return x
        return lax.all_to_all(x, "tm", 0, 0, axis_index_groups=plan.sharers(), tiled=True)

    def exchange(x, pair, after):
        sent = pack(plan, plane_arg, picks, x, pair, after)
        packed.append(sent[:1])
        if plan.matched:
            return {n: lax.ppermute(y, "tm", plan.pairs(n)) for n, y in zip(plan.links, sent)}
        far = sent[0].reshape(2, plan.planes, -1, HEAD_DIM)
        far = lax.all_to_all(far, "tm", 1, 1, axis_index_groups=plan.lines(), tiled=True)
        x = x[:, 2 * pair : 2 * pair + 2]
        return {
            "before": lax.ppermute(x[plan.group - 1], "tm", plan.halo(1)),
            "after": lax.ppermute(x[0], "tm", plan.halo(-1)),
            None: far.reshape(sent[0].shape),
        }

    sums = jnp.stack([jnp.sum(jnp.square(x.astype(jnp.float32)), axis=1) for x in (query, key)])
    q_rs, k_rs = lax.rsqrt(lax.psum(sums, "head") / full_width + EPSILON)[:, :, None]
    q_gain, k_gain = q_gain[None, :], k_gain[None, :]

    def pair(h):
        return [(key, h, k_rs, k_gain), (value, h, None, None)]

    heads = plan.heads
    queries = [(query, h, q_rs, q_gain) for h in range(heads)]
    rounds = [[h] for h in range(min(2, heads))]
    if heads > 3:
        rounds.append(list(range(2, heads - 1)))
    if heads > 2:
        rounds.append([heads - 1])
    packed, recvs, where, after = [], [], [], []
    out = None
    for index, chosen in enumerate(rounds):
        items = [item for h in chosen for item in pair(h)]
        ending = index + 1 == len(rounds)
        x = share(select(plan, items + (queries if ending else []), after))
        where += [(x, 2 * n) for n in range(len(chosen))]
        if ending:
            q, first_q = x, len(items)
        else:
            for n in range(len(chosen)):
                recvs.append(exchange(x, n, []))
                if n == 0:
                    after = packed[-1]
    pos = far_positions(plan, plane, far_frames, far_pick)

    def run(chosen, at_out, of, out):
        args = [(q, first_q + h, *where[h], recvs[h]) for h in chosen]
        return attend(plan, plane_arg, pos, args, at_out, of, out)

    early = min(2, heads - 1)
    if early:
        out = merge(plan, share(run(range(early), 0, early, [])), 0, [])
    recvs.append(exchange(x, 0, [out] if early else []))
    held = []
    for h in range(early, heads):
        held = [run([h], h - early, heads - early, held)]
    return merge(plan, share(held[0]), early, [out] if early else [])


def solution(mesh):
    placed = (P("tm", "head"), P("tm", "head"), P("tm", "head"), P("head"), P("head"), P(), P())
    return jax.shard_map(
        local, mesh=mesh, in_specs=placed, out_specs=P("tm", "head"), check_vma=False
    )
```

```python
import functools
import math

import jax
import jax.numpy as jnp
from jax import lax
from jax.experimental import pallas as pl
from jax.experimental.pallas import tpu as pltpu
from jax.sharding import PartitionSpec as P

HEAD_DIM = 128
BLOCK = 64
NFAR = 12
EPSILON = 1e-06
MASKED = -1e30
VMEM_LIMIT = 56 * 1024 * 1024


class Plan:
    def __init__(self, frames, rows, heads):
        self.frames, self.rows = frames, rows
        self.group = 4 if heads % 4 == 0 and frames % 4 == 0 else 1
        self.planes = frames // self.group
        self.blocks = rows // BLOCK
        self.heads = heads // self.group
        bands = sum(2**band <= frames - 1 for band in range(1, NFAR // 2 + 1))
        self.slots = [*range(bands), *range(NFAR // 2, NFAR // 2 + bands)]
        self.square = self.group * self.group
        self.near0 = self.blocks
        self.far0 = self.blocks * (self.group + 2)
        self.total = self.far0 + self.planes * self.square

    def halo(self, step):
        step *= self.group
        return [(i, i + step) for i in range(self.frames) if 0 <= i + step < self.frames]

    def swap(self, j):
        g = self.group
        return [(i, i // g * g + (i % g ^ j)) for i in range(self.frames)]

    def lines(self):
        g = self.group
        return [[p * g + i for p in range(self.planes)] for i in range(g)]


def params():
    return dict(
        compiler_params=pltpu.CompilerParams(vmem_limit_bytes=VMEM_LIMIT),
        cost_estimate=pl.CostEstimate(flops=1, bytes_accessed=1, transcendentals=0),
    )


def select_body(scaled, n_after, group, place_ref, *refs):
    outs = refs[len(refs) - group :]
    refs = list(refs[: len(refs) - group - n_after])
    values = []
    for with_scale in scaled:
        x = refs.pop(0)[...]
        if with_scale:
            rs, gain = refs.pop(0), refs.pop(0)
            x = x.astype(jnp.float32) * rs[...] * gain[...]
        values.append(x.astype(jnp.bfloat16))
    for j, out in enumerate(outs):

        @pl.when(pl.program_id(0) == j)
        def _(out=out):
            for item, x in enumerate(values):
                out[item] = x


def select(plan, place, items, after):
    args, specs = [], []
    for x, head, rs, gain in items:

        def at(j, place, head=head):
            return 0, (place[1] ^ j) * plan.heads + head

        args.append(x)
        specs.append(pl.BlockSpec((plan.rows, HEAD_DIM), at))
        if rs is not None:
            args += [rs, gain]
            specs.append(pl.BlockSpec((plan.rows, 1), lambda j, place: (0, 0)))
            specs.append(pl.BlockSpec((1, HEAD_DIM), at))
    shape = (len(items), plan.rows, HEAD_DIM)
    scaled = [rs is not None for _, _, rs, _ in items]
    return pl.pallas_call(
        functools.partial(select_body, scaled, len(after), plan.group),
        grid_spec=pltpu.PrefetchScalarGridSpec(
            num_scalar_prefetch=1,
            grid=(plan.group,),
            in_specs=specs + [pl.BlockSpec(memory_space=pl.ANY)] * len(after),
            out_specs=[pl.BlockSpec(shape, lambda j, place: (0, 0, 0))] * plan.group,
        ),
        out_shape=[jax.ShapeDtypeStruct(shape, jnp.bfloat16)] * plan.group,
        name="select",
        **params(),
    )(place, *args, *after)


def pack_body(plan, n_after, place_ref, pick_ref, *refs):
    group, blocks = plan.group, plan.blocks
    xs = refs[:group]
    far, to_next, to_prev, sem = refs[group + n_after :]
    plane, lane = place_ref[0], place_ref[1]

    def copies(dest):
        made = []
        for f in range(group):
            for j in range(group):
                g = lane ^ j
                block = pick_ref[(dest * group + f) * plan.frames + plane * group + g]
                src = pl.ds(pl.multiple_of(block * BLOCK, BLOCK), BLOCK)
                dst = pl.ds(pl.multiple_of((f * group + g) * BLOCK, BLOCK), BLOCK)
                made.append(
                    pltpu.make_async_copy(
                        xs[j].at[:, src, :], far.at[dest, :, dst, :], sem.at[dest, len(made)]
                    )
                )
        return made

    def halo(act):
        for j in range(group):
            for at, (g, out) in enumerate(((group - 1, to_next), (0, to_prev))):

                @pl.when((lane ^ j) == g)
                def _(j=j, at=at, out=out):
                    act(pltpu.make_async_copy(xs[j], out, sem.at[plan.planes, at]))

    def for_each(act):
        halo(act)

        def one_plane(dest, carry):
            @pl.when(dest != plane)
            def _():
                for copy in copies(dest):
                    act(copy)

            return carry

        lax.fori_loop(0, plan.planes, one_plane, 0)

    for_each(lambda copy: copy.start())
    for_each(lambda copy: copy.wait())


def pack(plan, place, picks, xs, pair, after):
    smem = pl.BlockSpec(memory_space=pltpu.SMEM)
    any_spec = pl.BlockSpec(memory_space=pl.ANY)
    frame = jax.ShapeDtypeStruct((2, plan.rows, HEAD_DIM), jnp.bfloat16)
    far = jax.ShapeDtypeStruct((plan.planes, 2, plan.square * BLOCK, HEAD_DIM), jnp.bfloat16)
    return pl.pallas_call(
        functools.partial(pack_body, plan, len(after)),
        grid=(1,),
        in_specs=[smem, smem]
        + [pl.BlockSpec((2, plan.rows, HEAD_DIM), lambda i: (pair, 0, 0))] * plan.group
        + [any_spec] * len(after),
        out_specs=[any_spec] * 3,
        out_shape=[far, frame, frame],
        scratch_shapes=[pltpu.SemaphoreType.DMA((plan.planes + 1, max(plan.square, 2)))],
        name="pack",
        **params(),
    )(place, picks, *xs, *after)


def attend_body(plan, heads, at_out, n_out, *refs):
    place_ref, pos_ref = refs[:2]
    group, rows, nfar = plan.group, plan.rows, len(plan.slots)
    step = 2 * group + 3
    inputs = [refs[2 + h * step : 2 + (h + 1) * step] for h in range(len(heads))]
    refs = refs[2 + len(heads) * step + n_out :]
    outs, (qbuf, kvbuf, obuf, fark, farv, sem, out_sem) = refs[:group], refs[group:]
    plane, lane = place_ref[0], place_ref[1]
    scale = math.log2(math.e) / math.sqrt(HEAD_DIM)
    tile = min(rows, 256)
    per_tile = tile // BLOCK
    lanes = lax.broadcasted_iota(jnp.int32, (1, nfar * BLOCK), 1) // BLOCK
    contract = (((1,), (1,)), ((), ()))

    def copies(h):
        made, slot = [], h % 2
        qs, kvs, recvs = inputs[h][:group], inputs[h][group : 2 * group], inputs[h][2 * group :]
        at_q, at_k = heads[h]

        def add(src, dst):
            made.append(pltpu.make_async_copy(src, dst, sem.at[slot, len(made)]))

        def at(first, count):
            first = first * BLOCK
            if not isinstance(first, int):
                first = pl.multiple_of(first, BLOCK)
            return kvbuf.at[slot, :, pl.ds(first, count * BLOCK), :]

        for j in range(group):
            g = lane ^ j
            add(qs[j].at[at_q], qbuf.at[slot, g])
            add(kvs[j].at[at_k : at_k + 2], at(plan.near0 + g * plan.blocks, plan.blocks))
        far, before, after = recvs
        add(before, at(0, plan.blocks))
        add(after, at(plan.near0 + group * plan.blocks, plan.blocks))
        for p in range(plan.planes):
            add(far.at[p], at(plan.far0 + p * plan.square, plan.square))
        return made

    def one_frame(f, h):
        slot = h % 2
        first = pl.multiple_of((plan.near0 + (f - 1) * plan.blocks) * BLOCK, BLOCK)
        frame = plane * group + f
        for t in range(rows // tile):
            q = qbuf[slot, f, t * tile : (t + 1) * tile, :]
            scores = []
            for part, ok in enumerate((frame > 0, None, frame < plan.frames - 1)):
                k = kvbuf[slot, 0, pl.ds(first + part * rows, rows), :]
                s = lax.dot_general(q, k, contract, preferred_element_type=jnp.float32)
                scores.append(s if ok is None else jnp.where(ok, s, MASKED))
            far = []
            for i in range(per_tile):
                block = t * per_tile + i
                ok = lanes < 0
                for n in range(nfar):
                    at = pos_ref[(f * plan.blocks + block) * nfar + n]
                    src = pl.ds(pl.multiple_of(jnp.maximum(at, 0) * BLOCK, BLOCK), BLOCK)
                    fark[block, n * BLOCK : (n + 1) * BLOCK, :] = kvbuf[slot, 0, src, :]
                    farv[block, n * BLOCK : (n + 1) * BLOCK, :] = kvbuf[slot, 1, src, :]
                    ok = ok | ((lanes == n) & (at >= 0))
                s = lax.dot_general(
                    q[i * BLOCK : (i + 1) * BLOCK],
                    fark[block],
                    contract,
                    preferred_element_type=jnp.float32,
                )
                far.append(jnp.where(ok, s, MASKED))
            far = jnp.concatenate(far, axis=0)
            peak = jnp.max(far, axis=1, keepdims=True)
            for s in scores:
                peak = jnp.maximum(peak, jnp.max(s, axis=1, keepdims=True))
            total, out = 0.0, 0.0
            for part, s in enumerate(scores):
                p = jnp.exp2((s - peak) * scale)
                total += jnp.sum(p, axis=1, keepdims=True)
                v = kvbuf[slot, 1, pl.ds(first + part * rows, rows), :]
                out += jnp.dot(p.astype(jnp.bfloat16), v, preferred_element_type=jnp.float32)
            p = jnp.exp2((far - peak) * scale)
            total += jnp.sum(p, axis=1, keepdims=True)
            p = p.astype(jnp.bfloat16)
            far_out = [
                jnp.dot(
                    p[i * BLOCK : (i + 1) * BLOCK],
                    farv[t * per_tile + i],
                    preferred_element_type=jnp.float32,
                )
                for i in range(per_tile)
            ]
            out = (out + jnp.concatenate(far_out, axis=0)) / total
            obuf[f, h, t * tile : (t + 1) * tile, :] = out.astype(jnp.bfloat16)

    for copy in copies(0):
        copy.start()
    for h in range(len(heads)):
        if h + 1 < len(heads):
            for copy in copies(h + 1):
                copy.start()
        for copy in copies(h):
            copy.wait()
        lax.fori_loop(0, group, lambda f, c, h=h: (one_frame(f, h), c)[1], 0)
    made = []
    for j in range(group):
        dst = outs[j].at[at_out : at_out + len(heads)]
        made.append(pltpu.make_async_copy(obuf.at[lane ^ j], dst, out_sem.at[j]))
    for copy in made:
        copy.start()
    for copy in made:
        copy.wait()


def attend(plan, place, pos, heads, at_out, of, outs):
    nfar, count = len(plan.slots), len(heads)
    any_spec = pl.BlockSpec(memory_space=pl.ANY)
    smem = pl.BlockSpec(memory_space=pltpu.SMEM)
    args = [y for q, _, kv, _, recv in heads for y in (*q, *kv, *recv)]
    items = [(at_q, at_k) for _, at_q, _, at_k, _ in heads]
    shape = jax.ShapeDtypeStruct((of, plan.rows, HEAD_DIM), jnp.bfloat16)
    return pl.pallas_call(
        functools.partial(attend_body, plan, items, at_out, len(outs)),
        in_specs=[smem, smem] + [any_spec] * (len(args) + len(outs)),
        out_specs=[any_spec] * plan.group,
        out_shape=[shape] * plan.group,
        input_output_aliases={2 + len(args) + j: j for j in range(len(outs))},
        scratch_shapes=[
            pltpu.VMEM((2, plan.group, plan.rows, HEAD_DIM), jnp.bfloat16),
            pltpu.VMEM((2, 2, plan.total * BLOCK, HEAD_DIM), jnp.bfloat16),
            pltpu.VMEM((plan.group, count, plan.rows, HEAD_DIM), jnp.bfloat16),
            pltpu.VMEM((plan.blocks, nfar * BLOCK, HEAD_DIM), jnp.bfloat16),
            pltpu.VMEM((plan.blocks, nfar * BLOCK, HEAD_DIM), jnp.bfloat16),
            pltpu.SemaphoreType.DMA((2, 2 * plan.group + 2 + plan.planes)),
            pltpu.SemaphoreType.DMA((plan.group,)),
        ],
        name="attend",
        **params(),
    )(place, pos, *args, *outs)


def merge_body(plan, first, place_ref, *refs):
    xs, (out, sem) = refs[: plan.group], refs[-2:]
    copies = []
    for j, x in enumerate(xs):
        for h in range(x.shape[0]):
            start = ((place_ref[1] ^ j) * plan.heads + first + h) * HEAD_DIM
            dst = out.at[:, pl.ds(pl.multiple_of(start, HEAD_DIM), HEAD_DIM)]
            copies.append(pltpu.make_async_copy(x.at[h], dst, sem.at[len(copies)]))
    for copy in copies:
        copy.start()
    for copy in copies:
        copy.wait()


def merge(plan, place, xs, first, out):
    width = plan.group * plan.heads * HEAD_DIM
    any_spec = pl.BlockSpec(memory_space=pl.ANY)
    vmem = pl.BlockSpec(memory_space=pltpu.VMEM)
    return pl.pallas_call(
        functools.partial(merge_body, plan, first),
        in_specs=[pl.BlockSpec(memory_space=pltpu.SMEM)]
        + [vmem] * plan.group
        + [any_spec] * len(out),
        out_specs=any_spec,
        out_shape=jax.ShapeDtypeStruct((plan.rows, width), jnp.bfloat16),
        input_output_aliases={1 + plan.group: 0} if out else {},
        scratch_shapes=[pltpu.SemaphoreType.DMA((plan.group * xs[0].shape[0],))],
        name="merge",
        **params(),
    )(place, *xs, *out)


def far_positions(plan, plane, far_frames, far_pick):
    group, blocks = plan.group, plan.blocks
    own = group * blocks
    lists = lax.dynamic_slice_in_dim(far_frames, plane * own, own, 0)
    lists = jnp.concatenate([lists[:, s : s + 1] for s in plan.slots], axis=1)
    g = jnp.maximum(lists, 0)
    rows = lax.dynamic_slice_in_dim(far_pick, plane * group, group, 0)
    rows = jnp.repeat(rows, blocks, axis=0)
    hit = g[:, :, None] == jnp.arange(plan.frames)
    pick = jnp.sum(jnp.where(hit, rows[:, None, :], 0), axis=2)
    f = (jnp.arange(own) // blocks)[:, None]
    source, lane = g // group, g % group
    pos = plan.far0 + (source * group + f) * group + lane
    away = g - plane * group
    near = (away >= -1) & (away <= group)
    pos = jnp.where(near, plan.near0 + away * blocks + pick, pos)
    return jnp.where(lists >= 0, pos, -1).astype(jnp.int32).reshape(-1)


def local(query, key, value, q_gain, k_gain, far_frames, far_pick):
    rows, width = query.shape
    full_width = width * lax.axis_size("head")
    plan = Plan(lax.axis_size("tm"), rows, width // HEAD_DIM)
    frame = lax.axis_index("tm").astype(jnp.int32)
    plane = frame // plan.group
    place = jnp.stack([plane, frame % plan.group])
    picks = far_pick.reshape(-1)

    def share(xs):
        return [xs[0]] + [lax.ppermute(xs[j], "tm", plan.swap(j)) for j in range(1, plan.group)]

    def exchange(xs, pair, after):
        far, to_next, to_prev = pack(plan, place, picks, xs, pair, after)
        packed.append([far])
        return (
            lax.all_to_all(far, "tm", 0, 0, axis_index_groups=plan.lines(), tiled=True),
            lax.ppermute(to_next, "tm", plan.halo(1)),
            lax.ppermute(to_prev, "tm", plan.halo(-1)),
        )

    sums = jnp.stack([jnp.sum(jnp.square(x.astype(jnp.float32)), axis=1) for x in (query, key)])
    q_rs, k_rs = lax.rsqrt(lax.psum(sums, "head") / full_width + EPSILON)[:, :, None]
    q_gain, k_gain = q_gain[None, :], k_gain[None, :]

    def pair(h):
        return [(key, h, k_rs, k_gain), (value, h, None, None)]

    heads = plan.heads
    queries = [(query, h, q_rs, q_gain) for h in range(heads)]
    rounds = [[h] for h in range(min(2, heads))]
    if heads > 3:
        rounds.append(list(range(2, heads - 1)))
    if heads > 2:
        rounds.append([heads - 1])
    packed, recvs, where, after = [], [], [], []
    out = None
    for index, chosen in enumerate(rounds):
        items = [item for h in chosen for item in pair(h)]
        ending = index + 1 == len(rounds)
        x = share(select(plan, place, items + (queries if ending else []), after))
        where += [(x, 2 * n) for n in range(len(chosen))]
        if ending:
            q, first_q = x, len(items)
        else:
            for n in range(len(chosen)):
                recvs.append(exchange(x, n, []))
                if n == 0:
                    after = packed[-1]
    pos = far_positions(plan, plane, far_frames, far_pick)

    def run(chosen, at_out, of, out):
        args = [(q, first_q + h, *where[h], recvs[h]) for h in chosen]
        return attend(plan, place, pos, args, at_out, of, out)

    early = min(2, heads - 1)
    if early:
        out = merge(plan, place, share(run(range(early), 0, early, [])), 0, [])
    recvs.append(exchange(x, 0, [out] if early else []))
    held = []
    for h in range(early, heads):
        held = run([h], h - early, heads - early, held)
    return merge(plan, place, share(held), early, [out] if early else [])


def solution(mesh):
    placed = (P("tm", "head"), P("tm", "head"), P("tm", "head"), P("head"), P("head"), P(), P())
    return jax.shard_map(
        local, mesh=mesh, in_specs=placed, out_specs=P("tm", "head"), check_vma=False
    )
```

```python
import functools
import math

import jax
import jax.numpy as jnp
from jax import lax
from jax.experimental import pallas as pl
from jax.experimental.pallas import tpu as pltpu
from jax.sharding import PartitionSpec as P

HEAD_DIM = 128
BLOCK = 64
NFAR = 12
EPSILON = 1e-06
MASKED = -1e30
VMEM_LIMIT = 56 * 1024 * 1024


class Plan:
    def __init__(self, frames, rows, heads):
        self.frames, self.rows = frames, rows
        self.group = 4 if heads % 4 == 0 and frames % 4 == 0 else 1
        self.planes = frames // self.group
        self.blocks = rows // BLOCK
        self.heads = heads // self.group
        bands = sum(2**band <= frames - 1 for band in range(1, NFAR // 2 + 1))
        self.slots = [*range(bands), *range(NFAR // 2, NFAR // 2 + bands)]
        self.square = self.group * self.group
        self.near0 = self.blocks
        self.far0 = self.blocks * (self.group + 2)
        self.total = self.far0 + self.planes * self.square

    def halo(self, step):
        step *= self.group
        return [(i, i + step) for i in range(self.frames) if 0 <= i + step < self.frames]

    def swap(self, j):
        g = self.group
        return [(i, i // g * g + (i % g ^ j)) for i in range(self.frames)]

    def lines(self):
        g = self.group
        return [[p * g + i for p in range(self.planes)] for i in range(g)]


def params():
    return dict(
        compiler_params=pltpu.CompilerParams(vmem_limit_bytes=VMEM_LIMIT),
        cost_estimate=pl.CostEstimate(flops=1, bytes_accessed=1, transcendentals=0),
    )


def select_body(scaled, n_after, group, place_ref, *refs):
    outs = refs[len(refs) - group :]
    refs = list(refs[: len(refs) - group - n_after])
    values = []
    for with_scale in scaled:
        x = refs.pop(0)[...]
        if with_scale:
            rs, gain = refs.pop(0), refs.pop(0)
            x = x.astype(jnp.float32) * rs[...] * gain[...]
        values.append(x.astype(jnp.bfloat16))
    for j, out in enumerate(outs):

        @pl.when(pl.program_id(0) == j)
        def _(out=out):
            for item, x in enumerate(values):
                out[item] = x


def select(plan, place, items, after):
    args, specs = [], []
    for x, head, rs, gain in items:

        def at(j, place, head=head):
            return 0, (place[1] ^ j) * plan.heads + head

        args.append(x)
        specs.append(pl.BlockSpec((plan.rows, HEAD_DIM), at))
        if rs is not None:
            args += [rs, gain]
            specs.append(pl.BlockSpec((plan.rows, 1), lambda j, place: (0, 0)))
            specs.append(pl.BlockSpec((1, HEAD_DIM), at))
    shape = (len(items), plan.rows, HEAD_DIM)
    scaled = [rs is not None for _, _, rs, _ in items]
    return pl.pallas_call(
        functools.partial(select_body, scaled, len(after), plan.group),
        grid_spec=pltpu.PrefetchScalarGridSpec(
            num_scalar_prefetch=1,
            grid=(plan.group,),
            in_specs=specs + [pl.BlockSpec(memory_space=pl.ANY)] * len(after),
            out_specs=[pl.BlockSpec(shape, lambda j, place: (0, 0, 0))] * plan.group,
        ),
        out_shape=[jax.ShapeDtypeStruct(shape, jnp.bfloat16)] * plan.group,
        name="select",
        **params(),
    )(place, *args, *after)


def pack_body(plan, n_after, place_ref, pick_ref, *refs):
    group, blocks = plan.group, plan.blocks
    xs = refs[:group]
    far, to_next, to_prev, sem = refs[group + n_after :]
    plane, lane = place_ref[0], place_ref[1]

    def copies(dest):
        made = []
        for f in range(group):
            for j in range(group):
                g = lane ^ j
                block = pick_ref[(dest * group + f) * plan.frames + plane * group + g]
                src = pl.ds(pl.multiple_of(block * BLOCK, BLOCK), BLOCK)
                dst = pl.ds(pl.multiple_of((f * group + g) * BLOCK, BLOCK), BLOCK)
                made.append(
                    pltpu.make_async_copy(
                        xs[j].at[:, src, :], far.at[dest, :, dst, :], sem.at[dest, len(made)]
                    )
                )
        return made

    def halo(act):
        for j in range(group):
            for at, (g, out) in enumerate(((group - 1, to_next), (0, to_prev))):

                @pl.when((lane ^ j) == g)
                def _(j=j, at=at, out=out):
                    act(pltpu.make_async_copy(xs[j], out, sem.at[plan.planes, at]))

    def for_each(act):
        halo(act)

        def one_plane(dest, carry):
            @pl.when(dest != plane)
            def _():
                for copy in copies(dest):
                    act(copy)

            return carry

        lax.fori_loop(0, plan.planes, one_plane, 0)

    for_each(lambda copy: copy.start())
    for_each(lambda copy: copy.wait())


def pack(plan, place, picks, xs, pair, after):
    smem = pl.BlockSpec(memory_space=pltpu.SMEM)
    any_spec = pl.BlockSpec(memory_space=pl.ANY)
    frame = jax.ShapeDtypeStruct((2, plan.rows, HEAD_DIM), jnp.bfloat16)
    far = jax.ShapeDtypeStruct((plan.planes, 2, plan.square * BLOCK, HEAD_DIM), jnp.bfloat16)
    return pl.pallas_call(
        functools.partial(pack_body, plan, len(after)),
        grid=(1,),
        in_specs=[smem, smem]
        + [pl.BlockSpec((2, plan.rows, HEAD_DIM), lambda i: (pair, 0, 0))] * plan.group
        + [any_spec] * len(after),
        out_specs=[any_spec] * 3,
        out_shape=[far, frame, frame],
        scratch_shapes=[pltpu.SemaphoreType.DMA((plan.planes + 1, max(plan.square, 2)))],
        name="pack",
        **params(),
    )(place, picks, *xs, *after)


def attend_body(plan, heads, at_out, n_out, *refs):
    place_ref, pos_ref = refs[:2]
    group, rows, nfar = plan.group, plan.rows, len(plan.slots)
    step = 2 * group + 3
    inputs = [refs[2 + h * step : 2 + (h + 1) * step] for h in range(len(heads))]
    refs = refs[2 + len(heads) * step + n_out :]
    outs, (qbuf, kvbuf, obuf, fark, farv, sem, out_sem) = refs[:group], refs[group:]
    plane, lane = place_ref[0], place_ref[1]
    scale = math.log2(math.e) / math.sqrt(HEAD_DIM)
    tile = min(rows, 256)
    per_tile = tile // BLOCK
    lanes = lax.broadcasted_iota(jnp.int32, (1, nfar * BLOCK), 1) // BLOCK
    contract = (((1,), (1,)), ((), ()))

    def copies(h):
        made, slot = [], h % 2
        qs, kvs, recvs = inputs[h][:group], inputs[h][group : 2 * group], inputs[h][2 * group :]
        at_q, at_k = heads[h]

        def add(src, dst):
            made.append(pltpu.make_async_copy(src, dst, sem.at[slot, len(made)]))

        def at(first, count):
            first = first * BLOCK
            if not isinstance(first, int):
                first = pl.multiple_of(first, BLOCK)
            return kvbuf.at[slot, :, pl.ds(first, count * BLOCK), :]

        for j in range(group):
            g = lane ^ j
            add(qs[j].at[at_q], qbuf.at[slot, g])
            add(kvs[j].at[at_k : at_k + 2], at(plan.near0 + g * plan.blocks, plan.blocks))
        far, before, after = recvs
        add(before, at(0, plan.blocks))
        add(after, at(plan.near0 + group * plan.blocks, plan.blocks))
        for p in range(plan.planes):
            add(far.at[p], at(plan.far0 + p * plan.square, plan.square))
        return made

    def one_frame(f, h):
        slot = h % 2
        first = pl.multiple_of((plan.near0 + (f - 1) * plan.blocks) * BLOCK, BLOCK)
        frame = plane * group + f
        for t in range(rows // tile):
            q = qbuf[slot, f, t * tile : (t + 1) * tile, :]
            scores = []
            for part, ok in enumerate((frame > 0, None, frame < plan.frames - 1)):
                k = kvbuf[slot, 0, pl.ds(first + part * rows, rows), :]
                s = lax.dot_general(q, k, contract, preferred_element_type=jnp.float32)
                scores.append(s if ok is None else jnp.where(ok, s, MASKED))
            far = []
            for i in range(per_tile):
                block = t * per_tile + i
                ok = lanes < 0
                for n in range(nfar):
                    at = pos_ref[(f * plan.blocks + block) * nfar + n]
                    src = pl.ds(pl.multiple_of(jnp.maximum(at, 0) * BLOCK, BLOCK), BLOCK)
                    fark[block, n * BLOCK : (n + 1) * BLOCK, :] = kvbuf[slot, 0, src, :]
                    farv[block, n * BLOCK : (n + 1) * BLOCK, :] = kvbuf[slot, 1, src, :]
                    ok = ok | ((lanes == n) & (at >= 0))
                s = lax.dot_general(
                    q[i * BLOCK : (i + 1) * BLOCK],
                    fark[block],
                    contract,
                    preferred_element_type=jnp.float32,
                )
                far.append(jnp.where(ok, s, MASKED))
            far = jnp.concatenate(far, axis=0)
            peak = jnp.max(far, axis=1, keepdims=True)
            for s in scores:
                peak = jnp.maximum(peak, jnp.max(s, axis=1, keepdims=True))
            total, out = 0.0, 0.0
            for part, s in enumerate(scores):
                p = jnp.exp2((s - peak) * scale)
                total += jnp.sum(p, axis=1, keepdims=True)
                v = kvbuf[slot, 1, pl.ds(first + part * rows, rows), :]
                out += jnp.dot(p.astype(jnp.bfloat16), v, preferred_element_type=jnp.float32)
            p = jnp.exp2((far - peak) * scale)
            total += jnp.sum(p, axis=1, keepdims=True)
            p = p.astype(jnp.bfloat16)
            far_out = [
                jnp.dot(
                    p[i * BLOCK : (i + 1) * BLOCK],
                    farv[t * per_tile + i],
                    preferred_element_type=jnp.float32,
                )
                for i in range(per_tile)
            ]
            out = (out + jnp.concatenate(far_out, axis=0)) / total
            obuf[f, h, t * tile : (t + 1) * tile, :] = out.astype(jnp.bfloat16)

    for copy in copies(0):
        copy.start()
    for h in range(len(heads)):
        if h + 1 < len(heads):
            for copy in copies(h + 1):
                copy.start()
        for copy in copies(h):
            copy.wait()
        lax.fori_loop(0, group, lambda f, c, h=h: (one_frame(f, h), c)[1], 0)
    made = []
    for j in range(group):
        dst = outs[j].at[at_out : at_out + len(heads)]
        made.append(pltpu.make_async_copy(obuf.at[lane ^ j], dst, out_sem.at[j]))
    for copy in made:
        copy.start()
    for copy in made:
        copy.wait()


def attend(plan, place, pos, heads, at_out, of, outs):
    nfar, count = len(plan.slots), len(heads)
    any_spec = pl.BlockSpec(memory_space=pl.ANY)
    smem = pl.BlockSpec(memory_space=pltpu.SMEM)
    args = [y for q, _, kv, _, recv in heads for y in (*q, *kv, *recv)]
    items = [(at_q, at_k) for _, at_q, _, at_k, _ in heads]
    shape = jax.ShapeDtypeStruct((of, plan.rows, HEAD_DIM), jnp.bfloat16)
    return pl.pallas_call(
        functools.partial(attend_body, plan, items, at_out, len(outs)),
        in_specs=[smem, smem] + [any_spec] * (len(args) + len(outs)),
        out_specs=[any_spec] * plan.group,
        out_shape=[shape] * plan.group,
        input_output_aliases={2 + len(args) + j: j for j in range(len(outs))},
        scratch_shapes=[
            pltpu.VMEM((2, plan.group, plan.rows, HEAD_DIM), jnp.bfloat16),
            pltpu.VMEM((2, 2, plan.total * BLOCK, HEAD_DIM), jnp.bfloat16),
            pltpu.VMEM((plan.group, count, plan.rows, HEAD_DIM), jnp.bfloat16),
            pltpu.VMEM((plan.blocks, nfar * BLOCK, HEAD_DIM), jnp.bfloat16),
            pltpu.VMEM((plan.blocks, nfar * BLOCK, HEAD_DIM), jnp.bfloat16),
            pltpu.SemaphoreType.DMA((2, 2 * plan.group + 2 + plan.planes)),
            pltpu.SemaphoreType.DMA((plan.group,)),
        ],
        name="attend",
        **params(),
    )(place, pos, *args, *outs)


def merge_body(plan, first, place_ref, *refs):
    xs, (out, sem) = refs[: plan.group], refs[-2:]
    copies = []
    for j, x in enumerate(xs):
        for h in range(x.shape[0]):
            start = ((place_ref[1] ^ j) * plan.heads + first + h) * HEAD_DIM
            dst = out.at[:, pl.ds(pl.multiple_of(start, HEAD_DIM), HEAD_DIM)]
            copies.append(pltpu.make_async_copy(x.at[h], dst, sem.at[len(copies)]))
    for copy in copies:
        copy.start()
    for copy in copies:
        copy.wait()


def merge(plan, place, xs, first, out):
    width = plan.group * plan.heads * HEAD_DIM
    any_spec = pl.BlockSpec(memory_space=pl.ANY)
    vmem = pl.BlockSpec(memory_space=pltpu.VMEM)
    return pl.pallas_call(
        functools.partial(merge_body, plan, first),
        in_specs=[pl.BlockSpec(memory_space=pltpu.SMEM)]
        + [vmem] * plan.group
        + [any_spec] * len(out),
        out_specs=any_spec,
        out_shape=jax.ShapeDtypeStruct((plan.rows, width), jnp.bfloat16),
        input_output_aliases={1 + plan.group: 0} if out else {},
        scratch_shapes=[pltpu.SemaphoreType.DMA((plan.group * xs[0].shape[0],))],
        name="merge",
        **params(),
    )(place, *xs, *out)


def far_positions(plan, plane, far_frames, far_pick):
    group, blocks = plan.group, plan.blocks
    own = group * blocks
    lists = lax.dynamic_slice_in_dim(far_frames, plane * own, own, 0)
    lists = jnp.concatenate([lists[:, s : s + 1] for s in plan.slots], axis=1)
    g = jnp.maximum(lists, 0)
    rows = lax.dynamic_slice_in_dim(far_pick, plane * group, group, 0)
    rows = jnp.repeat(rows, blocks, axis=0)
    hit = g[:, :, None] == jnp.arange(plan.frames)
    pick = jnp.sum(jnp.where(hit, rows[:, None, :], 0), axis=2)
    f = (jnp.arange(own) // blocks)[:, None]
    source, lane = g // group, g % group
    pos = plan.far0 + (source * group + f) * group + lane
    away = g - plane * group
    near = (away >= -1) & (away <= group)
    pos = jnp.where(near, plan.near0 + away * blocks + pick, pos)
    return jnp.where(lists >= 0, pos, -1).astype(jnp.int32).reshape(-1)


def local(query, key, value, q_gain, k_gain, far_frames, far_pick):
    rows, width = query.shape
    full_width = width * lax.axis_size("head")
    plan = Plan(lax.axis_size("tm"), rows, width // HEAD_DIM)
    frame = lax.axis_index("tm").astype(jnp.int32)
    plane = frame // plan.group
    place = jnp.stack([plane, frame % plan.group])
    picks = far_pick.reshape(-1)

    def share(xs):
        return [xs[0]] + [lax.ppermute(xs[j], "tm", plan.swap(j)) for j in range(1, plan.group)]

    def exchange(xs, pair, after):
        far, to_next, to_prev = pack(plan, place, picks, xs, pair, after)
        packed.append([far])
        return (
            lax.all_to_all(far, "tm", 0, 0, axis_index_groups=plan.lines(), tiled=True),
            lax.ppermute(to_next, "tm", plan.halo(1)),
            lax.ppermute(to_prev, "tm", plan.halo(-1)),
        )

    sums = jnp.stack([jnp.sum(jnp.square(x.astype(jnp.float32)), axis=1) for x in (query, key)])
    q_rs, k_rs = lax.rsqrt(lax.psum(sums, "head") / full_width + EPSILON)[:, :, None]
    q_gain, k_gain = q_gain[None, :], k_gain[None, :]

    def pair(h):
        return [(key, h, k_rs, k_gain), (value, h, None, None)]

    heads = plan.heads
    queries = [(query, h, q_rs, q_gain) for h in range(heads)]
    rounds = [[h] for h in range(min(2, heads))]
    if heads > 3:
        rounds.append(list(range(2, heads - 1)))
    if heads > 2:
        rounds.append([heads - 1])
    packed, recvs, where, after, rest = [], [], [], [], []

    def near():
        return list(recvs[-1][1:]) if recvs else []

    for index, chosen in enumerate(rounds):
        items = [item for h in chosen for item in pair(h)]
        ending = index + 1 == len(rounds)
        x = share(select(plan, place, items + (queries if ending else []), after))
        for old, n in rest:
            recvs.append(exchange(old, n, near() + x))
        where += [(x, 2 * n) for n in range(len(chosen))]
        if not ending:
            recvs.append(exchange(x, 0, near()))
            after = packed[-1]
            rest = [(x, n) for n in range(1, len(chosen))]
    pos = far_positions(plan, plane, far_frames, far_pick)

    def run(chosen, at_out, of, out):
        args = [(x, len(items) + h, *where[h], recvs[h]) for h in chosen]
        return list(attend(plan, place, pos, args, at_out, of, out))

    early = min(2, heads - 1)
    first, out = [], []
    if early:
        first = run(range(early), 0, early, [])
    recvs.append(exchange(x, 0, near() + first))
    if early:
        out = [merge(plan, place, share(first), 0, [])]
    held = []
    for h in range(early, heads):
        held = run([h], h - early, heads - early, held)
    return merge(plan, place, share(held), early, out)


def solution(mesh):
    placed = (P("tm", "head"), P("tm", "head"), P("tm", "head"), P("head"), P("head"), P(), P())
    return jax.shard_map(
        local, mesh=mesh, in_specs=placed, out_specs=P("tm", "head"), check_vma=False
    )
```

```python
import functools
import math

import jax
import jax.numpy as jnp
from jax import lax
from jax.experimental import pallas as pl
from jax.experimental.pallas import tpu as pltpu
from jax.sharding import PartitionSpec as P

HEAD_DIM = 128
BLOCK = 64
NFAR = 12
EPSILON = 1e-06
MASKED = -1e30
VMEM_LIMIT = 56 * 1024 * 1024


class Plan:
    def __init__(self, frames, rows, heads):
        self.frames, self.rows = frames, rows
        self.group = 4 if heads % 4 == 0 and frames % 4 == 0 else 1
        self.planes = frames // self.group
        self.blocks = rows // BLOCK
        self.heads = heads // self.group
        bands = sum(2**band <= frames - 1 for band in range(1, NFAR // 2 + 1))
        self.slots = [*range(bands), *range(NFAR // 2, NFAR // 2 + bands)]
        self.square = self.group * self.group
        self.near0 = self.blocks
        self.far0 = self.blocks * (self.group + 2)
        self.total = self.far0 + self.planes * self.square

    def halo(self, step):
        step *= self.group
        return [(i, i + step) for i in range(self.frames) if 0 <= i + step < self.frames]

    def swap(self, j):
        g = self.group
        return [(i, i // g * g + (i % g ^ j)) for i in range(self.frames)]

    def lines(self):
        g = self.group
        return [[p * g + i for p in range(self.planes)] for i in range(g)]


def params():
    return dict(
        compiler_params=pltpu.CompilerParams(vmem_limit_bytes=VMEM_LIMIT),
        cost_estimate=pl.CostEstimate(flops=1, bytes_accessed=1, transcendentals=0),
    )


def select_body(scaled, n_after, group, place_ref, *refs):
    outs = refs[len(refs) - group :]
    refs = list(refs[: len(refs) - group - n_after])
    values = []
    for with_scale in scaled:
        x = refs.pop(0)[...]
        if with_scale:
            rs, gain = refs.pop(0), refs.pop(0)
            x = x.astype(jnp.float32) * rs[...] * gain[...]
        values.append(x.astype(jnp.bfloat16))
    for j, out in enumerate(outs):

        @pl.when(pl.program_id(0) == j)
        def _(out=out):
            for item, x in enumerate(values):
                out[item] = x


def select(plan, place, items, after):
    args, specs = [], []
    for x, head, rs, gain in items:

        def at(j, place, head=head):
            return 0, (place[1] ^ j) * plan.heads + head

        args.append(x)
        specs.append(pl.BlockSpec((plan.rows, HEAD_DIM), at))
        if rs is not None:
            args += [rs, gain]
            specs.append(pl.BlockSpec((plan.rows, 1), lambda j, place: (0, 0)))
            specs.append(pl.BlockSpec((1, HEAD_DIM), at))
    shape = (len(items), plan.rows, HEAD_DIM)
    scaled = [rs is not None for _, _, rs, _ in items]
    return pl.pallas_call(
        functools.partial(select_body, scaled, len(after), plan.group),
        grid_spec=pltpu.PrefetchScalarGridSpec(
            num_scalar_prefetch=1,
            grid=(plan.group,),
            in_specs=specs + [pl.BlockSpec(memory_space=pl.ANY)] * len(after),
            out_specs=[pl.BlockSpec(shape, lambda j, place: (0, 0, 0))] * plan.group,
        ),
        out_shape=[jax.ShapeDtypeStruct(shape, jnp.bfloat16)] * plan.group,
        name="select",
        **params(),
    )(place, *args, *after)


def pack_body(plan, n_after, place_ref, pick_ref, *refs):
    group, blocks = plan.group, plan.blocks
    xs = refs[:group]
    far, to_next, to_prev, sem = refs[group + n_after :]
    plane, lane = place_ref[0], place_ref[1]

    def copies(dest):
        made = []
        for f in range(group):
            for j in range(group):
                g = lane ^ j
                block = pick_ref[(dest * group + f) * plan.frames + plane * group + g]
                src = pl.ds(pl.multiple_of(block * BLOCK, BLOCK), BLOCK)
                dst = pl.ds(pl.multiple_of((f * group + g) * BLOCK, BLOCK), BLOCK)
                made.append(
                    pltpu.make_async_copy(
                        xs[j].at[:, src, :], far.at[dest, :, dst, :], sem.at[dest, len(made)]
                    )
                )
        return made

    def halo(act):
        for j in range(group):
            for at, (g, out) in enumerate(((group - 1, to_next), (0, to_prev))):

                @pl.when((lane ^ j) == g)
                def _(j=j, at=at, out=out):
                    act(pltpu.make_async_copy(xs[j], out, sem.at[plan.planes, at]))

    def for_each(act):
        halo(act)

        def one_plane(dest, carry):
            @pl.when(dest != plane)
            def _():
                for copy in copies(dest):
                    act(copy)

            return carry

        lax.fori_loop(0, plan.planes, one_plane, 0)

    for_each(lambda copy: copy.start())
    for_each(lambda copy: copy.wait())


def pack(plan, place, picks, xs, pair, after):
    smem = pl.BlockSpec(memory_space=pltpu.SMEM)
    any_spec = pl.BlockSpec(memory_space=pl.ANY)
    frame = jax.ShapeDtypeStruct((2, plan.rows, HEAD_DIM), jnp.bfloat16)
    far = jax.ShapeDtypeStruct((plan.planes, 2, plan.square * BLOCK, HEAD_DIM), jnp.bfloat16)
    return pl.pallas_call(
        functools.partial(pack_body, plan, len(after)),
        grid=(1,),
        in_specs=[smem, smem]
        + [pl.BlockSpec((2, plan.rows, HEAD_DIM), lambda i: (pair, 0, 0))] * plan.group
        + [any_spec] * len(after),
        out_specs=[any_spec] * 3,
        out_shape=[far, frame, frame],
        scratch_shapes=[pltpu.SemaphoreType.DMA((plan.planes + 1, max(plan.square, 2)))],
        name="pack",
        **params(),
    )(place, picks, *xs, *after)


def attend_body(plan, heads, n_wait, *refs):
    place_ref, pos_ref = refs[:2]
    group, rows, nfar = plan.group, plan.rows, len(plan.slots)
    step = 2 * group + 3
    inputs = [refs[2 + h * step : 2 + (h + 1) * step] for h in range(len(heads))]
    refs = refs[2 + len(heads) * step + n_wait :]
    outs, (qbuf, kvbuf, obuf, fark, farv, sem, out_sem) = refs[:group], refs[group:]
    plane, lane = place_ref[0], place_ref[1]
    scale = math.log2(math.e) / math.sqrt(HEAD_DIM)
    tile = min(rows, 256)
    per_tile = tile // BLOCK
    lanes = lax.broadcasted_iota(jnp.int32, (1, nfar * BLOCK), 1) // BLOCK
    contract = (((1,), (1,)), ((), ()))

    def copies(h):
        made, slot = [], h % 2
        qs, kvs, recvs = inputs[h][:group], inputs[h][group : 2 * group], inputs[h][2 * group :]
        at_q, at_k = heads[h]

        def add(src, dst):
            made.append(pltpu.make_async_copy(src, dst, sem.at[slot, len(made)]))

        def at(first, count):
            first = first * BLOCK
            if not isinstance(first, int):
                first = pl.multiple_of(first, BLOCK)
            return kvbuf.at[slot, :, pl.ds(first, count * BLOCK), :]

        for j in range(group):
            g = lane ^ j
            add(qs[j].at[at_q], qbuf.at[slot, g])
            add(kvs[j].at[at_k : at_k + 2], at(plan.near0 + g * plan.blocks, plan.blocks))
        far, before, after = recvs
        add(before, at(0, plan.blocks))
        add(after, at(plan.near0 + group * plan.blocks, plan.blocks))
        for p in range(plan.planes):
            add(far.at[p], at(plan.far0 + p * plan.square, plan.square))
        return made

    def one_frame(f, h):
        slot = h % 2
        first = pl.multiple_of((plan.near0 + (f - 1) * plan.blocks) * BLOCK, BLOCK)
        frame = plane * group + f
        for t in range(rows // tile):
            q = qbuf[slot, f, t * tile : (t + 1) * tile, :]
            scores = []
            for part, ok in enumerate((frame > 0, None, frame < plan.frames - 1)):
                k = kvbuf[slot, 0, pl.ds(first + part * rows, rows), :]
                s = lax.dot_general(q, k, contract, preferred_element_type=jnp.float32)
                scores.append(s if ok is None else jnp.where(ok, s, MASKED))
            far = []
            for i in range(per_tile):
                block = t * per_tile + i
                ok = lanes < 0
                for n in range(nfar):
                    at = pos_ref[(f * plan.blocks + block) * nfar + n]
                    src = pl.ds(pl.multiple_of(jnp.maximum(at, 0) * BLOCK, BLOCK), BLOCK)
                    fark[block, n * BLOCK : (n + 1) * BLOCK, :] = kvbuf[slot, 0, src, :]
                    farv[block, n * BLOCK : (n + 1) * BLOCK, :] = kvbuf[slot, 1, src, :]
                    ok = ok | ((lanes == n) & (at >= 0))
                s = lax.dot_general(
                    q[i * BLOCK : (i + 1) * BLOCK],
                    fark[block],
                    contract,
                    preferred_element_type=jnp.float32,
                )
                far.append(jnp.where(ok, s, MASKED))
            far = jnp.concatenate(far, axis=0)
            peak = jnp.max(far, axis=1, keepdims=True)
            for s in scores:
                peak = jnp.maximum(peak, jnp.max(s, axis=1, keepdims=True))
            total, out = 0.0, 0.0
            for part, s in enumerate(scores):
                p = jnp.exp2((s - peak) * scale)
                total += jnp.sum(p, axis=1, keepdims=True)
                v = kvbuf[slot, 1, pl.ds(first + part * rows, rows), :]
                out += jnp.dot(p.astype(jnp.bfloat16), v, preferred_element_type=jnp.float32)
            p = jnp.exp2((far - peak) * scale)
            total += jnp.sum(p, axis=1, keepdims=True)
            p = p.astype(jnp.bfloat16)
            far_out = [
                jnp.dot(
                    p[i * BLOCK : (i + 1) * BLOCK],
                    farv[t * per_tile + i],
                    preferred_element_type=jnp.float32,
                )
                for i in range(per_tile)
            ]
            out = (out + jnp.concatenate(far_out, axis=0)) / total
            obuf[f, h, t * tile : (t + 1) * tile, :] = out.astype(jnp.bfloat16)

    for copy in copies(0):
        copy.start()
    for h in range(len(heads)):
        if h + 1 < len(heads):
            for copy in copies(h + 1):
                copy.start()
        for copy in copies(h):
            copy.wait()
        lax.fori_loop(0, group, lambda f, c, h=h: (one_frame(f, h), c)[1], 0)
    made = []
    for j in range(group):
        made.append(pltpu.make_async_copy(obuf.at[lane ^ j], outs[j], out_sem.at[j]))
    for copy in made:
        copy.start()
    for copy in made:
        copy.wait()


def attend(plan, place, pos, heads, wait):
    nfar, count = len(plan.slots), len(heads)
    any_spec = pl.BlockSpec(memory_space=pl.ANY)
    smem = pl.BlockSpec(memory_space=pltpu.SMEM)
    args = [y for q, _, kv, _, recv in heads for y in (*q, *kv, *recv)]
    items = [(at_q, at_k) for _, at_q, _, at_k, _ in heads]
    shape = jax.ShapeDtypeStruct((count, plan.rows, HEAD_DIM), jnp.bfloat16)
    return pl.pallas_call(
        functools.partial(attend_body, plan, items, len(wait)),
        in_specs=[smem, smem] + [any_spec] * (len(args) + len(wait)),
        out_specs=[any_spec] * plan.group,
        out_shape=[shape] * plan.group,
        scratch_shapes=[
            pltpu.VMEM((2, plan.group, plan.rows, HEAD_DIM), jnp.bfloat16),
            pltpu.VMEM((2, 2, plan.total * BLOCK, HEAD_DIM), jnp.bfloat16),
            pltpu.VMEM((plan.group, count, plan.rows, HEAD_DIM), jnp.bfloat16),
            pltpu.VMEM((plan.blocks, nfar * BLOCK, HEAD_DIM), jnp.bfloat16),
            pltpu.VMEM((plan.blocks, nfar * BLOCK, HEAD_DIM), jnp.bfloat16),
            pltpu.SemaphoreType.DMA((2, 2 * plan.group + 2 + plan.planes)),
            pltpu.SemaphoreType.DMA((plan.group,)),
        ],
        name="attend",
        **params(),
    )(place, pos, *args, *wait)


def merge_body(plan, first, place_ref, *refs):
    xs, (out, sem) = refs[: plan.group], refs[-2:]
    copies = []
    for j, x in enumerate(xs):
        for h in range(x.shape[0]):
            start = ((place_ref[1] ^ j) * plan.heads + first + h) * HEAD_DIM
            dst = out.at[:, pl.ds(pl.multiple_of(start, HEAD_DIM), HEAD_DIM)]
            copies.append(pltpu.make_async_copy(x.at[h], dst, sem.at[len(copies)]))
    for copy in copies:
        copy.start()
    for copy in copies:
        copy.wait()


def merge(plan, place, xs, first, out):
    width = plan.group * plan.heads * HEAD_DIM
    any_spec = pl.BlockSpec(memory_space=pl.ANY)
    vmem = pl.BlockSpec(memory_space=pltpu.VMEM)
    return pl.pallas_call(
        functools.partial(merge_body, plan, first),
        in_specs=[pl.BlockSpec(memory_space=pltpu.SMEM)]
        + [vmem] * plan.group
        + [any_spec] * len(out),
        out_specs=any_spec,
        out_shape=jax.ShapeDtypeStruct((plan.rows, width), jnp.bfloat16),
        input_output_aliases={1 + plan.group: 0} if out else {},
        scratch_shapes=[pltpu.SemaphoreType.DMA((plan.group * xs[0].shape[0],))],
        name="merge",
        **params(),
    )(place, *xs, *out)


def far_positions(plan, plane, far_frames, far_pick):
    group, blocks = plan.group, plan.blocks
    own = group * blocks
    lists = lax.dynamic_slice_in_dim(far_frames, plane * own, own, 0)
    lists = jnp.concatenate([lists[:, s : s + 1] for s in plan.slots], axis=1)
    g = jnp.maximum(lists, 0)
    rows = lax.dynamic_slice_in_dim(far_pick, plane * group, group, 0)
    rows = jnp.repeat(rows, blocks, axis=0)
    hit = g[:, :, None] == jnp.arange(plan.frames)
    pick = jnp.sum(jnp.where(hit, rows[:, None, :], 0), axis=2)
    f = (jnp.arange(own) // blocks)[:, None]
    source, lane = g // group, g % group
    pos = plan.far0 + (source * group + f) * group + lane
    away = g - plane * group
    near = (away >= -1) & (away <= group)
    pos = jnp.where(near, plan.near0 + away * blocks + pick, pos)
    return jnp.where(lists >= 0, pos, -1).astype(jnp.int32).reshape(-1)


def local(query, key, value, q_gain, k_gain, far_frames, far_pick):
    rows, width = query.shape
    full_width = width * lax.axis_size("head")
    plan = Plan(lax.axis_size("tm"), rows, width // HEAD_DIM)
    frame = lax.axis_index("tm").astype(jnp.int32)
    plane = frame // plan.group
    place = jnp.stack([plane, frame % plan.group])
    picks = far_pick.reshape(-1)

    def share(xs):
        return [xs[0]] + [lax.ppermute(xs[j], "tm", plan.swap(j)) for j in range(1, plan.group)]

    def exchange(xs, pair, after):
        far, to_next, to_prev = pack(plan, place, picks, xs, pair, after)
        packed.append([far])
        return (
            lax.all_to_all(far, "tm", 0, 0, axis_index_groups=plan.lines(), tiled=True),
            lax.ppermute(to_next, "tm", plan.halo(1)),
            lax.ppermute(to_prev, "tm", plan.halo(-1)),
        )

    sums = jnp.stack([jnp.sum(jnp.square(x.astype(jnp.float32)), axis=1) for x in (query, key)])
    q_rs, k_rs = lax.rsqrt(lax.psum(sums, "head") / full_width + EPSILON)[:, :, None]
    q_gain, k_gain = q_gain[None, :], k_gain[None, :]

    def pair(h):
        return [(key, h, k_rs, k_gain), (value, h, None, None)]

    heads = plan.heads
    queries = [(query, h, q_rs, q_gain) for h in range(heads)]
    rounds = [[h] for h in range(min(2, heads))]
    if heads > 3:
        rounds.append(list(range(2, heads - 1)))
    if heads > 2:
        rounds.append([heads - 1])
    packed, recvs, where, after, rest = [], [], [], [], []

    def near():
        return list(recvs[-2][1:]) if len(recvs) > 1 else []

    for index, chosen in enumerate(rounds):
        items = [item for h in chosen for item in pair(h)]
        ending = index + 1 == len(rounds)
        x = share(select(plan, place, items + (queries if ending else []), after))
        for old, n in rest:
            recvs.append(exchange(old, n, near() + x))
        where += [(x, 2 * n) for n in range(len(chosen))]
        if not ending:
            recvs.append(exchange(x, 0, near()))
            after = packed[-1]
            rest = [(x, n) for n in range(1, len(chosen))]
    pos = far_positions(plan, plane, far_frames, far_pick)

    def run(chosen, wait):
        args = [(x, len(items) + h, *where[h], recvs[h]) for h in chosen]
        return list(attend(plan, place, pos, args, wait))

    early = min(2, heads - 1)
    first, out = [], []
    if early:
        first = run(range(early), [])
    recvs.append(exchange(x, 0, near() + first))
    if early:
        out = [merge(plan, place, share(first), 0, out)]
    for h in range(early, heads - 1, 2):
        chosen = range(h, min(h + 2, heads - 1))
        out = [merge(plan, place, share(run(chosen, [])), h, out)]
    return merge(plan, place, share(run([heads - 1], out)), heads - 1, out)


def solution(mesh):
    placed = (P("tm", "head"), P("tm", "head"), P("tm", "head"), P("head"), P("head"), P(), P())
    return jax.shard_map(
        local, mesh=mesh, in_specs=placed, out_specs=P("tm", "head"), check_vma=False
    )
```

```python
import functools
import math

import jax
import jax.numpy as jnp
from jax import lax
from jax.experimental import pallas as pl
from jax.experimental.pallas import tpu as pltpu
from jax.sharding import PartitionSpec as P

HEAD_DIM = 128
BLOCK = 64
NFAR = 12
EPSILON = 1e-06
MASKED = -1e30
VMEM_LIMIT = 56 * 1024 * 1024


class Plan:
    def __init__(self, frames, rows, heads):
        self.frames, self.rows = frames, rows
        self.group = 4 if heads % 4 == 0 and frames % 4 == 0 else 1
        self.planes = frames // self.group
        self.blocks = rows // BLOCK
        self.heads = heads // self.group
        bands = sum(2**band <= frames - 1 for band in range(1, NFAR // 2 + 1))
        self.slots = [*range(bands), *range(NFAR // 2, NFAR // 2 + bands)]
        full = self.group * self.group
        self.rooms = sorted({full * 13 // 16, full * 14 // 16, full}) if self.group > 1 else [full]
        self.near0 = self.blocks
        self.far0 = self.blocks * (self.group + 2)

    def total(self, room):
        return self.far0 + self.planes * room

    def halo(self, step):
        step *= self.group
        return [(i, i + step) for i in range(self.frames) if 0 <= i + step < self.frames]

    def swap(self, j):
        g = self.group
        return [(i, i // g * g + (i % g ^ j)) for i in range(self.frames)]

    def lines(self):
        g = self.group
        return [[p * g + i for p in range(self.planes)] for i in range(g)]


def params():
    return dict(
        compiler_params=pltpu.CompilerParams(vmem_limit_bytes=VMEM_LIMIT),
        cost_estimate=pl.CostEstimate(flops=1, bytes_accessed=1, transcendentals=0),
    )


def select_body(scaled, n_after, group, place_ref, *refs):
    outs = refs[len(refs) - group :]
    refs = list(refs[: len(refs) - group - n_after])
    values = []
    for with_scale in scaled:
        x = refs.pop(0)[...]
        if with_scale:
            rs, gain = refs.pop(0), refs.pop(0)
            x = x.astype(jnp.float32) * rs[...] * gain[...]
        values.append(x.astype(jnp.bfloat16))
    for j, out in enumerate(outs):

        @pl.when(pl.program_id(0) == j)
        def _(out=out):
            for item, x in enumerate(values):
                out[item] = x


def select(plan, place, items, after):
    args, specs = [], []
    for x, head, rs, gain in items:

        def at(j, place, head=head):
            return 0, (place[1] ^ j) * plan.heads + head

        args.append(x)
        specs.append(pl.BlockSpec((plan.rows, HEAD_DIM), at))
        if rs is not None:
            args += [rs, gain]
            specs.append(pl.BlockSpec((plan.rows, 1), lambda j, place: (0, 0)))
            specs.append(pl.BlockSpec((1, HEAD_DIM), at))
    shape = (len(items), plan.rows, HEAD_DIM)
    scaled = [rs is not None for _, _, rs, _ in items]
    return pl.pallas_call(
        functools.partial(select_body, scaled, len(after), plan.group),
        grid_spec=pltpu.PrefetchScalarGridSpec(
            num_scalar_prefetch=1,
            grid=(plan.group,),
            in_specs=specs + [pl.BlockSpec(memory_space=pl.ANY)] * len(after),
            out_specs=[pl.BlockSpec(shape, lambda j, place: (0, 0, 0))] * plan.group,
        ),
        out_shape=[jax.ShapeDtypeStruct(shape, jnp.bfloat16)] * plan.group,
        name="select",
        **params(),
    )(place, *args, *after)


def pack_body(plan, place_ref, slot_ref, *refs):
    group, blocks = plan.group, plan.blocks
    xs = refs[:group]
    far, to_next, to_prev, sem = refs[group:]
    plane, lane = place_ref[0], place_ref[1]

    def halo(act):
        for j in range(group):
            for at, (g, out) in enumerate(((group - 1, to_next), (0, to_prev))):

                @pl.when((lane ^ j) == g)
                def _(j=j, at=at, out=out):
                    act(pltpu.make_async_copy(xs[j], out, sem.at[plan.planes, at]))

    def for_each(act):
        halo(act)

        def one_plane(dest, carry):
            for j in range(group):
                for b in range(blocks):
                    slot = slot_ref[(dest * group + (lane ^ j)) * blocks + b]

                    @pl.when(slot >= 0)
                    def _(j=j, b=b, slot=slot):
                        dst = pl.ds(pl.multiple_of(slot * BLOCK, BLOCK), BLOCK)
                        src = xs[j].at[:, b * BLOCK : (b + 1) * BLOCK, :]
                        place = sem.at[dest, j * blocks + b]
                        act(pltpu.make_async_copy(src, far.at[dest, :, dst, :], place))

            return carry

        lax.fori_loop(0, plan.planes, one_plane, 0)

    for_each(lambda copy: copy.start())
    for_each(lambda copy: copy.wait())


def pack(plan, room, place, slots, xs, pair):
    smem = pl.BlockSpec(memory_space=pltpu.SMEM)
    any_spec = pl.BlockSpec(memory_space=pl.ANY)
    frame = jax.ShapeDtypeStruct((2, plan.rows, HEAD_DIM), jnp.bfloat16)
    far = jax.ShapeDtypeStruct((plan.planes, 2, room * BLOCK, HEAD_DIM), jnp.bfloat16)
    return pl.pallas_call(
        functools.partial(pack_body, plan),
        grid=(1,),
        in_specs=[smem, smem]
        + [pl.BlockSpec((2, plan.rows, HEAD_DIM), lambda i: (pair, 0, 0))] * plan.group,
        out_specs=[any_spec] * 3,
        out_shape=[far, frame, frame],
        scratch_shapes=[pltpu.SemaphoreType.DMA((plan.planes + 1, plan.group * plan.blocks))],
        name="pack",
        **params(),
    )(place, slots, *xs)


def hold_body(*refs):
    pass


def hold(x, after):
    any_spec = pl.BlockSpec(memory_space=pl.ANY)
    return pl.pallas_call(
        hold_body,
        in_specs=[any_spec] * (1 + len(after)),
        out_specs=any_spec,
        out_shape=jax.ShapeDtypeStruct(x.shape, x.dtype),
        input_output_aliases={0: 0},
        name="hold",
        **params(),
    )(x, *after)


def attend_body(plan, room, heads, n_wait, *refs):
    place_ref, pos_ref = refs[:2]
    group, rows, nfar = plan.group, plan.rows, len(plan.slots)
    step = 2 * group + 3
    inputs = [refs[2 + h * step : 2 + (h + 1) * step] for h in range(len(heads))]
    refs = refs[2 + len(heads) * step + n_wait :]
    outs, (qbuf, kvbuf, obuf, fark, farv, sem, out_sem) = refs[:group], refs[group:]
    plane, lane = place_ref[0], place_ref[1]
    scale = math.log2(math.e) / math.sqrt(HEAD_DIM)
    tile = min(rows, 256)
    per_tile = tile // BLOCK
    lanes = lax.broadcasted_iota(jnp.int32, (1, nfar * BLOCK), 1) // BLOCK
    contract = (((1,), (1,)), ((), ()))

    def copies(h):
        made, slot = [], h % 2
        qs, kvs, recvs = inputs[h][:group], inputs[h][group : 2 * group], inputs[h][2 * group :]
        at_q, at_k = heads[h]

        def add(src, dst):
            made.append(pltpu.make_async_copy(src, dst, sem.at[slot, len(made)]))

        def at(first, count):
            first = first * BLOCK
            if not isinstance(first, int):
                first = pl.multiple_of(first, BLOCK)
            return kvbuf.at[slot, :, pl.ds(first, count * BLOCK), :]

        for j in range(group):
            g = lane ^ j
            add(qs[j].at[at_q], qbuf.at[slot, g])
            add(kvs[j].at[at_k : at_k + 2], at(plan.near0 + g * plan.blocks, plan.blocks))
        far, before, after = recvs
        add(before, at(0, plan.blocks))
        add(after, at(plan.near0 + group * plan.blocks, plan.blocks))
        for p in range(plan.planes):
            add(far.at[p], at(plan.far0 + p * room, room))
        return made

    def one_frame(f, h):
        slot = h % 2
        first = pl.multiple_of((plan.near0 + (f - 1) * plan.blocks) * BLOCK, BLOCK)
        frame = plane * group + f
        for t in range(rows // tile):
            q = qbuf[slot, f, t * tile : (t + 1) * tile, :]
            scores = []
            for part, ok in enumerate((frame > 0, None, frame < plan.frames - 1)):
                k = kvbuf[slot, 0, pl.ds(first + part * rows, rows), :]
                s = lax.dot_general(q, k, contract, preferred_element_type=jnp.float32)
                scores.append(s if ok is None else jnp.where(ok, s, MASKED))
            far = []
            for i in range(per_tile):
                block = t * per_tile + i
                ok = lanes < 0
                for n in range(nfar):
                    at = pos_ref[(f * plan.blocks + block) * nfar + n]
                    src = pl.ds(pl.multiple_of(jnp.maximum(at, 0) * BLOCK, BLOCK), BLOCK)
                    fark[block, n * BLOCK : (n + 1) * BLOCK, :] = kvbuf[slot, 0, src, :]
                    farv[block, n * BLOCK : (n + 1) * BLOCK, :] = kvbuf[slot, 1, src, :]
                    ok = ok | ((lanes == n) & (at >= 0))
                s = lax.dot_general(
                    q[i * BLOCK : (i + 1) * BLOCK],
                    fark[block],
                    contract,
                    preferred_element_type=jnp.float32,
                )
                far.append(jnp.where(ok, s, MASKED))
            far = jnp.concatenate(far, axis=0)
            peak = jnp.max(far, axis=1, keepdims=True)
            for s in scores:
                peak = jnp.maximum(peak, jnp.max(s, axis=1, keepdims=True))
            total, out = 0.0, 0.0
            for part, s in enumerate(scores):
                p = jnp.exp2((s - peak) * scale)
                total += jnp.sum(p, axis=1, keepdims=True)
                v = kvbuf[slot, 1, pl.ds(first + part * rows, rows), :]
                out += jnp.dot(p.astype(jnp.bfloat16), v, preferred_element_type=jnp.float32)
            p = jnp.exp2((far - peak) * scale)
            total += jnp.sum(p, axis=1, keepdims=True)
            p = p.astype(jnp.bfloat16)
            far_out = [
                jnp.dot(
                    p[i * BLOCK : (i + 1) * BLOCK],
                    farv[t * per_tile + i],
                    preferred_element_type=jnp.float32,
                )
                for i in range(per_tile)
            ]
            out = (out + jnp.concatenate(far_out, axis=0)) / total
            obuf[f, h, t * tile : (t + 1) * tile, :] = out.astype(jnp.bfloat16)

    for copy in copies(0):
        copy.start()
    for h in range(len(heads)):
        if h + 1 < len(heads):
            for copy in copies(h + 1):
                copy.start()
        for copy in copies(h):
            copy.wait()
        lax.fori_loop(0, group, lambda f, c, h=h: (one_frame(f, h), c)[1], 0)
    made = []
    for j in range(group):
        made.append(pltpu.make_async_copy(obuf.at[lane ^ j], outs[j], out_sem.at[j]))
    for copy in made:
        copy.start()
    for copy in made:
        copy.wait()


def attend(plan, room, place, pos, heads, wait):
    nfar, count = len(plan.slots), len(heads)
    any_spec = pl.BlockSpec(memory_space=pl.ANY)
    smem = pl.BlockSpec(memory_space=pltpu.SMEM)
    args = [y for q, _, kv, _, recv in heads for y in (*q, *kv, *recv)]
    items = [(at_q, at_k) for _, at_q, _, at_k, _ in heads]
    shape = jax.ShapeDtypeStruct((count, plan.rows, HEAD_DIM), jnp.bfloat16)
    return pl.pallas_call(
        functools.partial(attend_body, plan, room, items, len(wait)),
        in_specs=[smem, smem] + [any_spec] * (len(args) + len(wait)),
        out_specs=[any_spec] * plan.group,
        out_shape=[shape] * plan.group,
        scratch_shapes=[
            pltpu.VMEM((2, plan.group, plan.rows, HEAD_DIM), jnp.bfloat16),
            pltpu.VMEM((2, 2, plan.total(room) * BLOCK, HEAD_DIM), jnp.bfloat16),
            pltpu.VMEM((plan.group, count, plan.rows, HEAD_DIM), jnp.bfloat16),
            pltpu.VMEM((plan.blocks, nfar * BLOCK, HEAD_DIM), jnp.bfloat16),
            pltpu.VMEM((plan.blocks, nfar * BLOCK, HEAD_DIM), jnp.bfloat16),
            pltpu.SemaphoreType.DMA((2, 2 * plan.group + 2 + plan.planes)),
            pltpu.SemaphoreType.DMA((plan.group,)),
        ],
        name="attend",
        **params(),
    )(place, pos, *args, *wait)


def merge_body(plan, first, place_ref, *refs):
    xs, (out, sem) = refs[: plan.group], refs[-2:]
    copies = []
    for j, x in enumerate(xs):
        for h in range(x.shape[0]):
            start = ((place_ref[1] ^ j) * plan.heads + first + h) * HEAD_DIM
            dst = out.at[:, pl.ds(pl.multiple_of(start, HEAD_DIM), HEAD_DIM)]
            copies.append(pltpu.make_async_copy(x.at[h], dst, sem.at[len(copies)]))
    for copy in copies:
        copy.start()
    for copy in copies:
        copy.wait()


def merge(plan, place, xs, first, out):
    width = plan.group * plan.heads * HEAD_DIM
    any_spec = pl.BlockSpec(memory_space=pl.ANY)
    vmem = pl.BlockSpec(memory_space=pltpu.VMEM)
    return pl.pallas_call(
        functools.partial(merge_body, plan, first),
        in_specs=[pl.BlockSpec(memory_space=pltpu.SMEM)]
        + [vmem] * plan.group
        + [any_spec] * len(out),
        out_specs=any_spec,
        out_shape=jax.ShapeDtypeStruct((plan.rows, width), jnp.bfloat16),
        input_output_aliases={1 + plan.group: 0} if out else {},
        scratch_shapes=[pltpu.SemaphoreType.DMA((plan.group * xs[0].shape[0],))],
        name="merge",
        **params(),
    )(place, *xs, *out)


def far_plan(plan, plane, far_frames, far_pick):
    group, blocks, frames, planes = plan.group, plan.blocks, plan.frames, plan.planes
    own = group * blocks
    lists = jnp.concatenate([far_frames[:, s : s + 1] for s in plan.slots], axis=1)
    every = jnp.arange(frames, dtype=jnp.int32)
    used = jnp.any(lists.reshape(frames, -1)[:, :, None] == every, axis=1)
    away = every[None, :] - (every // group * group)[:, None]
    used = used & ((away < -1) | (away > group))
    picked = far_pick[:, :, None] == jnp.arange(blocks, dtype=jnp.int32)
    needed = jnp.any((used[:, :, None] & picked).reshape(planes, group, frames, blocks), axis=1)
    needed = needed.reshape(planes * planes, own)
    before = (jnp.arange(own)[:, None] < jnp.arange(own)[None, :]).astype(jnp.float32)
    slot = jnp.dot(needed.astype(jnp.float32), before, precision=lax.Precision.HIGHEST)
    slot = jnp.where(needed, slot.astype(jnp.int32), -1).reshape(planes, planes, own)
    most = jnp.max(slot) + 1
    sent = lax.dynamic_slice_in_dim(slot, plane, 1, 1).reshape(-1)

    mine = lax.dynamic_slice_in_dim(lists, plane * own, own, 0)
    g = jnp.maximum(mine, 0)
    rows = lax.dynamic_slice_in_dim(far_pick, plane * group, group, 0)
    rows = jnp.repeat(rows, blocks, axis=0)
    pick = jnp.sum(jnp.where(g[:, :, None] == every, rows[:, None, :], 0), axis=2)
    come = lax.dynamic_slice_in_dim(slot, plane, 1, 0).reshape(-1)
    hit = (g * blocks + pick)[:, :, None] == jnp.arange(frames * blocks, dtype=jnp.int32)
    come = jnp.sum(jnp.where(hit, come, 0), axis=2)
    away = g - plane * group
    near = jnp.where((away >= -1) & (away <= group), plan.near0 + away * blocks + pick, -2)
    near = jnp.where(mine >= 0, near, -1)
    return most, sent, g // group, come, near


def local(query, key, value, q_gain, k_gain, far_frames, far_pick):
    rows, width = query.shape
    full_width = width * lax.axis_size("head")
    plan = Plan(lax.axis_size("tm"), rows, width // HEAD_DIM)
    frame = lax.axis_index("tm").astype(jnp.int32)
    plane = frame // plan.group
    place = jnp.stack([plane, frame % plan.group])

    def share(xs):
        return [xs[0]] + [lax.ppermute(xs[j], "tm", plan.swap(j)) for j in range(1, plan.group)]

    sums = jnp.stack([jnp.sum(jnp.square(x.astype(jnp.float32)), axis=1) for x in (query, key)])
    q_rs, k_rs = lax.rsqrt(lax.psum(sums, "head") / full_width + EPSILON)[:, :, None]
    q_gain, k_gain = q_gain[None, :], k_gain[None, :]

    def pair(h):
        return [(key, h, k_rs, k_gain), (value, h, None, None)]

    heads = plan.heads
    queries = [(query, h, q_rs, q_gain) for h in range(heads)]
    rounds = [[0]] + [list(range(h, min(h + 2, heads))) for h in range(1, heads, 2)]
    opening = share(select(plan, place, pair(0), []))
    most, slots, source, come, near = far_plan(plan, plane, far_frames, far_pick)

    def with_room(room, opening):
        far = plan.far0 + source * room + come
        pos = jnp.where(near == -2, far, near).reshape(-1)
        packs, where = [], []
        x = opening
        for index, chosen in enumerate(rounds):
            if index:
                items = [item for h in chosen for item in pair(h)]
                x = share(select(plan, place, items, packs[rounds[index - 1][0]][1:2]))
            for n in range(len(chosen)):
                packs.append(pack(plan, room, place, slots, x, n))
                where.append((x, 2 * n))
        q = share(select(plan, place, queries, packs[heads // 2][1:2]))
        halos = [
            (lax.ppermute(to_next, "tm", plan.halo(1)), lax.ppermute(to_prev, "tm", plan.halo(-1)))
            for _, to_next, to_prev in packs
        ]

        def send(h, after):
            x = hold(packs[h][0], after) if after else packs[h][0]
            x = lax.all_to_all(x, "tm", 0, 0, axis_index_groups=plan.lines(), tiled=True)
            return (x, *halos[h])

        def run(chosen, wait):
            args = [(q, h, *where[h], recvs[h]) for h in chosen]
            return list(attend(plan, room, place, pos, args, wait))

        recvs, out = [], []
        for h in range(heads - 1):
            after = list(halos[h - 1]) if h else []
            recvs.append(send(h, after + (q if h > 1 and h + 2 == heads else [])))
        early = min(2, heads - 1)
        first = run(range(early), []) if early else []
        after = [y for halo in halos[max(heads - 2, 0) :] for y in halo]
        recvs.append(send(heads - 1, after + first))
        if early:
            out = [merge(plan, place, share(first), 0, out)]
        for h in range(early, heads - 1, 2):
            chosen = range(h, min(h + 2, heads - 1))
            out = [merge(plan, place, share(run(chosen, [])), h, out)]
        return merge(plan, place, share(run([heads - 1], out)), heads - 1, out)

    forms = [functools.partial(with_room, room) for room in plan.rooms]
    if len(forms) == 1:
        return forms[0](opening)
    level = sum((most > room).astype(jnp.int32) for room in plan.rooms[:-1])
    return lax.switch(level, forms, opening)


def solution(mesh):
    placed = (P("tm", "head"), P("tm", "head"), P("tm", "head"), P("head"), P("head"), P(), P())
    return jax.shard_map(
        local, mesh=mesh, in_specs=placed, out_specs=P("tm", "head"), check_vma=False
    )
```

```python
import functools
import math

import jax
import jax.numpy as jnp
from jax import lax
from jax.experimental import pallas as pl
from jax.experimental.pallas import tpu as pltpu
from jax.sharding import PartitionSpec as P

HEAD_DIM = 128
BLOCK = 64
NFAR = 12
EPSILON = 1e-06
MASKED = -1e30
VMEM_LIMIT = 56 * 1024 * 1024


class Plan:
    def __init__(self, frames, rows, heads):
        self.frames, self.rows = frames, rows
        self.group = 4 if heads % 4 == 0 and frames % 4 == 0 else 1
        self.planes = frames // self.group
        self.blocks = rows // BLOCK
        self.heads = heads // self.group
        bands = sum(2**band <= frames - 1 for band in range(1, NFAR // 2 + 1))
        self.slots = [*range(bands), *range(NFAR // 2, NFAR // 2 + bands)]
        full = self.group * self.group
        self.rooms = sorted({full * 13 // 16, full * 14 // 16, full}) if self.group > 1 else [full]
        self.near0 = self.blocks
        self.far0 = self.blocks * (self.group + 2)

    def total(self, room):
        return self.far0 + self.planes * room

    def halo(self, step):
        step *= self.group
        return [(i, i + step) for i in range(self.frames) if 0 <= i + step < self.frames]

    def swap(self, j):
        g = self.group
        return [(i, i // g * g + (i % g ^ j)) for i in range(self.frames)]

    def lines(self):
        g = self.group
        return [[p * g + i for p in range(self.planes)] for i in range(g)]


def params():
    return dict(
        compiler_params=pltpu.CompilerParams(vmem_limit_bytes=VMEM_LIMIT),
        cost_estimate=pl.CostEstimate(flops=1, bytes_accessed=1, transcendentals=0),
    )


def select_body(scaled, n_after, group, place_ref, *refs):
    outs = refs[len(refs) - group :]
    refs = list(refs[: len(refs) - group - n_after])
    values = []
    for with_scale in scaled:
        x = refs.pop(0)[...]
        if with_scale:
            rs, gain = refs.pop(0), refs.pop(0)
            x = x.astype(jnp.float32) * rs[...] * gain[...]
        values.append(x.astype(jnp.bfloat16))
    for j, out in enumerate(outs):

        @pl.when(pl.program_id(0) == j)
        def _(out=out):
            for item, x in enumerate(values):
                out[item] = x


def select(plan, place, items, after):
    args, specs = [], []
    for x, head, rs, gain in items:

        def at(j, place, head=head):
            return 0, (place[1] ^ j) * plan.heads + head

        args.append(x)
        specs.append(pl.BlockSpec((plan.rows, HEAD_DIM), at))
        if rs is not None:
            args += [rs, gain]
            specs.append(pl.BlockSpec((plan.rows, 1), lambda j, place: (0, 0)))
            specs.append(pl.BlockSpec((1, HEAD_DIM), at))
    shape = (len(items), plan.rows, HEAD_DIM)
    scaled = [rs is not None for _, _, rs, _ in items]
    return pl.pallas_call(
        functools.partial(select_body, scaled, len(after), plan.group),
        grid_spec=pltpu.PrefetchScalarGridSpec(
            num_scalar_prefetch=1,
            grid=(plan.group,),
            in_specs=specs + [pl.BlockSpec(memory_space=pl.ANY)] * len(after),
            out_specs=[pl.BlockSpec(shape, lambda j, place: (0, 0, 0))] * plan.group,
        ),
        out_shape=[jax.ShapeDtypeStruct(shape, jnp.bfloat16)] * plan.group,
        name="select",
        **params(),
    )(place, *args, *after)


def pack_body(plan, place_ref, slot_ref, *refs):
    group, blocks = plan.group, plan.blocks
    xs = refs[:group]
    far, to_next, to_prev, sem = refs[group:]
    plane, lane = place_ref[0], place_ref[1]
    whole = slot_ref.shape[0] > plan.planes
    stride, from_plane = (plan.planes, plane) if whole else (1, 0)

    def halo(act):
        for j in range(group):
            for at, (g, out) in enumerate(((group - 1, to_next), (0, to_prev))):

                @pl.when((lane ^ j) == g)
                def _(j=j, at=at, out=out):
                    act(pltpu.make_async_copy(xs[j], out, sem.at[plan.planes, at]))

    def for_each(act):
        halo(act)

        def one_plane(dest, carry):
            for j in range(group):
                for b in range(blocks):
                    slot = slot_ref[dest * stride + from_plane, (lane ^ j) * blocks + b]

                    @pl.when(slot >= 0)
                    def _(j=j, b=b, slot=slot):
                        dst = pl.ds(pl.multiple_of(slot * BLOCK, BLOCK), BLOCK)
                        src = xs[j].at[:, b * BLOCK : (b + 1) * BLOCK, :]
                        place = sem.at[dest, j * blocks + b]
                        act(pltpu.make_async_copy(src, far.at[dest, :, dst, :], place))

            return carry

        lax.fori_loop(0, plan.planes, one_plane, 0)

    for_each(lambda copy: copy.start())
    for_each(lambda copy: copy.wait())


def pack(plan, room, place, slots, xs, pair):
    smem = pl.BlockSpec(memory_space=pltpu.SMEM)
    any_spec = pl.BlockSpec(memory_space=pl.ANY)
    frame = jax.ShapeDtypeStruct((2, plan.rows, HEAD_DIM), jnp.bfloat16)
    far = jax.ShapeDtypeStruct((plan.planes, 2, room * BLOCK, HEAD_DIM), jnp.bfloat16)
    return pl.pallas_call(
        functools.partial(pack_body, plan),
        grid=(1,),
        in_specs=[smem, smem]
        + [pl.BlockSpec((2, plan.rows, HEAD_DIM), lambda i: (pair, 0, 0))] * plan.group,
        out_specs=[any_spec] * 3,
        out_shape=[far, frame, frame],
        scratch_shapes=[pltpu.SemaphoreType.DMA((plan.planes + 1, plan.group * plan.blocks))],
        name="pack",
        **params(),
    )(place, slots, *xs)


def hold_body(*refs):
    pass


def hold(x, after):
    any_spec = pl.BlockSpec(memory_space=pl.ANY)
    return pl.pallas_call(
        hold_body,
        in_specs=[any_spec] * (1 + len(after)),
        out_specs=any_spec,
        out_shape=jax.ShapeDtypeStruct(x.shape, x.dtype),
        input_output_aliases={0: 0},
        name="hold",
        **params(),
    )(x, *after)


def attend_body(plan, room, heads, n_wait, *refs):
    place_ref, pos_ref = refs[:2]
    group, rows, nfar = plan.group, plan.rows, len(plan.slots)
    step = 2 * group + 3
    inputs = [refs[2 + h * step : 2 + (h + 1) * step] for h in range(len(heads))]
    refs = refs[2 + len(heads) * step + n_wait :]
    outs, scratch = refs[:group], refs[group:]
    qbuf, kvbuf, obuf, fark, farv, *bufs, sem, out_sem = scratch
    sbufs, mbufs = bufs[:2], bufs[2:]
    plane, lane = place_ref[0], place_ref[1]
    scale = math.log2(math.e) / math.sqrt(HEAD_DIM)
    tile = rows // 2
    per_tile = tile // BLOCK
    lanes = lax.broadcasted_iota(jnp.int32, (1, nfar * BLOCK), 1) // BLOCK
    contract = (((1,), (1,)), ((), ()))

    def copies(h):
        made, slot = [], h % 2
        qs, kvs, recvs = inputs[h][:group], inputs[h][group : 2 * group], inputs[h][2 * group :]
        at_q, at_k = heads[h]

        def add(src, dst):
            made.append(pltpu.make_async_copy(src, dst, sem.at[slot, len(made)]))

        def at(first, count):
            first = first * BLOCK
            if not isinstance(first, int):
                first = pl.multiple_of(first, BLOCK)
            return kvbuf.at[slot, :, pl.ds(first, count * BLOCK), :]

        for j in range(group):
            g = lane ^ j
            add(qs[j].at[at_q], qbuf.at[slot, g])
            add(kvs[j].at[at_k : at_k + 2], at(plan.near0 + g * plan.blocks, plan.blocks))
        far, before, after = recvs
        add(before, at(0, plan.blocks))
        add(after, at(plan.near0 + group * plan.blocks, plan.blocks))
        for p in range(plan.planes):
            add(far.at[p], at(plan.far0 + p * room, room))
        return made

    def score(h, f, t):
        slot = h % 2
        first = pl.multiple_of((plan.near0 + (f - 1) * plan.blocks) * BLOCK, BLOCK)
        q = qbuf[slot, f, t * tile : (t + 1) * tile, :]
        peak = None
        for part in range(3):
            k = kvbuf[slot, 0, pl.ds(first + part * rows, rows), :]
            s = lax.dot_general(q, k, contract, preferred_element_type=jnp.float32)
            sbufs[t][:, part * rows : (part + 1) * rows] = s
            s = functools.reduce(
                jnp.maximum, [s[:, c : c + HEAD_DIM] for c in range(0, rows, HEAD_DIM)]
            )
            ok = there(f, part)
            if ok is not None:
                s = jnp.where(ok, s, MASKED)
            peak = s if peak is None else jnp.maximum(peak, s)
        for i in range(per_tile):
            block = t * per_tile + i
            ok = lanes < 0
            for n in range(nfar):
                at = pos_ref[(f * plan.blocks + block) * nfar + n]
                src = pl.ds(pl.multiple_of(jnp.maximum(at, 0) * BLOCK, BLOCK), BLOCK)
                fark[block, n * BLOCK : (n + 1) * BLOCK, :] = kvbuf[slot, 0, src, :]
                farv[block, n * BLOCK : (n + 1) * BLOCK, :] = kvbuf[slot, 1, src, :]
                ok = ok | ((lanes == n) & (at >= 0))
            some = slice(i * BLOCK, (i + 1) * BLOCK)
            s = lax.dot_general(
                q[some], fark[block], contract, preferred_element_type=jnp.float32
            )
            s = jnp.where(ok, s, MASKED)
            sbufs[t][some, 3 * rows :] = s
            s = functools.reduce(
                jnp.maximum, [s[:, c : c + HEAD_DIM] for c in range(0, nfar * BLOCK, HEAD_DIM)]
            )
            mbufs[t][some, :] = jnp.maximum(peak[some], s)

    def there(f, part):
        frame = plane * group + f
        return (frame > 0, None, frame < plan.frames - 1)[part]

    def weigh(h, f, t):
        slot = h % 2
        first = pl.multiple_of((plan.near0 + (f - 1) * plan.blocks) * BLOCK, BLOCK)
        peak = jnp.max(mbufs[t][...], axis=1, keepdims=True)
        total, out = 0.0, 0.0
        for part in range(3):
            ok = there(f, part)
            less = peak if ok is None else jnp.where(ok, peak, -MASKED)
            p = jnp.exp2((sbufs[t][:, part * rows : (part + 1) * rows] - less) * scale)
            total += jnp.sum(p, axis=1, keepdims=True)
            v = kvbuf[slot, 1, pl.ds(first + part * rows, rows), :]
            out += jnp.dot(p.astype(jnp.bfloat16), v, preferred_element_type=jnp.float32)
        p = jnp.exp2((sbufs[t][:, 3 * rows :] - peak) * scale)
        total += jnp.sum(p, axis=1, keepdims=True)
        p = p.astype(jnp.bfloat16)
        far_out = [
            jnp.dot(
                p[i * BLOCK : (i + 1) * BLOCK],
                farv[t * per_tile + i],
                preferred_element_type=jnp.float32,
            )
            for i in range(per_tile)
        ]
        out = (out + jnp.concatenate(far_out, axis=0)) / total
        obuf[f, h, t * tile : (t + 1) * tile, :] = out.astype(jnp.bfloat16)

    def one_frame(f, h):
        score(h, f, 1)
        weigh(h, f, 0)
        score(h, jnp.minimum(f + 1, group - 1), 0)
        weigh(h, f, 1)

    for copy in copies(0):
        copy.start()
    for h in range(len(heads)):
        if h + 1 < len(heads):
            for copy in copies(h + 1):
                copy.start()
        for copy in copies(h):
            copy.wait()
        score(h, 0, 0)
        lax.fori_loop(0, group, lambda f, c, h=h: (one_frame(f, h), c)[1], 0)
    made = []
    for j in range(group):
        made.append(pltpu.make_async_copy(obuf.at[lane ^ j], outs[j], out_sem.at[j]))
    for copy in made:
        copy.start()
    for copy in made:
        copy.wait()


def attend(plan, room, place, pos, heads, wait):
    nfar, count = len(plan.slots), len(heads)
    any_spec = pl.BlockSpec(memory_space=pl.ANY)
    smem = pl.BlockSpec(memory_space=pltpu.SMEM)
    args = [y for q, _, kv, _, recv in heads for y in (*q, *kv, *recv)]
    items = [(at_q, at_k) for _, at_q, _, at_k, _ in heads]
    shape = jax.ShapeDtypeStruct((count, plan.rows, HEAD_DIM), jnp.bfloat16)
    return pl.pallas_call(
        functools.partial(attend_body, plan, room, items, len(wait)),
        in_specs=[smem, smem] + [any_spec] * (len(args) + len(wait)),
        out_specs=[any_spec] * plan.group,
        out_shape=[shape] * plan.group,
        scratch_shapes=[
            pltpu.VMEM((2, plan.group, plan.rows, HEAD_DIM), jnp.bfloat16),
            pltpu.VMEM((2, 2, plan.total(room) * BLOCK, HEAD_DIM), jnp.bfloat16),
            pltpu.VMEM((plan.group, count, plan.rows, HEAD_DIM), jnp.bfloat16),
            pltpu.VMEM((plan.blocks, nfar * BLOCK, HEAD_DIM), jnp.bfloat16),
            pltpu.VMEM((plan.blocks, nfar * BLOCK, HEAD_DIM), jnp.bfloat16),
            pltpu.VMEM((plan.rows // 2, 3 * plan.rows + nfar * BLOCK), jnp.float32),
            pltpu.VMEM((plan.rows // 2, 3 * plan.rows + nfar * BLOCK), jnp.float32),
            pltpu.VMEM((plan.rows // 2, HEAD_DIM), jnp.float32),
            pltpu.VMEM((plan.rows // 2, HEAD_DIM), jnp.float32),
            pltpu.SemaphoreType.DMA((2, 2 * plan.group + 2 + plan.planes)),
            pltpu.SemaphoreType.DMA((plan.group,)),
        ],
        name="attend",
        **params(),
    )(place, pos, *args, *wait)


def merge_body(plan, first, place_ref, *refs):
    xs, (out, sem) = refs[: plan.group], refs[-2:]
    copies = []
    for j, x in enumerate(xs):
        for h in range(x.shape[0]):
            start = ((place_ref[1] ^ j) * plan.heads + first + h) * HEAD_DIM
            dst = out.at[:, pl.ds(pl.multiple_of(start, HEAD_DIM), HEAD_DIM)]
            copies.append(pltpu.make_async_copy(x.at[h], dst, sem.at[len(copies)]))
    for copy in copies:
        copy.start()
    for copy in copies:
        copy.wait()


def merge(plan, place, xs, first, out):
    width = plan.group * plan.heads * HEAD_DIM
    any_spec = pl.BlockSpec(memory_space=pl.ANY)
    vmem = pl.BlockSpec(memory_space=pltpu.VMEM)
    return pl.pallas_call(
        functools.partial(merge_body, plan, first),
        in_specs=[pl.BlockSpec(memory_space=pltpu.SMEM)]
        + [vmem] * plan.group
        + [any_spec] * len(out),
        out_specs=any_spec,
        out_shape=jax.ShapeDtypeStruct((plan.rows, width), jnp.bfloat16),
        input_output_aliases={1 + plan.group: 0} if out else {},
        scratch_shapes=[pltpu.SemaphoreType.DMA((plan.group * xs[0].shape[0],))],
        name="merge",
        **params(),
    )(place, *xs, *out)


def far_plan(plan, plane, far_frames, far_pick):
    group, blocks, frames, planes = plan.group, plan.blocks, plan.frames, plan.planes
    own = group * blocks
    lists = jnp.concatenate([far_frames[:, s : s + 1] for s in plan.slots], axis=1)
    every = jnp.arange(frames, dtype=jnp.int32)
    used = jnp.any(lists.reshape(frames, -1)[:, :, None] == every, axis=1)
    away = every[None, :] - (every // group * group)[:, None]
    used = used & ((away < -1) | (away > group))
    picked = far_pick[:, :, None] == jnp.arange(blocks, dtype=jnp.int32)
    needed = jnp.any((used[:, :, None] & picked).reshape(planes, group, frames, blocks), axis=1)
    needed = needed.reshape(planes * planes, own)
    before = (jnp.arange(own)[:, None] < jnp.arange(own)[None, :]).astype(jnp.float32)
    slot = jnp.dot(needed.astype(jnp.float32), before, precision=lax.Precision.HIGHEST)
    slot = jnp.where(needed, slot.astype(jnp.int32), -1)
    most = jnp.max(slot) + 1

    mine = lax.dynamic_slice_in_dim(lists, plane * own, own, 0)
    g = jnp.maximum(mine, 0)
    rows = lax.dynamic_slice_in_dim(far_pick, plane * group, group, 0)
    rows = jnp.repeat(rows, blocks, axis=0)
    pick = jnp.sum(jnp.where(g[:, :, None] == every, rows[:, None, :], 0), axis=2)
    come = lax.dynamic_slice_in_dim(slot, plane * planes, planes, 0).reshape(-1)
    hit = (g * blocks + pick)[:, :, None] == jnp.arange(frames * blocks, dtype=jnp.int32)
    come = jnp.sum(jnp.where(hit, come, 0), axis=2)
    away = g - plane * group
    near = jnp.where((away >= -1) & (away <= group), plan.near0 + away * blocks + pick, -2)
    near = jnp.where(mine >= 0, near, -1)
    if planes > 8:
        slot = slot.reshape(planes, planes, own)
        slot = lax.dynamic_slice_in_dim(slot, plane, 1, 1).reshape(planes, own)
    return most, slot, g // group, come, near


def local(query, key, value, q_gain, k_gain, far_frames, far_pick):
    rows, width = query.shape
    full_width = width * lax.axis_size("head")
    plan = Plan(lax.axis_size("tm"), rows, width // HEAD_DIM)
    frame = lax.axis_index("tm").astype(jnp.int32)
    plane = frame // plan.group
    place = jnp.stack([plane, frame % plan.group])

    def share(xs):
        return [xs[0]] + [lax.ppermute(xs[j], "tm", plan.swap(j)) for j in range(1, plan.group)]

    sums = jnp.stack([jnp.sum(jnp.square(x.astype(jnp.float32)), axis=1) for x in (query, key)])
    q_rs, k_rs = lax.rsqrt(lax.psum(sums, "head") / full_width + EPSILON)[:, :, None]
    q_gain, k_gain = q_gain[None, :], k_gain[None, :]

    def pair(h):
        return [(key, h, k_rs, k_gain), (value, h, None, None)]

    heads = plan.heads
    queries = [(query, h, q_rs, q_gain) for h in range(heads)]
    rounds = [[0]] + [list(range(h, min(h + 2, heads))) for h in range(1, heads, 2)]
    opening = share(select(plan, place, pair(0), []))
    most, slots, source, come, near = far_plan(plan, plane, far_frames, far_pick)

    def with_room(room, opening):
        far = plan.far0 + source * room + come
        pos = jnp.where(near == -2, far, near).reshape(-1)
        packs, where = [], []
        x = opening
        for index, chosen in enumerate(rounds):
            if index:
                items = [item for h in chosen for item in pair(h)]
                x = share(select(plan, place, items, packs[rounds[index - 1][0]][1:2]))
            for n in range(len(chosen)):
                packs.append(pack(plan, room, place, slots, x, n))
                where.append((x, 2 * n))
        q = share(select(plan, place, queries, packs[heads // 2][1:2]))
        halos = [
            (lax.ppermute(to_next, "tm", plan.halo(1)), lax.ppermute(to_prev, "tm", plan.halo(-1)))
            for _, to_next, to_prev in packs
        ]

        def send(h, after):
            x = hold(packs[h][0], after) if after else packs[h][0]
            x = lax.all_to_all(x, "tm", 0, 0, axis_index_groups=plan.lines(), tiled=True)
            return (x, *halos[h])

        def run(chosen, wait):
            args = [(q, h, *where[h], recvs[h]) for h in chosen]
            return list(attend(plan, room, place, pos, args, wait))

        recvs, out = [], []
        for h in range(heads - 1):
            after = list(halos[h - 1]) if h else []
            if h > 1:
                after += q if h + 2 == heads else where[h + 1][0]
            recvs.append(send(h, after))
        early = min(2, heads - 1)
        first = run(range(early), []) if early else []
        after = [y for halo in halos[max(heads - 2, 0) :] for y in halo]
        recvs.append(send(heads - 1, after + first))
        if early:
            out = [merge(plan, place, share(first), 0, out)]
        for h in range(early, heads - 1, 2):
            chosen = range(h, min(h + 2, heads - 1))
            out = [merge(plan, place, share(run(chosen, [])), h, out)]
        return merge(plan, place, share(run([heads - 1], out)), heads - 1, out)

    forms = [functools.partial(with_room, room) for room in plan.rooms]
    if len(forms) == 1:
        return forms[0](opening)
    level = sum((most > room).astype(jnp.int32) for room in plan.rooms[:-1])
    return lax.switch(level, forms, opening)


def solution(mesh):
    placed = (P("tm", "head"), P("tm", "head"), P("tm", "head"), P("head"), P("head"), P(), P())
    return jax.shard_map(
        local, mesh=mesh, in_specs=placed, out_specs=P("tm", "head"), check_vma=False
    )
```

```python
import functools
import math

import jax
import jax.numpy as jnp
from jax import lax
from jax.experimental import pallas as pl
from jax.experimental.pallas import tpu as pltpu
from jax.sharding import PartitionSpec as P

HEAD_DIM = 128
BLOCK = 64
NFAR = 12
EPSILON = 1e-06
MASKED = -1e30
VMEM_LIMIT = 56 * 1024 * 1024


class Plan:
    def __init__(self, frames, rows, heads):
        self.frames, self.rows = frames, rows
        self.group = 4 if heads % 4 == 0 and frames % 4 == 0 else 1
        self.planes = frames // self.group
        self.blocks = rows // BLOCK
        self.heads = heads // self.group
        bands = sum(2**band <= frames - 1 for band in range(1, NFAR // 2 + 1))
        self.slots = [*range(bands), *range(NFAR // 2, NFAR // 2 + bands)]
        full = self.group * self.group
        self.rooms = sorted({full * 13 // 16, full * 14 // 16, full}) if self.group > 1 else [full]
        self.near0 = self.blocks
        self.far0 = self.blocks * (self.group + 2)

    def total(self, room):
        return self.far0 + self.planes * room

    def halo(self, step):
        step *= self.group
        return [(i, i + step) for i in range(self.frames) if 0 <= i + step < self.frames]

    def swap(self, j):
        g = self.group
        return [(i, i // g * g + (i % g ^ j)) for i in range(self.frames)]

    def lines(self):
        g = self.group
        return [[p * g + i for p in range(self.planes)] for i in range(g)]


def params():
    return dict(
        compiler_params=pltpu.CompilerParams(vmem_limit_bytes=VMEM_LIMIT),
        cost_estimate=pl.CostEstimate(flops=1, bytes_accessed=1, transcendentals=0),
    )


def select_body(scaled, n_after, group, place_ref, *refs):
    outs = refs[len(refs) - group :]
    refs = list(refs[: len(refs) - group - n_after])
    values = []
    for with_scale in scaled:
        x = refs.pop(0)[...]
        if with_scale:
            rs, gain = refs.pop(0), refs.pop(0)
            x = x.astype(jnp.float32) * rs[...] * gain[...]
        values.append(x.astype(jnp.bfloat16))
    for j, out in enumerate(outs):

        @pl.when(pl.program_id(0) == j)
        def _(out=out):
            for item, x in enumerate(values):
                out[item] = x


def select(plan, place, items, after):
    args, specs = [], []
    for x, head, rs, gain in items:

        def at(j, place, head=head):
            return 0, (place[1] ^ j) * plan.heads + head

        args.append(x)
        specs.append(pl.BlockSpec((plan.rows, HEAD_DIM), at))
        if rs is not None:
            args += [rs, gain]
            specs.append(pl.BlockSpec((plan.rows, 1), lambda j, place: (0, 0)))
            specs.append(pl.BlockSpec((1, HEAD_DIM), at))
    shape = (len(items), plan.rows, HEAD_DIM)
    scaled = [rs is not None for _, _, rs, _ in items]
    return pl.pallas_call(
        functools.partial(select_body, scaled, len(after), plan.group),
        grid_spec=pltpu.PrefetchScalarGridSpec(
            num_scalar_prefetch=1,
            grid=(plan.group,),
            in_specs=specs + [pl.BlockSpec(memory_space=pl.ANY)] * len(after),
            out_specs=[pl.BlockSpec(shape, lambda j, place: (0, 0, 0))] * plan.group,
        ),
        out_shape=[jax.ShapeDtypeStruct(shape, jnp.bfloat16)] * plan.group,
        name="select",
        **params(),
    )(place, *args, *after)


def pack_body(plan, place_ref, slot_ref, *refs):
    group, blocks = plan.group, plan.blocks
    xs = refs[:group]
    far, to_next, to_prev, sem = refs[group:]
    plane, lane = place_ref[0], place_ref[1]
    whole = slot_ref.shape[0] > plan.planes
    stride, from_plane = (plan.planes, plane) if whole else (1, 0)

    def halo(act):
        for j in range(group):
            for at, (g, out) in enumerate(((group - 1, to_next), (0, to_prev))):

                @pl.when((lane ^ j) == g)
                def _(j=j, at=at, out=out):
                    act(pltpu.make_async_copy(xs[j], out, sem.at[plan.planes, at]))

    def for_each(act):
        halo(act)

        def one_plane(dest, carry):
            for j in range(group):
                for b in range(blocks):
                    slot = slot_ref[dest * stride + from_plane, (lane ^ j) * blocks + b]

                    @pl.when(slot >= 0)
                    def _(j=j, b=b, slot=slot):
                        dst = pl.ds(pl.multiple_of(slot * BLOCK, BLOCK), BLOCK)
                        src = xs[j].at[:, b * BLOCK : (b + 1) * BLOCK, :]
                        place = sem.at[dest, j * blocks + b]
                        act(pltpu.make_async_copy(src, far.at[dest, :, dst, :], place))

            return carry

        lax.fori_loop(0, plan.planes, one_plane, 0)

    for_each(lambda copy: copy.start())
    for_each(lambda copy: copy.wait())


def pack(plan, room, place, slots, xs, first, count):
    smem = pl.BlockSpec(memory_space=pltpu.SMEM)
    any_spec = pl.BlockSpec(memory_space=pl.ANY)
    frame = jax.ShapeDtypeStruct((count, plan.rows, HEAD_DIM), jnp.bfloat16)
    far = jax.ShapeDtypeStruct((plan.planes, count, room * BLOCK, HEAD_DIM), jnp.bfloat16)
    return pl.pallas_call(
        functools.partial(pack_body, plan),
        grid=(1,),
        in_specs=[smem, smem]
        + [pl.BlockSpec((count, plan.rows, HEAD_DIM), lambda i: (first // count, 0, 0))] * plan.group,
        out_specs=[any_spec] * 3,
        out_shape=[far, frame, frame],
        scratch_shapes=[pltpu.SemaphoreType.DMA((plan.planes + 1, plan.group * plan.blocks))],
        name="pack",
        **params(),
    )(place, slots, *xs)


def hold_body(*refs):
    pass


def hold(x, after):
    any_spec = pl.BlockSpec(memory_space=pl.ANY)
    return pl.pallas_call(
        hold_body,
        in_specs=[any_spec] * (1 + len(after)),
        out_specs=any_spec,
        out_shape=jax.ShapeDtypeStruct(x.shape, x.dtype),
        input_output_aliases={0: 0},
        name="hold",
        **params(),
    )(x, *after)


def attend_body(plan, room, heads, n_wait, *refs):
    place_ref, pos_ref = refs[:2]
    group, rows, nfar = plan.group, plan.rows, len(plan.slots)
    step = 3 * group + 6
    inputs = [refs[2 + h * step : 2 + (h + 1) * step] for h in range(len(heads))]
    refs = refs[2 + len(heads) * step + n_wait :]
    outs, scratch = refs[:group], refs[group:]
    qbuf, kvbuf, obuf, fark, farv, *bufs, sem, out_sem = scratch
    sbufs, mbufs = bufs[:2], bufs[2:]
    plane, lane = place_ref[0], place_ref[1]
    scale = math.log2(math.e) / math.sqrt(HEAD_DIM)
    tile = rows // 2
    per_tile = tile // BLOCK
    lanes = lax.broadcasted_iota(jnp.int32, (1, nfar * BLOCK), 1) // BLOCK
    contract = (((1,), (1,)), ((), ()))

    def copies(h):
        made, slot = [], h % 2
        qs, rest = inputs[h][:group], inputs[h][group:]
        at_q, *at_kv = heads[h]

        def add(src, dst):
            made.append(pltpu.make_async_copy(src, dst, sem.at[slot, len(made)]))

        for j in range(group):
            add(qs[j].at[at_q], qbuf.at[slot, lane ^ j])
        for which, (item, of_set) in enumerate(at_kv):
            xs, (far, before, after) = rest[:group], rest[group : group + 3]
            rest = rest[group + 3 :]

            def at(first, count, which=which):
                first = first * BLOCK
                if not isinstance(first, int):
                    first = pl.multiple_of(first, BLOCK)
                return kvbuf.at[slot, which, pl.ds(first, count * BLOCK), :]

            for j in range(group):
                add(xs[j].at[item], at(plan.near0 + (lane ^ j) * plan.blocks, plan.blocks))
            add(before.at[of_set], at(0, plan.blocks))
            add(after.at[of_set], at(plan.near0 + group * plan.blocks, plan.blocks))
            for p in range(plan.planes):
                add(far.at[p, of_set], at(plan.far0 + p * room, room))
        return made

    def score(h, f, t):
        slot = h % 2
        first = pl.multiple_of((plan.near0 + (f - 1) * plan.blocks) * BLOCK, BLOCK)
        q = qbuf[slot, f, t * tile : (t + 1) * tile, :]
        peak = None
        for part in range(3):
            k = kvbuf[slot, 0, pl.ds(first + part * rows, rows), :]
            s = lax.dot_general(q, k, contract, preferred_element_type=jnp.float32)
            sbufs[t][:, part * rows : (part + 1) * rows] = s
            s = functools.reduce(
                jnp.maximum, [s[:, c : c + HEAD_DIM] for c in range(0, rows, HEAD_DIM)]
            )
            ok = there(f, part)
            if ok is not None:
                s = jnp.where(ok, s, MASKED)
            peak = s if peak is None else jnp.maximum(peak, s)
        for i in range(per_tile):
            block = t * per_tile + i
            ok = lanes < 0
            for n in range(nfar):
                at = pos_ref[(f * plan.blocks + block) * nfar + n]
                src = pl.ds(pl.multiple_of(jnp.maximum(at, 0) * BLOCK, BLOCK), BLOCK)
                fark[block, n * BLOCK : (n + 1) * BLOCK, :] = kvbuf[slot, 0, src, :]
                farv[block, n * BLOCK : (n + 1) * BLOCK, :] = kvbuf[slot, 1, src, :]
                ok = ok | ((lanes == n) & (at >= 0))
            some = slice(i * BLOCK, (i + 1) * BLOCK)
            s = lax.dot_general(
                q[some], fark[block], contract, preferred_element_type=jnp.float32
            )
            s = jnp.where(ok, s, MASKED)
            sbufs[t][some, 3 * rows :] = s
            s = functools.reduce(
                jnp.maximum, [s[:, c : c + HEAD_DIM] for c in range(0, nfar * BLOCK, HEAD_DIM)]
            )
            mbufs[t][some, :] = jnp.maximum(peak[some], s)

    def there(f, part):
        frame = plane * group + f
        return (frame > 0, None, frame < plan.frames - 1)[part]

    def weigh(h, f, t):
        slot = h % 2
        first = pl.multiple_of((plan.near0 + (f - 1) * plan.blocks) * BLOCK, BLOCK)
        peak = jnp.max(mbufs[t][...], axis=1, keepdims=True)
        total, out = 0.0, 0.0
        for part in range(3):
            ok = there(f, part)
            less = peak if ok is None else jnp.where(ok, peak, -MASKED)
            p = jnp.exp2((sbufs[t][:, part * rows : (part + 1) * rows] - less) * scale)
            total += jnp.sum(p, axis=1, keepdims=True)
            v = kvbuf[slot, 1, pl.ds(first + part * rows, rows), :]
            out += jnp.dot(p.astype(jnp.bfloat16), v, preferred_element_type=jnp.float32)
        p = jnp.exp2((sbufs[t][:, 3 * rows :] - peak) * scale)
        total += jnp.sum(p, axis=1, keepdims=True)
        p = p.astype(jnp.bfloat16)
        far_out = [
            jnp.dot(
                p[i * BLOCK : (i + 1) * BLOCK],
                farv[t * per_tile + i],
                preferred_element_type=jnp.float32,
            )
            for i in range(per_tile)
        ]
        out = (out + jnp.concatenate(far_out, axis=0)) / total
        obuf[f, h, t * tile : (t + 1) * tile, :] = out.astype(jnp.bfloat16)

    def one_frame(f, h):
        score(h, f, 1)
        weigh(h, f, 0)
        score(h, jnp.minimum(f + 1, group - 1), 0)
        weigh(h, f, 1)

    for copy in copies(0):
        copy.start()
    for h in range(len(heads)):
        if h + 1 < len(heads):
            for copy in copies(h + 1):
                copy.start()
        for copy in copies(h):
            copy.wait()
        score(h, 0, 0)
        lax.fori_loop(0, group, lambda f, c, h=h: (one_frame(f, h), c)[1], 0)
    made = []
    for j in range(group):
        made.append(pltpu.make_async_copy(obuf.at[lane ^ j], outs[j], out_sem.at[j]))
    for copy in made:
        copy.start()
    for copy in made:
        copy.wait()


def attend(plan, room, place, pos, heads, wait):
    nfar, count = len(plan.slots), len(heads)
    any_spec = pl.BlockSpec(memory_space=pl.ANY)
    smem = pl.BlockSpec(memory_space=pltpu.SMEM)
    args, items = [], []
    for q, at_q, *kv in heads:
        args += q
        items.append((at_q, *((item, of_set) for _, item, _, of_set in kv)))
        for xs, _, recv, _ in kv:
            args += [*xs, *recv]
    shape = jax.ShapeDtypeStruct((count, plan.rows, HEAD_DIM), jnp.bfloat16)
    return pl.pallas_call(
        functools.partial(attend_body, plan, room, items, len(wait)),
        in_specs=[smem, smem] + [any_spec] * (len(args) + len(wait)),
        out_specs=[any_spec] * plan.group,
        out_shape=[shape] * plan.group,
        scratch_shapes=[
            pltpu.VMEM((2, plan.group, plan.rows, HEAD_DIM), jnp.bfloat16),
            pltpu.VMEM((2, 2, plan.total(room) * BLOCK, HEAD_DIM), jnp.bfloat16),
            pltpu.VMEM((plan.group, count, plan.rows, HEAD_DIM), jnp.bfloat16),
            pltpu.VMEM((plan.blocks, nfar * BLOCK, HEAD_DIM), jnp.bfloat16),
            pltpu.VMEM((plan.blocks, nfar * BLOCK, HEAD_DIM), jnp.bfloat16),
            pltpu.VMEM((plan.rows // 2, 3 * plan.rows + nfar * BLOCK), jnp.float32),
            pltpu.VMEM((plan.rows // 2, 3 * plan.rows + nfar * BLOCK), jnp.float32),
            pltpu.VMEM((plan.rows // 2, HEAD_DIM), jnp.float32),
            pltpu.VMEM((plan.rows // 2, HEAD_DIM), jnp.float32),
            pltpu.SemaphoreType.DMA((2, 3 * plan.group + 2 * (2 + plan.planes))),
            pltpu.SemaphoreType.DMA((plan.group,)),
        ],
        name="attend",
        **params(),
    )(place, pos, *args, *wait)


def merge_body(plan, first, place_ref, *refs):
    xs, (out, sem) = refs[: plan.group], refs[-2:]
    copies = []
    for j, x in enumerate(xs):
        for h in range(x.shape[0]):
            start = ((place_ref[1] ^ j) * plan.heads + first + h) * HEAD_DIM
            dst = out.at[:, pl.ds(pl.multiple_of(start, HEAD_DIM), HEAD_DIM)]
            copies.append(pltpu.make_async_copy(x.at[h], dst, sem.at[len(copies)]))
    for copy in copies:
        copy.start()
    for copy in copies:
        copy.wait()


def merge(plan, place, xs, first, out):
    width = plan.group * plan.heads * HEAD_DIM
    any_spec = pl.BlockSpec(memory_space=pl.ANY)
    vmem = pl.BlockSpec(memory_space=pltpu.VMEM)
    return pl.pallas_call(
        functools.partial(merge_body, plan, first),
        in_specs=[pl.BlockSpec(memory_space=pltpu.SMEM)]
        + [vmem] * plan.group
        + [any_spec] * len(out),
        out_specs=any_spec,
        out_shape=jax.ShapeDtypeStruct((plan.rows, width), jnp.bfloat16),
        input_output_aliases={1 + plan.group: 0} if out else {},
        scratch_shapes=[pltpu.SemaphoreType.DMA((plan.group * xs[0].shape[0],))],
        name="merge",
        **params(),
    )(place, *xs, *out)


def far_plan(plan, plane, far_frames, far_pick):
    group, blocks, frames, planes = plan.group, plan.blocks, plan.frames, plan.planes
    own = group * blocks
    lists = jnp.concatenate([far_frames[:, s : s + 1] for s in plan.slots], axis=1)
    every = jnp.arange(frames, dtype=jnp.int32)
    used = jnp.any(lists.reshape(frames, -1)[:, :, None] == every, axis=1)
    away = every[None, :] - (every // group * group)[:, None]
    used = used & ((away < -1) | (away > group))
    picked = far_pick[:, :, None] == jnp.arange(blocks, dtype=jnp.int32)
    needed = jnp.any((used[:, :, None] & picked).reshape(planes, group, frames, blocks), axis=1)
    needed = needed.reshape(planes * planes, own)
    before = (jnp.arange(own)[:, None] < jnp.arange(own)[None, :]).astype(jnp.float32)
    slot = jnp.dot(needed.astype(jnp.float32), before, precision=lax.Precision.HIGHEST)
    slot = jnp.where(needed, slot.astype(jnp.int32), -1)
    most = jnp.max(slot) + 1

    mine = lax.dynamic_slice_in_dim(lists, plane * own, own, 0)
    g = jnp.maximum(mine, 0)
    rows = lax.dynamic_slice_in_dim(far_pick, plane * group, group, 0)
    rows = jnp.repeat(rows, blocks, axis=0)
    pick = jnp.sum(jnp.where(g[:, :, None] == every, rows[:, None, :], 0), axis=2)
    come = lax.dynamic_slice_in_dim(slot, plane * planes, planes, 0).reshape(-1)
    hit = (g * blocks + pick)[:, :, None] == jnp.arange(frames * blocks, dtype=jnp.int32)
    come = jnp.sum(jnp.where(hit, come, 0), axis=2)
    away = g - plane * group
    near = jnp.where((away >= -1) & (away <= group), plan.near0 + away * blocks + pick, -2)
    near = jnp.where(mine >= 0, near, -1)
    if planes > 8:
        slot = slot.reshape(planes, planes, own)
        slot = lax.dynamic_slice_in_dim(slot, plane, 1, 1).reshape(planes, own)
    return most, slot, g // group, come, near


def local(query, key, value, q_gain, k_gain, far_frames, far_pick):
    rows, width = query.shape
    full_width = width * lax.axis_size("head")
    plan = Plan(lax.axis_size("tm"), rows, width // HEAD_DIM)
    frame = lax.axis_index("tm").astype(jnp.int32)
    plane = frame // plan.group
    place = jnp.stack([plane, frame % plan.group])

    def share(xs):
        return [xs[0]] + [lax.ppermute(xs[j], "tm", plan.swap(j)) for j in range(1, plan.group)]

    sums = jnp.stack([jnp.sum(jnp.square(x.astype(jnp.float32)), axis=1) for x in (query, key)])
    q_rs, k_rs = lax.rsqrt(lax.psum(sums, "head") / full_width + EPSILON)[:, :, None]
    q_gain, k_gain = q_gain[None, :], k_gain[None, :]

    def item(name):
        kind, h = name
        if kind == "k":
            return key, h, k_rs, k_gain
        return (value, h, None, None) if kind == "v" else (query, h, q_rs, q_gain)

    heads = plan.heads
    early = min(2, heads)
    opening = [("v", h) for h in range(early)]
    second = [("k", h) for h in range(early)] + [(n, h) for h in range(2, heads)[:1] for n in "kv"]
    sets = [opening, second] + [[("k", h), ("v", h)] for h in range(3, heads)]
    rounds = [[0], [1]] + [list(range(n, min(n + 2, len(sets)))) for n in range(2, len(sets), 2)]
    opened = share(select(plan, place, [item(name) for name in opening], []))
    most, slots, source, come, near = far_plan(plan, plane, far_frames, far_pick)

    def with_room(room, x):
        far = plan.far0 + source * room + come
        pos = jnp.where(near == -2, far, near).reshape(-1)
        packs, where = [], {}
        for index, chosen in enumerate(rounds):
            names = [name for n in chosen for name in sets[n]]
            if index:
                wait = packs[rounds[index - 1][0]][1:2]
                x = share(select(plan, place, [item(name) for name in names], wait))
            for n in chosen:
                packs.append(pack(plan, room, place, slots, x, names.index(sets[n][0]), len(sets[n])))
                for at, name in enumerate(sets[n]):
                    where[name] = (x, names.index(name), n, at)
        queries = [item(("q", h)) for h in range(heads)]
        q = share(select(plan, place, queries, packs[min(2, len(sets) - 1)][1:2]))
        halos = [
            [lax.ppermute(to_next, "tm", plan.halo(1)), lax.ppermute(to_prev, "tm", plan.halo(-1))]
            for _, to_next, to_prev in packs
        ]

        def send(n, after):
            x = hold(packs[n][0], after) if after else packs[n][0]
            x = lax.all_to_all(x, "tm", 0, 0, axis_index_groups=plan.lines(), tiled=True)
            return (x, *halos[n])

        def run(chosen, wait):
            args = []
            for h in chosen:
                kv = [where[name] for name in (("k", h), ("v", h))]
                args.append((q, h, *((x, at, recvs[n], of) for x, at, n, of in kv)))
            return list(attend(plan, room, place, pos, args, wait))

        recvs, out, first, begun = [], [], [], min(3, heads - 1)
        for n in range(len(sets)):
            after = halos[n - 1] if n else []
            if len(sets) > 2 and n == len(sets) - 2:
                after = after + q
            if len(sets) > 2 and n == len(sets) - 1:
                first = run(range(begun), [])
                after = after + halos[n] + first
            recvs.append(send(n, after))
        if begun:
            out = [merge(plan, place, share(first or run(range(begun), [])), 0, out)]
        for h in range(begun, heads - 1, 2):
            chosen = range(h, min(h + 2, heads - 1))
            out = [merge(plan, place, share(run(chosen, [])), h, out)]
        return merge(plan, place, share(run([heads - 1], out)), heads - 1, out)

    forms = [functools.partial(with_room, room) for room in plan.rooms]
    if len(forms) == 1:
        return forms[0](opened)
    level = sum((most > room).astype(jnp.int32) for room in plan.rooms[:-1])
    return lax.switch(level, forms, opened)


def solution(mesh):
    placed = (P("tm", "head"), P("tm", "head"), P("tm", "head"), P("head"), P("head"), P(), P())
    return jax.shard_map(
        local, mesh=mesh, in_specs=placed, out_specs=P("tm", "head"), check_vma=False
    )
```

```python
import functools
import math

import jax
import jax.numpy as jnp
from jax import lax
from jax.experimental import pallas as pl
from jax.experimental.pallas import tpu as pltpu
from jax.sharding import PartitionSpec as P

HEAD_DIM = 128
BLOCK = 64
NFAR = 12
EPSILON = 1e-06
MASKED = -1e30
VMEM_LIMIT = 56 * 1024 * 1024


class Plan:
    def __init__(self, frames, rows, heads):
        self.frames, self.rows = frames, rows
        self.group = 4 if heads % 4 == 0 and frames % 4 == 0 else 1
        self.planes = frames // self.group
        self.blocks = rows // BLOCK
        self.heads = heads // self.group
        bands = sum(2**band <= frames - 1 for band in range(1, NFAR // 2 + 1))
        self.slots = [*range(bands), *range(NFAR // 2, NFAR // 2 + bands)]
        full = self.group * self.group
        self.rooms = [full * 14 // 16, full] if self.group > 1 else [full]
        self.near0 = self.blocks
        self.far0 = self.blocks * (self.group + 2)

    def total(self, room):
        return self.far0 + self.planes * room

    def halo(self, step):
        step *= self.group
        return [(i, i + step) for i in range(self.frames) if 0 <= i + step < self.frames]

    def swap(self, j):
        g = self.group
        return [(i, i // g * g + (i % g ^ j)) for i in range(self.frames)]

    def lines(self):
        g = self.group
        return [[p * g + i for p in range(self.planes)] for i in range(g)]


def params():
    return dict(
        compiler_params=pltpu.CompilerParams(vmem_limit_bytes=VMEM_LIMIT),
        cost_estimate=pl.CostEstimate(flops=1, bytes_accessed=1, transcendentals=0),
    )


def select_body(scaled, n_after, group, place_ref, *refs):
    outs = refs[len(refs) - group :]
    refs = list(refs[: len(refs) - group - n_after])
    values = []
    for with_scale in scaled:
        x = refs.pop(0)[...]
        if with_scale:
            rs, gain = refs.pop(0), refs.pop(0)
            x = x.astype(jnp.float32) * rs[...] * gain[...]
        values.append(x.astype(jnp.bfloat16))
    for j, out in enumerate(outs):

        @pl.when(pl.program_id(0) == j)
        def _(out=out):
            for item, x in enumerate(values):
                out[item] = x


def select(plan, place, items, after):
    args, specs = [], []
    for x, head, rs, gain in items:

        def at(j, place, head=head):
            return 0, (place[1] ^ j) * plan.heads + head

        args.append(x)
        specs.append(pl.BlockSpec((plan.rows, HEAD_DIM), at))
        if rs is not None:
            args += [rs, gain]
            specs.append(pl.BlockSpec((plan.rows, 1), lambda j, place: (0, 0)))
            specs.append(pl.BlockSpec((1, HEAD_DIM), at))
    shape = (len(items), plan.rows, HEAD_DIM)
    scaled = [rs is not None for _, _, rs, _ in items]
    return pl.pallas_call(
        functools.partial(select_body, scaled, len(after), plan.group),
        grid_spec=pltpu.PrefetchScalarGridSpec(
            num_scalar_prefetch=1,
            grid=(plan.group,),
            in_specs=specs + [pl.BlockSpec(memory_space=pl.ANY)] * len(after),
            out_specs=[pl.BlockSpec(shape, lambda j, place: (0, 0, 0))] * plan.group,
        ),
        out_shape=[jax.ShapeDtypeStruct(shape, jnp.bfloat16)] * plan.group,
        name="select",
        **params(),
    )(place, *args, *after)


def pack_body(plan, place_ref, slot_ref, *refs):
    group, blocks = plan.group, plan.blocks
    xs = refs[:group]
    far, to_next, to_prev, sem = refs[group:]
    plane, lane = place_ref[0], place_ref[1]
    whole = slot_ref.shape[0] > plan.planes
    stride, from_plane = (plan.planes, plane) if whole else (1, 0)

    def halo(act):
        for j in range(group):
            for at, (g, out) in enumerate(((group - 1, to_next), (0, to_prev))):

                @pl.when((lane ^ j) == g)
                def _(j=j, at=at, out=out):
                    act(pltpu.make_async_copy(xs[j], out, sem.at[plan.planes, at]))

    def for_each(act):
        halo(act)

        def one_plane(dest, carry):
            for j in range(group):
                for b in range(blocks):
                    slot = slot_ref[dest * stride + from_plane, (lane ^ j) * blocks + b]

                    @pl.when(slot >= 0)
                    def _(j=j, b=b, slot=slot):
                        dst = pl.ds(pl.multiple_of(slot * BLOCK, BLOCK), BLOCK)
                        src = xs[j].at[:, b * BLOCK : (b + 1) * BLOCK, :]
                        place = sem.at[dest, j * blocks + b]
                        act(pltpu.make_async_copy(src, far.at[dest, :, dst, :], place))

            return carry

        lax.fori_loop(0, plan.planes, one_plane, 0)

    for_each(lambda copy: copy.start())
    for_each(lambda copy: copy.wait())


def pack(plan, room, place, slots, xs, first, count):
    smem = pl.BlockSpec(memory_space=pltpu.SMEM)
    any_spec = pl.BlockSpec(memory_space=pl.ANY)
    frame = jax.ShapeDtypeStruct((count, plan.rows, HEAD_DIM), jnp.bfloat16)
    far = jax.ShapeDtypeStruct((plan.planes, count, room * BLOCK, HEAD_DIM), jnp.bfloat16)
    return pl.pallas_call(
        functools.partial(pack_body, plan),
        grid=(1,),
        in_specs=[smem, smem]
        + [pl.BlockSpec((count, plan.rows, HEAD_DIM), lambda i: (first // count, 0, 0))] * plan.group,
        out_specs=[any_spec] * 3,
        out_shape=[far, frame, frame],
        scratch_shapes=[pltpu.SemaphoreType.DMA((plan.planes + 1, plan.group * plan.blocks))],
        name="pack",
        **params(),
    )(place, slots, *xs)


def hold_body(*refs):
    pass


def hold(x, after):
    any_spec = pl.BlockSpec(memory_space=pl.ANY)
    return pl.pallas_call(
        hold_body,
        in_specs=[any_spec] * (1 + len(after)),
        out_specs=any_spec,
        out_shape=jax.ShapeDtypeStruct(x.shape, x.dtype),
        input_output_aliases={0: 0},
        name="hold",
        **params(),
    )(x, *after)


def attend_body(plan, room, heads, n_wait, *refs):
    place_ref, pos_ref = refs[:2]
    group, rows, nfar = plan.group, plan.rows, len(plan.slots)
    step = 3 * group + 6
    inputs = [refs[2 + h * step : 2 + (h + 1) * step] for h in range(len(heads))]
    refs = refs[2 + len(heads) * step + n_wait :]
    outs, scratch = refs[:group], refs[group:]
    qbuf, kvbuf, obuf, fark, farv, *bufs, sem, out_sem = scratch
    sbufs, mbufs = bufs[:2], bufs[2:]
    plane, lane = place_ref[0], place_ref[1]
    scale = math.log2(math.e) / math.sqrt(HEAD_DIM)
    tile = rows // 2
    per_tile = tile // BLOCK
    lanes = lax.broadcasted_iota(jnp.int32, (1, nfar * BLOCK), 1) // BLOCK
    contract = (((1,), (1,)), ((), ()))

    def copies(h):
        made, slot = [], h % 2
        qs, rest = inputs[h][:group], inputs[h][group:]
        at_q, *at_kv = heads[h]

        def add(src, dst):
            made.append(pltpu.make_async_copy(src, dst, sem.at[slot, len(made)]))

        for j in range(group):
            add(qs[j].at[at_q], qbuf.at[slot, lane ^ j])
        for which, (item, of_set) in enumerate(at_kv):
            xs, (far, before, after) = rest[:group], rest[group : group + 3]
            rest = rest[group + 3 :]

            def at(first, count, which=which):
                first = first * BLOCK
                if not isinstance(first, int):
                    first = pl.multiple_of(first, BLOCK)
                return kvbuf.at[slot, which, pl.ds(first, count * BLOCK), :]

            for j in range(group):
                add(xs[j].at[item], at(plan.near0 + (lane ^ j) * plan.blocks, plan.blocks))
            add(before.at[of_set], at(0, plan.blocks))
            add(after.at[of_set], at(plan.near0 + group * plan.blocks, plan.blocks))
            for p in range(plan.planes):
                add(far.at[p, of_set], at(plan.far0 + p * room, room))
        return made

    def score(h, f, t):
        slot = h % 2
        first = pl.multiple_of((plan.near0 + (f - 1) * plan.blocks) * BLOCK, BLOCK)
        q = qbuf[slot, f, t * tile : (t + 1) * tile, :]
        peak = None
        for part in range(3):
            k = kvbuf[slot, 0, pl.ds(first + part * rows, rows), :]
            s = lax.dot_general(q, k, contract, preferred_element_type=jnp.float32)
            sbufs[t][:, part * rows : (part + 1) * rows] = s
            s = functools.reduce(
                jnp.maximum, [s[:, c : c + HEAD_DIM] for c in range(0, rows, HEAD_DIM)]
            )
            ok = there(f, part)
            if ok is not None:
                s = jnp.where(ok, s, MASKED)
            peak = s if peak is None else jnp.maximum(peak, s)
        for i in range(per_tile):
            block = t * per_tile + i
            ok = lanes < 0
            for n in range(nfar):
                at = pos_ref[(f * plan.blocks + block) * nfar + n]
                src = pl.ds(pl.multiple_of(jnp.maximum(at, 0) * BLOCK, BLOCK), BLOCK)
                fark[block, n * BLOCK : (n + 1) * BLOCK, :] = kvbuf[slot, 0, src, :]
                farv[block, n * BLOCK : (n + 1) * BLOCK, :] = kvbuf[slot, 1, src, :]
                ok = ok | ((lanes == n) & (at >= 0))
            some = slice(i * BLOCK, (i + 1) * BLOCK)
            s = lax.dot_general(
                q[some], fark[block], contract, preferred_element_type=jnp.float32
            )
            s = jnp.where(ok, s, MASKED)
            sbufs[t][some, 3 * rows :] = s
            s = functools.reduce(
                jnp.maximum, [s[:, c : c + HEAD_DIM] for c in range(0, nfar * BLOCK, HEAD_DIM)]
            )
            mbufs[t][some, :] = jnp.maximum(peak[some], s)

    def there(f, part):
        frame = plane * group + f
        return (frame > 0, None, frame < plan.frames - 1)[part]

    def weigh(h, f, t):
        slot = h % 2
        first = pl.multiple_of((plan.near0 + (f - 1) * plan.blocks) * BLOCK, BLOCK)
        peak = jnp.max(mbufs[t][...], axis=1, keepdims=True)
        total, out = 0.0, 0.0
        for part in range(3):
            ok = there(f, part)
            less = peak if ok is None else jnp.where(ok, peak, -MASKED)
            p = jnp.exp2((sbufs[t][:, part * rows : (part + 1) * rows] - less) * scale)
            total += jnp.sum(p, axis=1, keepdims=True)
            v = kvbuf[slot, 1, pl.ds(first + part * rows, rows), :]
            out += jnp.dot(p.astype(jnp.bfloat16), v, preferred_element_type=jnp.float32)
        p = jnp.exp2((sbufs[t][:, 3 * rows :] - peak) * scale)
        total += jnp.sum(p, axis=1, keepdims=True)
        p = p.astype(jnp.bfloat16)
        far_out = [
            jnp.dot(
                p[i * BLOCK : (i + 1) * BLOCK],
                farv[t * per_tile + i],
                preferred_element_type=jnp.float32,
            )
            for i in range(per_tile)
        ]
        out = (out + jnp.concatenate(far_out, axis=0)) / total
        obuf[f, h, t * tile : (t + 1) * tile, :] = out.astype(jnp.bfloat16)

    def one_frame(f, h):
        score(h, f, 1)
        weigh(h, f, 0)
        score(h, jnp.minimum(f + 1, group - 1), 0)
        weigh(h, f, 1)

    for copy in copies(0):
        copy.start()
    for h in range(len(heads)):
        if h + 1 < len(heads):
            for copy in copies(h + 1):
                copy.start()
        for copy in copies(h):
            copy.wait()
        score(h, 0, 0)
        lax.fori_loop(0, group, lambda f, c, h=h: (one_frame(f, h), c)[1], 0)
    made = []
    for j in range(group):
        made.append(pltpu.make_async_copy(obuf.at[lane ^ j], outs[j], out_sem.at[j]))
    for copy in made:
        copy.start()
    for copy in made:
        copy.wait()


def attend(plan, room, place, pos, heads, wait):
    nfar, count = len(plan.slots), len(heads)
    any_spec = pl.BlockSpec(memory_space=pl.ANY)
    smem = pl.BlockSpec(memory_space=pltpu.SMEM)
    args, items = [], []
    for q, at_q, *kv in heads:
        args += q
        items.append((at_q, *((item, of_set) for _, item, _, of_set in kv)))
        for xs, _, recv, _ in kv:
            args += [*xs, *recv]
    shape = jax.ShapeDtypeStruct((count, plan.rows, HEAD_DIM), jnp.bfloat16)
    return pl.pallas_call(
        functools.partial(attend_body, plan, room, items, len(wait)),
        in_specs=[smem, smem] + [any_spec] * (len(args) + len(wait)),
        out_specs=[any_spec] * plan.group,
        out_shape=[shape] * plan.group,
        scratch_shapes=[
            pltpu.VMEM((2, plan.group, plan.rows, HEAD_DIM), jnp.bfloat16),
            pltpu.VMEM((2, 2, plan.total(room) * BLOCK, HEAD_DIM), jnp.bfloat16),
            pltpu.VMEM((plan.group, count, plan.rows, HEAD_DIM), jnp.bfloat16),
            pltpu.VMEM((plan.blocks, nfar * BLOCK, HEAD_DIM), jnp.bfloat16),
            pltpu.VMEM((plan.blocks, nfar * BLOCK, HEAD_DIM), jnp.bfloat16),
            pltpu.VMEM((plan.rows // 2, 3 * plan.rows + nfar * BLOCK), jnp.float32),
            pltpu.VMEM((plan.rows // 2, 3 * plan.rows + nfar * BLOCK), jnp.float32),
            pltpu.VMEM((plan.rows // 2, HEAD_DIM), jnp.float32),
            pltpu.VMEM((plan.rows // 2, HEAD_DIM), jnp.float32),
            pltpu.SemaphoreType.DMA((2, 3 * plan.group + 2 * (2 + plan.planes))),
            pltpu.SemaphoreType.DMA((plan.group,)),
        ],
        name="attend",
        **params(),
    )(place, pos, *args, *wait)


def merge_body(plan, first, place_ref, *refs):
    xs, (out, sem) = refs[: plan.group], refs[-2:]
    copies = []
    for j, x in enumerate(xs):
        for h in range(x.shape[0]):
            start = ((place_ref[1] ^ j) * plan.heads + first + h) * HEAD_DIM
            dst = out.at[:, pl.ds(pl.multiple_of(start, HEAD_DIM), HEAD_DIM)]
            copies.append(pltpu.make_async_copy(x.at[h], dst, sem.at[len(copies)]))
    for copy in copies:
        copy.start()
    for copy in copies:
        copy.wait()


def merge(plan, place, xs, first, out):
    width = plan.group * plan.heads * HEAD_DIM
    any_spec = pl.BlockSpec(memory_space=pl.ANY)
    vmem = pl.BlockSpec(memory_space=pltpu.VMEM)
    return pl.pallas_call(
        functools.partial(merge_body, plan, first),
        in_specs=[pl.BlockSpec(memory_space=pltpu.SMEM)]
        + [vmem] * plan.group
        + [any_spec] * len(out),
        out_specs=any_spec,
        out_shape=jax.ShapeDtypeStruct((plan.rows, width), jnp.bfloat16),
        input_output_aliases={1 + plan.group: 0} if out else {},
        scratch_shapes=[pltpu.SemaphoreType.DMA((plan.group * xs[0].shape[0],))],
        name="merge",
        **params(),
    )(place, *xs, *out)


def far_plan(plan, plane, far_frames, far_pick):
    group, blocks, frames, planes = plan.group, plan.blocks, plan.frames, plan.planes
    own = group * blocks
    lists = jnp.concatenate([far_frames[:, s : s + 1] for s in plan.slots], axis=1)
    every = jnp.arange(frames, dtype=jnp.int32)
    used = jnp.any(lists.reshape(frames, -1)[:, :, None] == every, axis=1)
    away = every[None, :] - (every // group * group)[:, None]
    used = used & ((away < -1) | (away > group))
    picked = far_pick[:, :, None] == jnp.arange(blocks, dtype=jnp.int32)
    needed = jnp.any((used[:, :, None] & picked).reshape(planes, group, frames, blocks), axis=1)
    needed = needed.reshape(planes * planes, own)
    before = (jnp.arange(own)[:, None] < jnp.arange(own)[None, :]).astype(jnp.float32)
    slot = jnp.dot(needed.astype(jnp.float32), before, precision=lax.Precision.HIGHEST)
    slot = jnp.where(needed, slot.astype(jnp.int32), -1)
    most = jnp.max(slot) + 1

    mine = lax.dynamic_slice_in_dim(lists, plane * own, own, 0)
    g = jnp.maximum(mine, 0)
    rows = lax.dynamic_slice_in_dim(far_pick, plane * group, group, 0)
    rows = jnp.repeat(rows, blocks, axis=0)
    pick = jnp.sum(jnp.where(g[:, :, None] == every, rows[:, None, :], 0), axis=2)
    come = lax.dynamic_slice_in_dim(slot, plane * planes, planes, 0).reshape(-1)
    hit = (g * blocks + pick)[:, :, None] == jnp.arange(frames * blocks, dtype=jnp.int32)
    come = jnp.sum(jnp.where(hit, come, 0), axis=2)
    away = g - plane * group
    near = jnp.where((away >= -1) & (away <= group), plan.near0 + away * blocks + pick, -2)
    near = jnp.where(mine >= 0, near, -1)
    if planes > 8:
        slot = slot.reshape(planes, planes, own)
        slot = lax.dynamic_slice_in_dim(slot, plane, 1, 1).reshape(planes, own)
    return most, slot, g // group, come, near


def local(query, key, value, q_gain, k_gain, far_frames, far_pick):
    rows, width = query.shape
    full_width = width * lax.axis_size("head")
    plan = Plan(lax.axis_size("tm"), rows, width // HEAD_DIM)
    frame = lax.axis_index("tm").astype(jnp.int32)
    plane = frame // plan.group
    place = jnp.stack([plane, frame % plan.group])

    def share(xs):
        return [xs[0]] + [lax.ppermute(xs[j], "tm", plan.swap(j)) for j in range(1, plan.group)]

    sums = jnp.stack([jnp.sum(jnp.square(x.astype(jnp.float32)), axis=1) for x in (query, key)])
    q_rs, k_rs = lax.rsqrt(lax.psum(sums, "head") / full_width + EPSILON)[:, :, None]
    q_gain, k_gain = q_gain[None, :], k_gain[None, :]

    def item(name):
        kind, h = name
        if kind == "k":
            return key, h, k_rs, k_gain
        return (value, h, None, None) if kind == "v" else (query, h, q_rs, q_gain)

    heads = plan.heads
    early = min(2, heads)
    opening = [("v", h) for h in range(early)]
    second = [("k", h) for h in range(early)] + [(n, h) for h in range(2, heads)[:1] for n in "kv"]
    sets = [opening, second] + [[("k", h), ("v", h)] for h in range(3, heads)]
    rounds = [[0], [1]] + [list(range(n, min(n + 2, len(sets)))) for n in range(2, len(sets), 2)]
    opened = share(select(plan, place, [item(name) for name in opening], []))
    most, slots, source, come, near = far_plan(plan, plane, far_frames, far_pick)

    def with_room(room, x):
        far = plan.far0 + source * room + come
        pos = jnp.where(near == -2, far, near).reshape(-1)
        packs, where = [], {}
        for index, chosen in enumerate(rounds):
            names = [name for n in chosen for name in sets[n]]
            if index:
                wait = packs[rounds[index - 1][0]][1:2]
                x = share(select(plan, place, [item(name) for name in names], wait))
            for n in chosen:
                packs.append(pack(plan, room, place, slots, x, names.index(sets[n][0]), len(sets[n])))
                for at, name in enumerate(sets[n]):
                    where[name] = (x, names.index(name), n, at)
        queries = [item(("q", h)) for h in range(heads)]
        q = share(select(plan, place, queries, packs[min(2, len(sets) - 1)][1:2]))
        halos = [
            [lax.ppermute(to_next, "tm", plan.halo(1)), lax.ppermute(to_prev, "tm", plan.halo(-1))]
            for _, to_next, to_prev in packs
        ]

        def send(n, after):
            x = hold(packs[n][0], after) if after else packs[n][0]
            x = lax.all_to_all(x, "tm", 0, 0, axis_index_groups=plan.lines(), tiled=True)
            return (x, *halos[n])

        def run(chosen, wait):
            args = []
            for h in chosen:
                kv = [where[name] for name in (("k", h), ("v", h))]
                args.append((q, h, *((x, at, recvs[n], of) for x, at, n, of in kv)))
            return list(attend(plan, room, place, pos, args, wait))

        recvs, out, first, begun = [], [], [], min(2, heads - 1)
        for n in range(len(sets)):
            after = halos[n - 1] if n else []
            if len(sets) > 2 and n == len(sets) - 2:
                after = after + q
            if len(sets) > 2 and n == len(sets) - 1:
                first = run(range(begun), [])
                after = after + halos[n] + first
            recvs.append(send(n, after))
        if begun:
            out = [merge(plan, place, share(first or run(range(begun), [])), 0, out)]
        for h in range(begun, heads - 1, 2):
            chosen = range(h, min(h + 2, heads - 1))
            out = [merge(plan, place, share(run(chosen, [])), h, out)]
        return merge(plan, place, share(run([heads - 1], out)), heads - 1, out)

    forms = [functools.partial(with_room, room) for room in plan.rooms]
    if len(forms) == 1:
        return forms[0](opened)
    return lax.cond(most > plan.rooms[0], forms[1], forms[0], opened)


def solution(mesh):
    placed = (P("tm", "head"), P("tm", "head"), P("tm", "head"), P("head"), P("head"), P(), P())
    return jax.shard_map(
        local, mesh=mesh, in_specs=placed, out_specs=P("tm", "head"), check_vma=False
    )
```

```python
import functools
import math

import jax
import jax.numpy as jnp
from jax import lax
from jax.experimental import pallas as pl
from jax.experimental.pallas import tpu as pltpu
from jax.sharding import PartitionSpec as P

HEAD_DIM = 128
BLOCK = 64
NFAR = 12
EPSILON = 1e-06
MASKED = -1e30
VMEM_LIMIT = 56 * 1024 * 1024


class Plan:
    def __init__(self, frames, rows, heads):
        self.frames, self.rows = frames, rows
        self.group = 4 if heads % 4 == 0 and frames % 4 == 0 else 1
        self.planes = frames // self.group
        self.blocks = rows // BLOCK
        self.heads = heads // self.group
        bands = sum(2**band <= frames - 1 for band in range(1, NFAR // 2 + 1))
        self.slots = [*range(bands), *range(NFAR // 2, NFAR // 2 + bands)]
        full = self.group * self.group
        self.rooms = [full * 14 // 16, full] if self.group > 1 else [full]
        self.near0 = self.blocks
        self.far0 = self.blocks * (self.group + 2)

    def total(self, room):
        return self.far0 + self.planes * room

    def halo(self, step):
        step *= self.group
        return [(i, i + step) for i in range(self.frames) if 0 <= i + step < self.frames]

    def swap(self, j):
        g = self.group
        return [(i, i // g * g + (i % g ^ j)) for i in range(self.frames)]

    def lines(self):
        g = self.group
        return [[p * g + i for p in range(self.planes)] for i in range(g)]


def params():
    return dict(
        compiler_params=pltpu.CompilerParams(vmem_limit_bytes=VMEM_LIMIT),
        cost_estimate=pl.CostEstimate(flops=1, bytes_accessed=1, transcendentals=0),
    )


def select_body(scaled, n_after, group, place_ref, *refs):
    outs = refs[len(refs) - group :]
    refs = list(refs[: len(refs) - group - n_after])
    values = []
    for with_scale in scaled:
        x = refs.pop(0)[...]
        if with_scale:
            rs, gain = refs.pop(0), refs.pop(0)
            x = x.astype(jnp.float32) * rs[...] * gain[...]
        values.append(x.astype(jnp.bfloat16))
    for j, out in enumerate(outs):

        @pl.when(pl.program_id(0) == j)
        def _(out=out):
            for item, x in enumerate(values):
                out[item] = x


def select(plan, place, items, after):
    args, specs = [], []
    for x, head, rs, gain in items:

        def at(j, place, head=head):
            return 0, (place[1] ^ j) * plan.heads + head

        args.append(x)
        specs.append(pl.BlockSpec((plan.rows, HEAD_DIM), at))
        if rs is not None:
            args += [rs, gain]
            specs.append(pl.BlockSpec((plan.rows, 1), lambda j, place: (0, 0)))
            specs.append(pl.BlockSpec((1, HEAD_DIM), at))
    shape = (len(items), plan.rows, HEAD_DIM)
    scaled = [rs is not None for _, _, rs, _ in items]
    return pl.pallas_call(
        functools.partial(select_body, scaled, len(after), plan.group),
        grid_spec=pltpu.PrefetchScalarGridSpec(
            num_scalar_prefetch=1,
            grid=(plan.group,),
            in_specs=specs + [pl.BlockSpec(memory_space=pl.ANY)] * len(after),
            out_specs=[pl.BlockSpec(shape, lambda j, place: (0, 0, 0))] * plan.group,
        ),
        out_shape=[jax.ShapeDtypeStruct(shape, jnp.bfloat16)] * plan.group,
        name="select",
        **params(),
    )(place, *args, *after)


def pack_body(plan, place_ref, slot_ref, *refs):
    group, blocks = plan.group, plan.blocks
    xs = refs[:group]
    far, to_next, to_prev, sem = refs[group:]
    plane, lane = place_ref[0], place_ref[1]
    whole = slot_ref.shape[0] > plan.planes
    stride, from_plane = (plan.planes, plane) if whole else (1, 0)

    def halo(act):
        for j in range(group):
            for at, (g, out) in enumerate(((group - 1, to_next), (0, to_prev))):

                @pl.when((lane ^ j) == g)
                def _(j=j, at=at, out=out):
                    act(pltpu.make_async_copy(xs[j], out, sem.at[plan.planes, at]))

    def for_each(act):
        halo(act)

        def one_plane(dest, carry):
            for j in range(group):
                for b in range(blocks):
                    slot = slot_ref[dest * stride + from_plane, (lane ^ j) * blocks + b]

                    @pl.when(slot >= 0)
                    def _(j=j, b=b, slot=slot):
                        dst = pl.ds(pl.multiple_of(slot * BLOCK, BLOCK), BLOCK)
                        src = xs[j].at[:, b * BLOCK : (b + 1) * BLOCK, :]
                        place = sem.at[dest, j * blocks + b]
                        act(pltpu.make_async_copy(src, far.at[dest, :, dst, :], place))

            return carry

        lax.fori_loop(0, plan.planes, one_plane, 0)

    for_each(lambda copy: copy.start())
    for_each(lambda copy: copy.wait())


def pack(plan, room, place, slots, xs, first, count):
    smem = pl.BlockSpec(memory_space=pltpu.SMEM)
    any_spec = pl.BlockSpec(memory_space=pl.ANY)
    frame = jax.ShapeDtypeStruct((count, plan.rows, HEAD_DIM), jnp.bfloat16)
    far = jax.ShapeDtypeStruct((plan.planes, count, room * BLOCK, HEAD_DIM), jnp.bfloat16)
    return pl.pallas_call(
        functools.partial(pack_body, plan),
        grid=(1,),
        in_specs=[smem, smem]
        + [pl.BlockSpec((count, plan.rows, HEAD_DIM), lambda i: (first // count, 0, 0))] * plan.group,
        out_specs=[any_spec] * 3,
        out_shape=[far, frame, frame],
        scratch_shapes=[pltpu.SemaphoreType.DMA((plan.planes + 1, plan.group * plan.blocks))],
        name="pack",
        **params(),
    )(place, slots, *xs)


def hold_body(*refs):
    pass


def hold(x, after):
    any_spec = pl.BlockSpec(memory_space=pl.ANY)
    return pl.pallas_call(
        hold_body,
        in_specs=[any_spec] * (1 + len(after)),
        out_specs=any_spec,
        out_shape=jax.ShapeDtypeStruct(x.shape, x.dtype),
        input_output_aliases={0: 0},
        name="hold",
        **params(),
    )(x, *after)


def tile_rows(plan):
    return plan.rows if plan.group % 2 == 0 else plan.rows // 2


def attend_body(plan, room, heads, n_wait, *refs):
    place_ref, pos_ref = refs[:2]
    group, rows, nfar = plan.group, plan.rows, len(plan.slots)
    step = 3 * group + 6
    inputs = [refs[2 + h * step : 2 + (h + 1) * step] for h in range(len(heads))]
    refs = refs[2 + len(heads) * step + n_wait :]
    outs, scratch = refs[:group], refs[group:]
    qbuf, kvbuf, obuf, fark, farv, *bufs, sem, out_sem = scratch
    sbufs, mbufs = bufs[:2], bufs[2:]
    plane, lane = place_ref[0], place_ref[1]
    scale = math.log2(math.e) / math.sqrt(HEAD_DIM)
    tile = tile_rows(plan)
    per_tile = tile // BLOCK
    lanes = lax.broadcasted_iota(jnp.int32, (1, nfar * BLOCK), 1) // BLOCK
    contract = (((1,), (1,)), ((), ()))

    def copies(h):
        made, slot = [], h % 2
        qs, rest = inputs[h][:group], inputs[h][group:]
        at_q, *at_kv = heads[h]

        def add(src, dst):
            made.append(pltpu.make_async_copy(src, dst, sem.at[slot, len(made)]))

        for j in range(group):
            add(qs[j].at[at_q], qbuf.at[slot, lane ^ j])
        for which, (item, of_set) in enumerate(at_kv):
            xs, (far, before, after) = rest[:group], rest[group : group + 3]
            rest = rest[group + 3 :]

            def at(first, count, which=which):
                first = first * BLOCK
                if not isinstance(first, int):
                    first = pl.multiple_of(first, BLOCK)
                return kvbuf.at[slot, which, pl.ds(first, count * BLOCK), :]

            for j in range(group):
                add(xs[j].at[item], at(plan.near0 + (lane ^ j) * plan.blocks, plan.blocks))
            add(before.at[of_set], at(0, plan.blocks))
            add(after.at[of_set], at(plan.near0 + group * plan.blocks, plan.blocks))
            for p in range(plan.planes):
                add(far.at[p, of_set], at(plan.far0 + p * room, room))
        return made

    def score(h, i, b):
        slot = h % 2
        f, t = unit(i, b)
        first = pl.multiple_of((plan.near0 + (f - 1) * plan.blocks) * BLOCK, BLOCK)
        q = qbuf[slot, f, t * tile : (t + 1) * tile, :]
        peak = None
        for part in range(3):
            k = kvbuf[slot, 0, pl.ds(first + part * rows, rows), :]
            s = lax.dot_general(q, k, contract, preferred_element_type=jnp.float32)
            sbufs[b][:, part * rows : (part + 1) * rows] = s
            s = functools.reduce(
                jnp.maximum, [s[:, c : c + HEAD_DIM] for c in range(0, rows, HEAD_DIM)]
            )
            ok = there(f, part)
            if ok is not None:
                s = jnp.where(ok, s, MASKED)
            peak = s if peak is None else jnp.maximum(peak, s)
        for n_block in range(per_tile):
            block = t * per_tile + n_block
            at_far = b * per_tile + n_block
            ok = lanes < 0
            for n in range(nfar):
                at = pos_ref[(f * plan.blocks + block) * nfar + n]
                src = pl.ds(pl.multiple_of(jnp.maximum(at, 0) * BLOCK, BLOCK), BLOCK)
                fark[at_far, n * BLOCK : (n + 1) * BLOCK, :] = kvbuf[slot, 0, src, :]
                farv[at_far, n * BLOCK : (n + 1) * BLOCK, :] = kvbuf[slot, 1, src, :]
                ok = ok | ((lanes == n) & (at >= 0))
            some = slice(n_block * BLOCK, (n_block + 1) * BLOCK)
            s = lax.dot_general(
                q[some], fark[at_far], contract, preferred_element_type=jnp.float32
            )
            s = jnp.where(ok, s, MASKED)
            sbufs[b][some, 3 * rows :] = s
            s = functools.reduce(
                jnp.maximum, [s[:, c : c + HEAD_DIM] for c in range(0, nfar * BLOCK, HEAD_DIM)]
            )
            mbufs[b][some, :] = jnp.maximum(peak[some], s)

    def unit(i, b):
        return (2 * i + b, 0) if tile == rows else (i, b)

    def there(f, part):
        frame = plane * group + f
        return (frame > 0, None, frame < plan.frames - 1)[part]

    def weigh(h, i, b):
        slot = h % 2
        f, t = unit(i, b)
        first = pl.multiple_of((plan.near0 + (f - 1) * plan.blocks) * BLOCK, BLOCK)
        peak = jnp.max(mbufs[b][...], axis=1, keepdims=True)
        total, out = 0.0, 0.0
        for part in range(3):
            ok = there(f, part)
            less = peak if ok is None else jnp.where(ok, peak, -MASKED)
            p = jnp.exp2((sbufs[b][:, part * rows : (part + 1) * rows] - less) * scale)
            total += jnp.sum(p, axis=1, keepdims=True)
            v = kvbuf[slot, 1, pl.ds(first + part * rows, rows), :]
            out += jnp.dot(p.astype(jnp.bfloat16), v, preferred_element_type=jnp.float32)
        p = jnp.exp2((sbufs[b][:, 3 * rows :] - peak) * scale)
        total += jnp.sum(p, axis=1, keepdims=True)
        p = p.astype(jnp.bfloat16)
        far_out = [
            jnp.dot(
                p[n * BLOCK : (n + 1) * BLOCK],
                farv[b * per_tile + n],
                preferred_element_type=jnp.float32,
            )
            for n in range(per_tile)
        ]
        out = (out + jnp.concatenate(far_out, axis=0)) / total
        obuf[f, h, t * tile : (t + 1) * tile, :] = out.astype(jnp.bfloat16)

    pairs = group * rows // tile // 2

    def one_pair(i, h):
        score(h, i, 1)
        weigh(h, i, 0)
        score(h, jnp.minimum(i + 1, pairs - 1), 0)
        weigh(h, i, 1)

    for copy in copies(0):
        copy.start()
    for h in range(len(heads)):
        if h + 1 < len(heads):
            for copy in copies(h + 1):
                copy.start()
        for copy in copies(h):
            copy.wait()
        score(h, 0, 0)
        lax.fori_loop(0, pairs, lambda i, c, h=h: (one_pair(i, h), c)[1], 0)
    made = []
    for j in range(group):
        made.append(pltpu.make_async_copy(obuf.at[lane ^ j], outs[j], out_sem.at[j]))
    for copy in made:
        copy.start()
    for copy in made:
        copy.wait()


def attend(plan, room, place, pos, heads, wait):
    nfar, count, tile = len(plan.slots), len(heads), tile_rows(plan)
    any_spec = pl.BlockSpec(memory_space=pl.ANY)
    smem = pl.BlockSpec(memory_space=pltpu.SMEM)
    args, items = [], []
    for q, at_q, *kv in heads:
        args += q
        items.append((at_q, *((item, of_set) for _, item, _, of_set in kv)))
        for xs, _, recv, _ in kv:
            args += [*xs, *recv]
    shape = jax.ShapeDtypeStruct((count, plan.rows, HEAD_DIM), jnp.bfloat16)
    return pl.pallas_call(
        functools.partial(attend_body, plan, room, items, len(wait)),
        in_specs=[smem, smem] + [any_spec] * (len(args) + len(wait)),
        out_specs=[any_spec] * plan.group,
        out_shape=[shape] * plan.group,
        scratch_shapes=[
            pltpu.VMEM((2, plan.group, plan.rows, HEAD_DIM), jnp.bfloat16),
            pltpu.VMEM((2, 2, plan.total(room) * BLOCK, HEAD_DIM), jnp.bfloat16),
            pltpu.VMEM((plan.group, count, plan.rows, HEAD_DIM), jnp.bfloat16),
            pltpu.VMEM((2 * tile // BLOCK, nfar * BLOCK, HEAD_DIM), jnp.bfloat16),
            pltpu.VMEM((2 * tile // BLOCK, nfar * BLOCK, HEAD_DIM), jnp.bfloat16),
            pltpu.VMEM((tile, 3 * plan.rows + nfar * BLOCK), jnp.float32),
            pltpu.VMEM((tile, 3 * plan.rows + nfar * BLOCK), jnp.float32),
            pltpu.VMEM((tile, HEAD_DIM), jnp.float32),
            pltpu.VMEM((tile, HEAD_DIM), jnp.float32),
            pltpu.SemaphoreType.DMA((2, 3 * plan.group + 2 * (2 + plan.planes))),
            pltpu.SemaphoreType.DMA((plan.group,)),
        ],
        name="attend",
        **params(),
    )(place, pos, *args, *wait)


def merge_body(plan, first, place_ref, *refs):
    xs, (out, sem) = refs[: plan.group], refs[-2:]
    copies = []
    for j, x in enumerate(xs):
        for h in range(x.shape[0]):
            start = ((place_ref[1] ^ j) * plan.heads + first + h) * HEAD_DIM
            dst = out.at[:, pl.ds(pl.multiple_of(start, HEAD_DIM), HEAD_DIM)]
            copies.append(pltpu.make_async_copy(x.at[h], dst, sem.at[len(copies)]))
    for copy in copies:
        copy.start()
    for copy in copies:
        copy.wait()


def merge(plan, place, xs, first, out):
    width = plan.group * plan.heads * HEAD_DIM
    any_spec = pl.BlockSpec(memory_space=pl.ANY)
    vmem = pl.BlockSpec(memory_space=pltpu.VMEM)
    return pl.pallas_call(
        functools.partial(merge_body, plan, first),
        in_specs=[pl.BlockSpec(memory_space=pltpu.SMEM)]
        + [vmem] * plan.group
        + [any_spec] * len(out),
        out_specs=any_spec,
        out_shape=jax.ShapeDtypeStruct((plan.rows, width), jnp.bfloat16),
        input_output_aliases={1 + plan.group: 0} if out else {},
        scratch_shapes=[pltpu.SemaphoreType.DMA((plan.group * xs[0].shape[0],))],
        name="merge",
        **params(),
    )(place, *xs, *out)


def far_plan(plan, plane, far_frames, far_pick):
    group, blocks, frames, planes = plan.group, plan.blocks, plan.frames, plan.planes
    own = group * blocks
    lists = jnp.concatenate([far_frames[:, s : s + 1] for s in plan.slots], axis=1)
    every = jnp.arange(frames, dtype=jnp.int32)
    used = jnp.any(lists.reshape(frames, -1)[:, :, None] == every, axis=1)
    away = every[None, :] - (every // group * group)[:, None]
    used = used & ((away < -1) | (away > group))
    picked = far_pick[:, :, None] == jnp.arange(blocks, dtype=jnp.int32)
    needed = jnp.any((used[:, :, None] & picked).reshape(planes, group, frames, blocks), axis=1)
    needed = needed.reshape(planes * planes, own)
    before = (jnp.arange(own)[:, None] < jnp.arange(own)[None, :]).astype(jnp.float32)
    slot = jnp.dot(needed.astype(jnp.float32), before, precision=lax.Precision.HIGHEST)
    slot = jnp.where(needed, slot.astype(jnp.int32), -1)
    most = jnp.max(slot) + 1

    mine = lax.dynamic_slice_in_dim(lists, plane * own, own, 0)
    g = jnp.maximum(mine, 0)
    rows = lax.dynamic_slice_in_dim(far_pick, plane * group, group, 0)
    rows = jnp.repeat(rows, blocks, axis=0)
    pick = jnp.sum(jnp.where(g[:, :, None] == every, rows[:, None, :], 0), axis=2)
    come = lax.dynamic_slice_in_dim(slot, plane * planes, planes, 0).reshape(-1)
    hit = (g * blocks + pick)[:, :, None] == jnp.arange(frames * blocks, dtype=jnp.int32)
    come = jnp.sum(jnp.where(hit, come, 0), axis=2)
    away = g - plane * group
    near = jnp.where((away >= -1) & (away <= group), plan.near0 + away * blocks + pick, -2)
    near = jnp.where(mine >= 0, near, -1)
    if planes > 8:
        slot = slot.reshape(planes, planes, own)
        slot = lax.dynamic_slice_in_dim(slot, plane, 1, 1).reshape(planes, own)
    return most, slot, g // group, come, near


def local(query, key, value, q_gain, k_gain, far_frames, far_pick):
    rows, width = query.shape
    full_width = width * lax.axis_size("head")
    plan = Plan(lax.axis_size("tm"), rows, width // HEAD_DIM)
    frame = lax.axis_index("tm").astype(jnp.int32)
    plane = frame // plan.group
    place = jnp.stack([plane, frame % plan.group])

    def share(xs):
        return [xs[0]] + [lax.ppermute(xs[j], "tm", plan.swap(j)) for j in range(1, plan.group)]

    sums = jnp.stack([jnp.sum(jnp.square(x.astype(jnp.float32)), axis=1) for x in (query, key)])
    q_rs, k_rs = lax.rsqrt(lax.psum(sums, "head") / full_width + EPSILON)[:, :, None]
    q_gain, k_gain = q_gain[None, :], k_gain[None, :]

    def item(name):
        kind, h = name
        if kind == "k":
            return key, h, k_rs, k_gain
        return (value, h, None, None) if kind == "v" else (query, h, q_rs, q_gain)

    heads = plan.heads
    early = min(2, heads)
    opening = [("v", h) for h in range(early)]
    second = [("k", h) for h in range(early)] + [(n, h) for h in range(2, heads)[:1] for n in "kv"]
    sets = [opening, second] + [[("k", h), ("v", h)] for h in range(3, heads)]
    rounds = [[0], [1]] + [list(range(n, min(n + 2, len(sets)))) for n in range(2, len(sets), 2)]
    opened = share(select(plan, place, [item(name) for name in opening], []))
    most, slots, source, come, near = far_plan(plan, plane, far_frames, far_pick)

    def with_room(room, x):
        far = plan.far0 + source * room + come
        pos = jnp.where(near == -2, far, near).reshape(-1)
        packs, where = [], {}
        for index, chosen in enumerate(rounds):
            names = [name for n in chosen for name in sets[n]]
            if index:
                wait = packs[rounds[index - 1][0]][1:2]
                x = share(select(plan, place, [item(name) for name in names], wait))
            for n in chosen:
                packs.append(pack(plan, room, place, slots, x, names.index(sets[n][0]), len(sets[n])))
                for at, name in enumerate(sets[n]):
                    where[name] = (x, names.index(name), n, at)
        halos = [
            [lax.ppermute(to_next, "tm", plan.halo(1)), lax.ppermute(to_prev, "tm", plan.halo(-1))]
            for _, to_next, to_prev in packs
        ]
        wait = [packs[min(2, len(sets) - 1)][1]] + (halos[1] if len(sets) > 2 else [])
        q = share(select(plan, place, [item(("q", h)) for h in range(heads)], wait))

        def send(n, after):
            x = hold(packs[n][0], after) if after else packs[n][0]
            x = lax.all_to_all(x, "tm", 0, 0, axis_index_groups=plan.lines(), tiled=True)
            return (x, *halos[n])

        def run(chosen, wait):
            args = []
            for h in chosen:
                kv = [where[name] for name in (("k", h), ("v", h))]
                args.append((q, h, *((x, at, recvs[n], of) for x, at, n, of in kv)))
            return list(attend(plan, room, place, pos, args, wait))

        recvs, out, first, begun = [], [], [], min(2, heads - 1)
        for n in range(len(sets)):
            after = halos[n - 1] if n else []
            if len(sets) > 2 and n == len(sets) - 2:
                after = after + q[:1]
            if len(sets) > 2 and n == len(sets) - 1:
                first = run(range(begun), [])
                after = after + halos[n] + first
            recvs.append(send(n, after))
        if begun:
            out = [merge(plan, place, share(first or run(range(begun), [])), 0, out)]
        for h in range(begun, heads - 1, 2):
            chosen = range(h, min(h + 2, heads - 1))
            out = [merge(plan, place, share(run(chosen, [])), h, out)]
        return merge(plan, place, share(run([heads - 1], out)), heads - 1, out)

    forms = [functools.partial(with_room, room) for room in plan.rooms]
    if len(forms) == 1:
        return forms[0](opened)
    return lax.cond(most > plan.rooms[0], forms[1], forms[0], opened)


def solution(mesh):
    placed = (P("tm", "head"), P("tm", "head"), P("tm", "head"), P("head"), P("head"), P(), P())
    return jax.shard_map(
        local, mesh=mesh, in_specs=placed, out_specs=P("tm", "head"), check_vma=False
    )
```

```python
import functools
import math

import jax
import jax.numpy as jnp
from jax import lax
from jax.experimental import pallas as pl
from jax.experimental.pallas import tpu as pltpu
from jax.sharding import PartitionSpec as P

HEAD_DIM = 128
BLOCK = 64
NFAR = 12
EPSILON = 1e-06
MASKED = -1e30
VMEM_LIMIT = 56 * 1024 * 1024


class Plan:
    def __init__(self, frames, rows, heads):
        self.frames, self.rows = frames, rows
        self.group = 4 if heads % 4 == 0 and frames % 4 == 0 else 1
        self.planes = frames // self.group
        self.blocks = rows // BLOCK
        self.heads = heads // self.group
        bands = sum(2**band <= frames - 1 for band in range(1, NFAR // 2 + 1))
        self.slots = [*range(bands), *range(NFAR // 2, NFAR // 2 + bands)]
        full = self.group * self.group
        self.rooms = [full * 14 // 16, full] if self.group > 1 else [full]
        self.near0 = self.blocks
        self.far0 = self.blocks * (self.group + 2)

    def total(self, room):
        return self.far0 + self.planes * room

    def halo(self, step):
        step *= self.group
        return [(i, i + step) for i in range(self.frames) if 0 <= i + step < self.frames]

    def swap(self, j):
        g = self.group
        return [(i, i // g * g + (i % g ^ j)) for i in range(self.frames)]

    def lines(self):
        g = self.group
        return [[p * g + i for p in range(self.planes)] for i in range(g)]


def params():
    return dict(
        compiler_params=pltpu.CompilerParams(vmem_limit_bytes=VMEM_LIMIT),
        cost_estimate=pl.CostEstimate(flops=1, bytes_accessed=1, transcendentals=0),
    )


def select_body(scaled, n_after, group, place_ref, *refs):
    outs = refs[len(refs) - group :]
    refs = list(refs[: len(refs) - group - n_after])
    values = []
    for with_scale in scaled:
        x = refs.pop(0)[...]
        if with_scale:
            rs, gain = refs.pop(0), refs.pop(0)
            x = x.astype(jnp.float32) * rs[...] * gain[...]
        values.append(x.astype(jnp.bfloat16))
    for j, out in enumerate(outs):

        @pl.when(pl.program_id(0) == j)
        def _(out=out):
            for item, x in enumerate(values):
                out[item] = x


def select(plan, place, items, after):
    args, specs = [], []
    for x, head, rs, gain in items:

        def at(j, place, head=head):
            return 0, (place[1] ^ j) * plan.heads + head

        args.append(x)
        specs.append(pl.BlockSpec((plan.rows, HEAD_DIM), at))
        if rs is not None:
            args += [rs, gain]
            specs.append(pl.BlockSpec((plan.rows, 1), lambda j, place: (0, 0)))
            specs.append(pl.BlockSpec((1, HEAD_DIM), at))
    shape = (len(items), plan.rows, HEAD_DIM)
    scaled = [rs is not None for _, _, rs, _ in items]
    return pl.pallas_call(
        functools.partial(select_body, scaled, len(after), plan.group),
        grid_spec=pltpu.PrefetchScalarGridSpec(
            num_scalar_prefetch=1,
            grid=(plan.group,),
            in_specs=specs + [pl.BlockSpec(memory_space=pl.ANY)] * len(after),
            out_specs=[pl.BlockSpec(shape, lambda j, place: (0, 0, 0))] * plan.group,
        ),
        out_shape=[jax.ShapeDtypeStruct(shape, jnp.bfloat16)] * plan.group,
        name="select",
        **params(),
    )(place, *args, *after)


def pack_body(plan, keep, n_extra, place_ref, slot_ref, *refs):
    group, blocks = plan.group, plan.blocks
    xs = refs[:group]
    extra = refs[group : group + n_extra]
    far, to_next, to_prev, sem = refs[group + n_extra :]
    plane, lane = place_ref[0], place_ref[1]
    whole = slot_ref.shape[0] > plan.planes
    stride, from_plane = (plan.planes, plane) if whole else (1, 0)

    def halo(act):
        for j in range(group):
            for at, (g, out) in enumerate(((group - 1, to_next), (0, to_prev))):

                @pl.when((lane ^ j) == g)
                def _(j=j, at=at, out=out):
                    begin = out.shape[0] - keep
                    own = xs[j].at[0:keep]
                    place = sem.at[plan.planes, 2 * at]
                    act(pltpu.make_async_copy(own, out.at[begin : begin + keep], place))
                    if extra:
                        place = sem.at[plan.planes, 2 * at + 1]
                        act(pltpu.make_async_copy(extra[j], out.at[0:begin], place))

    def for_each(act):
        halo(act)

        def one_plane(dest, carry):
            for j in range(group):
                for b in range(blocks):
                    slot = slot_ref[dest * stride + from_plane, (lane ^ j) * blocks + b]

                    @pl.when(slot >= 0)
                    def _(j=j, b=b, slot=slot):
                        dst = pl.ds(pl.multiple_of(slot * BLOCK, BLOCK), BLOCK)
                        src = xs[j].at[:, b * BLOCK : (b + 1) * BLOCK, :]
                        place = sem.at[dest, j * blocks + b]
                        act(pltpu.make_async_copy(src, far.at[dest, :, dst, :], place))

            return carry

        lax.fori_loop(0, plan.planes, one_plane, 0)

    for_each(lambda copy: copy.start())
    for_each(lambda copy: copy.wait())


def pack(plan, room, place, slots, xs, first, count, keep, extra):
    smem = pl.BlockSpec(memory_space=pltpu.SMEM)
    any_spec = pl.BlockSpec(memory_space=pl.ANY)
    frames = keep + (2 if extra else 0)
    frame = jax.ShapeDtypeStruct((frames, plan.rows, HEAD_DIM), jnp.bfloat16)
    far = jax.ShapeDtypeStruct((plan.planes, count, room * BLOCK, HEAD_DIM), jnp.bfloat16)
    return pl.pallas_call(
        functools.partial(pack_body, plan, keep, len(extra)),
        grid=(1,),
        in_specs=[smem, smem]
        + [pl.BlockSpec((count, plan.rows, HEAD_DIM), lambda i: (first // count, 0, 0))] * plan.group
        + [pl.BlockSpec((2, plan.rows, HEAD_DIM), lambda i: (1, 0, 0))] * len(extra),
        out_specs=[any_spec] * 3,
        out_shape=[far, frame, frame],
        scratch_shapes=[pltpu.SemaphoreType.DMA((plan.planes + 1, plan.group * plan.blocks))],
        name="pack",
        **params(),
    )(place, slots, *xs, *extra)


def hold_body(*refs):
    pass


def hold(x, after):
    any_spec = pl.BlockSpec(memory_space=pl.ANY)
    return pl.pallas_call(
        hold_body,
        in_specs=[any_spec] * (1 + len(after)),
        out_specs=any_spec,
        out_shape=jax.ShapeDtypeStruct(x.shape, x.dtype),
        input_output_aliases={0: 0},
        name="hold",
        **params(),
    )(x, *after)


def attend_body(plan, room, heads, n_wait, *refs):
    place_ref, pos_ref = refs[:2]
    group, rows, nfar = plan.group, plan.rows, len(plan.slots)
    step = 3 * group + 6
    inputs = [refs[2 + h * step : 2 + (h + 1) * step] for h in range(len(heads))]
    refs = refs[2 + len(heads) * step + n_wait :]
    outs, scratch = refs[:group], refs[group:]
    qbuf, kvbuf, obuf, fark, farv, *bufs, sem, out_sem = scratch
    sbufs, mbufs = bufs[:2], bufs[2:]
    plane, lane = place_ref[0], place_ref[1]
    scale = math.log2(math.e) / math.sqrt(HEAD_DIM)
    tile = rows // 2
    per_tile = tile // BLOCK
    lanes = lax.broadcasted_iota(jnp.int32, (1, nfar * BLOCK), 1) // BLOCK
    contract = (((1,), (1,)), ((), ()))

    def copies(h):
        made, slot = [], h % 2
        qs, rest = inputs[h][:group], inputs[h][group:]
        at_q, *at_kv = heads[h]

        def add(src, dst):
            made.append(pltpu.make_async_copy(src, dst, sem.at[slot, len(made)]))

        for j in range(group):
            add(qs[j].at[at_q], qbuf.at[slot, lane ^ j])
        for which, (item, of_set, of_near) in enumerate(at_kv):
            xs, (far, before, after) = rest[:group], rest[group : group + 3]
            rest = rest[group + 3 :]

            def at(first, count, which=which):
                first = first * BLOCK
                if not isinstance(first, int):
                    first = pl.multiple_of(first, BLOCK)
                return kvbuf.at[slot, which, pl.ds(first, count * BLOCK), :]

            for j in range(group):
                add(xs[j].at[item], at(plan.near0 + (lane ^ j) * plan.blocks, plan.blocks))
            add(before.at[of_near], at(0, plan.blocks))
            add(after.at[of_near], at(plan.near0 + group * plan.blocks, plan.blocks))
            for p in range(plan.planes):
                add(far.at[p, of_set], at(plan.far0 + p * room, room))
        return made

    def score(h, f, t):
        slot = h % 2
        first = pl.multiple_of((plan.near0 + (f - 1) * plan.blocks) * BLOCK, BLOCK)
        q = qbuf[slot, f, t * tile : (t + 1) * tile, :]
        peak = None
        for part in range(3):
            k = kvbuf[slot, 0, pl.ds(first + part * rows, rows), :]
            s = lax.dot_general(q, k, contract, preferred_element_type=jnp.float32)
            sbufs[t][:, part * rows : (part + 1) * rows] = s
            s = functools.reduce(
                jnp.maximum, [s[:, c : c + HEAD_DIM] for c in range(0, rows, HEAD_DIM)]
            )
            ok = there(f, part)
            if ok is not None:
                s = jnp.where(ok, s, MASKED)
            peak = s if peak is None else jnp.maximum(peak, s)
        for i in range(per_tile):
            block = t * per_tile + i
            ok = lanes < 0
            for n in range(nfar):
                at = pos_ref[(f * plan.blocks + block) * nfar + n]
                src = pl.ds(pl.multiple_of(jnp.maximum(at, 0) * BLOCK, BLOCK), BLOCK)
                fark[block, n * BLOCK : (n + 1) * BLOCK, :] = kvbuf[slot, 0, src, :]
                farv[block, n * BLOCK : (n + 1) * BLOCK, :] = kvbuf[slot, 1, src, :]
                ok = ok | ((lanes == n) & (at >= 0))
            some = slice(i * BLOCK, (i + 1) * BLOCK)
            s = lax.dot_general(
                q[some], fark[block], contract, preferred_element_type=jnp.float32
            )
            s = jnp.where(ok, s, MASKED)
            sbufs[t][some, 3 * rows :] = s
            s = functools.reduce(
                jnp.maximum, [s[:, c : c + HEAD_DIM] for c in range(0, nfar * BLOCK, HEAD_DIM)]
            )
            mbufs[t][some, :] = jnp.maximum(peak[some], s)

    def there(f, part):
        frame = plane * group + f
        return (frame > 0, None, frame < plan.frames - 1)[part]

    def weigh(h, f, t):
        slot = h % 2
        first = pl.multiple_of((plan.near0 + (f - 1) * plan.blocks) * BLOCK, BLOCK)
        peak = jnp.max(mbufs[t][...], axis=1, keepdims=True)
        total, out = 0.0, 0.0
        for part in range(3):
            ok = there(f, part)
            less = peak if ok is None else jnp.where(ok, peak, -MASKED)
            p = jnp.exp2((sbufs[t][:, part * rows : (part + 1) * rows] - less) * scale)
            total += jnp.sum(p, axis=1, keepdims=True)
            v = kvbuf[slot, 1, pl.ds(first + part * rows, rows), :]
            out += jnp.dot(p.astype(jnp.bfloat16), v, preferred_element_type=jnp.float32)
        p = jnp.exp2((sbufs[t][:, 3 * rows :] - peak) * scale)
        total += jnp.sum(p, axis=1, keepdims=True)
        p = p.astype(jnp.bfloat16)
        far_out = [
            jnp.dot(
                p[i * BLOCK : (i + 1) * BLOCK],
                farv[t * per_tile + i],
                preferred_element_type=jnp.float32,
            )
            for i in range(per_tile)
        ]
        out = (out + jnp.concatenate(far_out, axis=0)) / total
        obuf[f, h, t * tile : (t + 1) * tile, :] = out.astype(jnp.bfloat16)

    def one_frame(f, h):
        score(h, f, 1)
        weigh(h, f, 0)
        score(h, jnp.minimum(f + 1, group - 1), 0)
        weigh(h, f, 1)

    for copy in copies(0):
        copy.start()
    for h in range(len(heads)):
        if h + 1 < len(heads):
            for copy in copies(h + 1):
                copy.start()
        for copy in copies(h):
            copy.wait()
        score(h, 0, 0)
        lax.fori_loop(0, group, lambda f, c, h=h: (one_frame(f, h), c)[1], 0)
    made = []
    for j in range(group):
        made.append(pltpu.make_async_copy(obuf.at[lane ^ j], outs[j], out_sem.at[j]))
    for copy in made:
        copy.start()
    for copy in made:
        copy.wait()


def attend(plan, room, place, pos, heads, wait):
    nfar, count = len(plan.slots), len(heads)
    any_spec = pl.BlockSpec(memory_space=pl.ANY)
    smem = pl.BlockSpec(memory_space=pltpu.SMEM)
    args, items = [], []
    for q, at_q, *kv in heads:
        args += q
        items.append((at_q, *((item, *of) for _, item, _, *of in kv)))
        for xs, _, recv, *_ in kv:
            args += [*xs, *recv]
    shape = jax.ShapeDtypeStruct((count, plan.rows, HEAD_DIM), jnp.bfloat16)
    return pl.pallas_call(
        functools.partial(attend_body, plan, room, items, len(wait)),
        in_specs=[smem, smem] + [any_spec] * (len(args) + len(wait)),
        out_specs=[any_spec] * plan.group,
        out_shape=[shape] * plan.group,
        scratch_shapes=[
            pltpu.VMEM((2, plan.group, plan.rows, HEAD_DIM), jnp.bfloat16),
            pltpu.VMEM((2, 2, plan.total(room) * BLOCK, HEAD_DIM), jnp.bfloat16),
            pltpu.VMEM((plan.group, count, plan.rows, HEAD_DIM), jnp.bfloat16),
            pltpu.VMEM((plan.blocks, nfar * BLOCK, HEAD_DIM), jnp.bfloat16),
            pltpu.VMEM((plan.blocks, nfar * BLOCK, HEAD_DIM), jnp.bfloat16),
            pltpu.VMEM((plan.rows // 2, 3 * plan.rows + nfar * BLOCK), jnp.float32),
            pltpu.VMEM((plan.rows // 2, 3 * plan.rows + nfar * BLOCK), jnp.float32),
            pltpu.VMEM((plan.rows // 2, HEAD_DIM), jnp.float32),
            pltpu.VMEM((plan.rows // 2, HEAD_DIM), jnp.float32),
            pltpu.SemaphoreType.DMA((2, 3 * plan.group + 2 * (2 + plan.planes))),
            pltpu.SemaphoreType.DMA((plan.group,)),
        ],
        name="attend",
        **params(),
    )(place, pos, *args, *wait)


def merge_body(plan, first, place_ref, *refs):
    xs, (out, sem) = refs[: plan.group], refs[-2:]
    copies = []
    for j, x in enumerate(xs):
        for h in range(x.shape[0]):
            start = ((place_ref[1] ^ j) * plan.heads + first + h) * HEAD_DIM
            dst = out.at[:, pl.ds(pl.multiple_of(start, HEAD_DIM), HEAD_DIM)]
            copies.append(pltpu.make_async_copy(x.at[h], dst, sem.at[len(copies)]))
    for copy in copies:
        copy.start()
    for copy in copies:
        copy.wait()


def merge(plan, place, xs, first, out):
    width = plan.group * plan.heads * HEAD_DIM
    any_spec = pl.BlockSpec(memory_space=pl.ANY)
    vmem = pl.BlockSpec(memory_space=pltpu.VMEM)
    return pl.pallas_call(
        functools.partial(merge_body, plan, first),
        in_specs=[pl.BlockSpec(memory_space=pltpu.SMEM)]
        + [vmem] * plan.group
        + [any_spec] * len(out),
        out_specs=any_spec,
        out_shape=jax.ShapeDtypeStruct((plan.rows, width), jnp.bfloat16),
        input_output_aliases={1 + plan.group: 0} if out else {},
        scratch_shapes=[pltpu.SemaphoreType.DMA((plan.group * xs[0].shape[0],))],
        name="merge",
        **params(),
    )(place, *xs, *out)


def far_plan(plan, plane, far_frames, far_pick):
    group, blocks, frames, planes = plan.group, plan.blocks, plan.frames, plan.planes
    own = group * blocks
    lists = jnp.concatenate([far_frames[:, s : s + 1] for s in plan.slots], axis=1)
    every = jnp.arange(frames, dtype=jnp.int32)
    used = jnp.any(lists.reshape(frames, -1)[:, :, None] == every, axis=1)
    away = every[None, :] - (every // group * group)[:, None]
    used = used & ((away < -1) | (away > group))
    picked = far_pick[:, :, None] == jnp.arange(blocks, dtype=jnp.int32)
    needed = jnp.any((used[:, :, None] & picked).reshape(planes, group, frames, blocks), axis=1)
    needed = needed.reshape(planes * planes, own)
    before = (jnp.arange(own)[:, None] < jnp.arange(own)[None, :]).astype(jnp.float32)
    slot = jnp.dot(needed.astype(jnp.float32), before, precision=lax.Precision.HIGHEST)
    slot = jnp.where(needed, slot.astype(jnp.int32), -1)
    most = jnp.max(slot) + 1

    mine = lax.dynamic_slice_in_dim(lists, plane * own, own, 0)
    g = jnp.maximum(mine, 0)
    rows = lax.dynamic_slice_in_dim(far_pick, plane * group, group, 0)
    rows = jnp.repeat(rows, blocks, axis=0)
    pick = jnp.sum(jnp.where(g[:, :, None] == every, rows[:, None, :], 0), axis=2)
    come = lax.dynamic_slice_in_dim(slot, plane * planes, planes, 0).reshape(-1)
    hit = (g * blocks + pick)[:, :, None] == jnp.arange(frames * blocks, dtype=jnp.int32)
    come = jnp.sum(jnp.where(hit, come, 0), axis=2)
    away = g - plane * group
    near = jnp.where((away >= -1) & (away <= group), plan.near0 + away * blocks + pick, -2)
    near = jnp.where(mine >= 0, near, -1)
    if planes > 8:
        slot = slot.reshape(planes, planes, own)
        slot = lax.dynamic_slice_in_dim(slot, plane, 1, 1).reshape(planes, own)
    return most, slot, g // group, come, near


def local(query, key, value, q_gain, k_gain, far_frames, far_pick):
    rows, width = query.shape
    full_width = width * lax.axis_size("head")
    plan = Plan(lax.axis_size("tm"), rows, width // HEAD_DIM)
    frame = lax.axis_index("tm").astype(jnp.int32)
    plane = frame // plan.group
    place = jnp.stack([plane, frame % plan.group])

    def share(xs):
        return [xs[0]] + [lax.ppermute(xs[j], "tm", plan.swap(j)) for j in range(1, plan.group)]

    sums = jnp.stack([jnp.sum(jnp.square(x.astype(jnp.float32)), axis=1) for x in (query, key)])
    q_rs, k_rs = lax.rsqrt(lax.psum(sums, "head") / full_width + EPSILON)[:, :, None]
    q_gain, k_gain = q_gain[None, :], k_gain[None, :]

    def item(name):
        kind, h = name
        if kind == "k":
            return key, h, k_rs, k_gain
        return (value, h, None, None) if kind == "v" else (query, h, q_rs, q_gain)

    heads = plan.heads
    early = min(2, heads)
    opening = [("v", h) for h in range(early)]
    second = [("k", h) for h in range(early)] + [(n, h) for h in range(2, heads)[:1] for n in "kv"]
    sets = [opening, second] + [[("k", h), ("v", h)] for h in range(3, heads)]
    rounds = [[0], [1]] + [list(range(n, min(n + 2, len(sets)))) for n in range(2, len(sets), 2)]
    opened = share(select(plan, place, [item(name) for name in opening], []))
    most, slots, source, come, near = far_plan(plan, plane, far_frames, far_pick)

    def with_room(room, x):
        far = plan.far0 + source * room + come
        pos = jnp.where(near == -2, far, near).reshape(-1)
        packs, where = [], {}
        for index, chosen in enumerate(rounds):
            names = [name for n in chosen for name in sets[n]]
            if index:
                wait = packs[rounds[index - 1][0]][1:2]
                x = share(select(plan, place, [item(name) for name in names], wait))
            for n in chosen:
                own = len(sets[n])
                late = len(sets) > 2 and n == 1
                keep = early if late else own
                extra = carried if n == 2 else []
                if late:
                    carried = x
                begin = names.index(sets[n][0])
                packs.append(pack(plan, room, place, slots, x, begin, own, keep, extra))
                for at, name in enumerate(sets[n]):
                    of_near = (2, at - keep) if at >= keep else (n, at + (2 if extra else 0))
                    where[name] = (x, names.index(name), n, at, *of_near)
        queries = [item(("q", h)) for h in range(heads)]
        q = share(select(plan, place, queries, packs[min(2, len(sets) - 1)][1:2]))
        halos = [
            [lax.ppermute(to_next, "tm", plan.halo(1)), lax.ppermute(to_prev, "tm", plan.halo(-1))]
            for _, to_next, to_prev in packs
        ]

        def send(n, after):
            x = hold(packs[n][0], after) if after else packs[n][0]
            x = lax.all_to_all(x, "tm", 0, 0, axis_index_groups=plan.lines(), tiled=True)
            return x

        def run(chosen, wait):
            args = []
            for h in chosen:
                kv = [where[name] for name in (("k", h), ("v", h))]
                args.append(
                    (q, h, *((x, at, (recvs[n], *halos[m]), *of) for x, at, n, of_n, m, of_m in kv for of in [(of_n, of_m)]))
                )
            return list(attend(plan, room, place, pos, args, wait))

        recvs, out, first, begun = [], [], [], min(2, heads - 1)
        for n in range(len(sets)):
            after = halos[n - 1] if n else []
            if len(sets) > 2 and n == len(sets) - 2:
                after = after + q
            if len(sets) > 2 and n == len(sets) - 1:
                first = run(range(begun), [])
                after = after + halos[n] + first
            recvs.append(send(n, after))
        if begun:
            out = [merge(plan, place, share(first or run(range(begun), [])), 0, out)]
        for h in range(begun, heads - 1, 2):
            chosen = range(h, min(h + 2, heads - 1))
            out = [merge(plan, place, share(run(chosen, [])), h, out)]
        return merge(plan, place, share(run([heads - 1], out)), heads - 1, out)

    forms = [functools.partial(with_room, room) for room in plan.rooms]
    if len(forms) == 1:
        return forms[0](opened)
    return lax.cond(most > plan.rooms[0], forms[1], forms[0], opened)


def solution(mesh):
    placed = (P("tm", "head"), P("tm", "head"), P("tm", "head"), P("head"), P("head"), P(), P())
    return jax.shard_map(
        local, mesh=mesh, in_specs=placed, out_specs=P("tm", "head"), check_vma=False
    )
```

```python
import functools
import math

import jax
import jax.numpy as jnp
from jax import lax
from jax.experimental import pallas as pl
from jax.experimental.pallas import tpu as pltpu
from jax.sharding import PartitionSpec as P

HEAD_DIM = 128
BLOCK = 64
NFAR = 12
EPSILON = 1e-06
MASKED = -1e30
VMEM_LIMIT = 56 * 1024 * 1024


class Plan:
    def __init__(self, frames, rows, heads):
        self.frames, self.rows = frames, rows
        self.group = 4 if heads % 4 == 0 and frames % 4 == 0 else 1
        self.planes = frames // self.group
        self.blocks = rows // BLOCK
        self.heads = heads // self.group
        bands = sum(2**band <= frames - 1 for band in range(1, NFAR // 2 + 1))
        self.slots = [*range(bands), *range(NFAR // 2, NFAR // 2 + bands)]
        full = self.group * self.group
        self.rooms = [full * 14 // 16, full] if self.group > 1 else [full]
        self.near0 = self.blocks
        self.far0 = self.blocks * (self.group + 2)

    def total(self, room):
        return self.far0 + self.planes * room

    def halo(self, step):
        step *= self.group
        return [(i, i + step) for i in range(self.frames) if 0 <= i + step < self.frames]

    def swap(self, j):
        g = self.group
        return [(i, i // g * g + (i % g ^ j)) for i in range(self.frames)]

    def lines(self):
        g = self.group
        return [[p * g + i for p in range(self.planes)] for i in range(g)]


def params():
    return dict(
        compiler_params=pltpu.CompilerParams(vmem_limit_bytes=VMEM_LIMIT),
        cost_estimate=pl.CostEstimate(flops=1, bytes_accessed=1, transcendentals=0),
    )


def select_body(scaled, n_after, group, place_ref, *refs):
    outs = refs[len(refs) - group :]
    refs = list(refs[: len(refs) - group - n_after])
    values = []
    for with_scale in scaled:
        x = refs.pop(0)[...]
        if with_scale:
            rs, gain = refs.pop(0), refs.pop(0)
            x = x.astype(jnp.float32) * rs[...] * gain[...]
        values.append(x.astype(jnp.bfloat16))
    for j, out in enumerate(outs):

        @pl.when(pl.program_id(0) == j)
        def _(out=out):
            for item, x in enumerate(values):
                out[item] = x


def select(plan, place, items, after):
    args, specs = [], []
    for x, head, rs, gain in items:

        def at(j, place, head=head):
            return 0, (place[1] ^ j) * plan.heads + head

        args.append(x)
        specs.append(pl.BlockSpec((plan.rows, HEAD_DIM), at))
        if rs is not None:
            args += [rs, gain]
            specs.append(pl.BlockSpec((plan.rows, 1), lambda j, place: (0, 0)))
            specs.append(pl.BlockSpec((1, HEAD_DIM), at))
    shape = (len(items), plan.rows, HEAD_DIM)
    scaled = [rs is not None for _, _, rs, _ in items]
    return pl.pallas_call(
        functools.partial(select_body, scaled, len(after), plan.group),
        grid_spec=pltpu.PrefetchScalarGridSpec(
            num_scalar_prefetch=1,
            grid=(plan.group,),
            in_specs=specs + [pl.BlockSpec(memory_space=pl.ANY)] * len(after),
            out_specs=[pl.BlockSpec(shape, lambda j, place: (0, 0, 0))] * plan.group,
        ),
        out_shape=[jax.ShapeDtypeStruct(shape, jnp.bfloat16)] * plan.group,
        name="select",
        **params(),
    )(place, *args, *after)


def pack_body(plan, place_ref, slot_ref, *refs):
    group, blocks = plan.group, plan.blocks
    xs = refs[:group]
    far, to_next, to_prev, sem = refs[group:]
    plane, lane = place_ref[0], place_ref[1]
    whole = slot_ref.shape[0] > plan.planes
    stride, from_plane = (plan.planes, plane) if whole else (1, 0)

    def halo(act):
        for j in range(group):
            for at, (g, out) in enumerate(((group - 1, to_next), (0, to_prev))):

                @pl.when((lane ^ j) == g)
                def _(j=j, at=at, out=out):
                    act(pltpu.make_async_copy(xs[j], out, sem.at[plan.planes, at]))

    def for_each(act):
        halo(act)

        def one_plane(n, carry):
            dest = n + jnp.where(n >= plane, 1, 0)
            for j in range(group):
                for b in range(blocks):
                    slot = slot_ref[dest * stride + from_plane, (lane ^ j) * blocks + b]

                    @pl.when(slot >= 0)
                    def _(j=j, b=b, slot=slot):
                        dst = pl.ds(pl.multiple_of(slot * BLOCK, BLOCK), BLOCK)
                        src = xs[j].at[:, b * BLOCK : (b + 1) * BLOCK, :]
                        place = sem.at[dest, j * blocks + b]
                        act(pltpu.make_async_copy(src, far.at[dest, :, dst, :], place))

            return carry

        lax.fori_loop(0, plan.planes - 1, one_plane, 0)

    for_each(lambda copy: copy.start())
    for_each(lambda copy: copy.wait())


def pack(plan, room, place, slots, xs, first, count):
    smem = pl.BlockSpec(memory_space=pltpu.SMEM)
    any_spec = pl.BlockSpec(memory_space=pl.ANY)
    frame = jax.ShapeDtypeStruct((count, plan.rows, HEAD_DIM), jnp.bfloat16)
    far = jax.ShapeDtypeStruct((plan.planes, count, room * BLOCK, HEAD_DIM), jnp.bfloat16)
    return pl.pallas_call(
        functools.partial(pack_body, plan),
        grid=(1,),
        in_specs=[smem, smem]
        + [pl.BlockSpec((count, plan.rows, HEAD_DIM), lambda i: (first // count, 0, 0))] * plan.group,
        out_specs=[any_spec] * 3,
        out_shape=[far, frame, frame],
        scratch_shapes=[pltpu.SemaphoreType.DMA((plan.planes + 1, plan.group * plan.blocks))],
        name="pack",
        **params(),
    )(place, slots, *xs)


def hold_body(*refs):
    pass


def hold(x, after):
    any_spec = pl.BlockSpec(memory_space=pl.ANY)
    return pl.pallas_call(
        hold_body,
        in_specs=[any_spec] * (1 + len(after)),
        out_specs=any_spec,
        out_shape=jax.ShapeDtypeStruct(x.shape, x.dtype),
        input_output_aliases={0: 0},
        name="hold",
        **params(),
    )(x, *after)


def attend_body(plan, room, heads, n_wait, *refs):
    place_ref, pos_ref = refs[:2]
    group, rows, nfar = plan.group, plan.rows, len(plan.slots)
    step = 3 * group + 6
    inputs = [refs[2 + h * step : 2 + (h + 1) * step] for h in range(len(heads))]
    refs = refs[2 + len(heads) * step + n_wait :]
    outs, scratch = refs[:group], refs[group:]
    qbuf, kvbuf, obuf, fark, farv, *bufs, sem, out_sem = scratch
    sbufs, mbufs = bufs[:2], bufs[2:]
    plane, lane = place_ref[0], place_ref[1]
    scale = math.log2(math.e) / math.sqrt(HEAD_DIM)
    tile = rows // 2
    per_tile = tile // BLOCK
    lanes = lax.broadcasted_iota(jnp.int32, (1, nfar * BLOCK), 1) // BLOCK
    contract = (((1,), (1,)), ((), ()))

    def copies(h):
        made, slot = [], h % 2
        qs, rest = inputs[h][:group], inputs[h][group:]
        at_q, *at_kv = heads[h]

        def add(src, dst):
            made.append(pltpu.make_async_copy(src, dst, sem.at[slot, len(made)]))

        for j in range(group):
            add(qs[j].at[at_q], qbuf.at[slot, lane ^ j])
        for which, (item, of_set) in enumerate(at_kv):
            xs, (far, before, after) = rest[:group], rest[group : group + 3]
            rest = rest[group + 3 :]

            def at(first, count, which=which):
                first = first * BLOCK
                if not isinstance(first, int):
                    first = pl.multiple_of(first, BLOCK)
                return kvbuf.at[slot, which, pl.ds(first, count * BLOCK), :]

            for j in range(group):
                add(xs[j].at[item], at(plan.near0 + (lane ^ j) * plan.blocks, plan.blocks))
            add(before.at[of_set], at(0, plan.blocks))
            add(after.at[of_set], at(plan.near0 + group * plan.blocks, plan.blocks))
            for p in range(plan.planes):
                add(far.at[p, of_set], at(plan.far0 + p * room, room))
        return made

    def score(h, f, t):
        slot = h % 2
        first = pl.multiple_of((plan.near0 + (f - 1) * plan.blocks) * BLOCK, BLOCK)
        q = qbuf[slot, f, t * tile : (t + 1) * tile, :]
        peak = None
        for part in range(3):
            k = kvbuf[slot, 0, pl.ds(first + part * rows, rows), :]
            s = lax.dot_general(q, k, contract, preferred_element_type=jnp.float32)
            sbufs[t][:, part * rows : (part + 1) * rows] = s
            s = functools.reduce(
                jnp.maximum, [s[:, c : c + HEAD_DIM] for c in range(0, rows, HEAD_DIM)]
            )
            ok = there(f, part)
            if ok is not None:
                s = jnp.where(ok, s, MASKED)
            peak = s if peak is None else jnp.maximum(peak, s)
        for i in range(per_tile):
            block = t * per_tile + i
            ok = lanes < 0
            for n in range(nfar):
                at = pos_ref[(f * plan.blocks + block) * nfar + n]
                src = pl.ds(pl.multiple_of(jnp.maximum(at, 0) * BLOCK, BLOCK), BLOCK)
                fark[block, n * BLOCK : (n + 1) * BLOCK, :] = kvbuf[slot, 0, src, :]
                farv[block, n * BLOCK : (n + 1) * BLOCK, :] = kvbuf[slot, 1, src, :]
                ok = ok | ((lanes == n) & (at >= 0))
            some = slice(i * BLOCK, (i + 1) * BLOCK)
            s = lax.dot_general(
                q[some], fark[block], contract, preferred_element_type=jnp.float32
            )
            s = jnp.where(ok, s, MASKED)
            sbufs[t][some, 3 * rows :] = s
            s = functools.reduce(
                jnp.maximum, [s[:, c : c + HEAD_DIM] for c in range(0, nfar * BLOCK, HEAD_DIM)]
            )
            mbufs[t][some, :] = jnp.maximum(peak[some], s)

    def there(f, part):
        frame = plane * group + f
        return (frame > 0, None, frame < plan.frames - 1)[part]

    def weigh(h, f, t):
        slot = h % 2
        first = pl.multiple_of((plan.near0 + (f - 1) * plan.blocks) * BLOCK, BLOCK)
        peak = jnp.max(mbufs[t][...], axis=1, keepdims=True)
        total, out = 0.0, 0.0
        for part in range(3):
            ok = there(f, part)
            less = peak if ok is None else jnp.where(ok, peak, -MASKED)
            p = jnp.exp2((sbufs[t][:, part * rows : (part + 1) * rows] - less) * scale)
            total += jnp.sum(p, axis=1, keepdims=True)
            v = kvbuf[slot, 1, pl.ds(first + part * rows, rows), :]
            out += jnp.dot(p.astype(jnp.bfloat16), v, preferred_element_type=jnp.float32)
        p = jnp.exp2((sbufs[t][:, 3 * rows :] - peak) * scale)
        total += jnp.sum(p, axis=1, keepdims=True)
        p = p.astype(jnp.bfloat16)
        far_out = [
            jnp.dot(
                p[i * BLOCK : (i + 1) * BLOCK],
                farv[t * per_tile + i],
                preferred_element_type=jnp.float32,
            )
            for i in range(per_tile)
        ]
        out = (out + jnp.concatenate(far_out, axis=0)) / total
        obuf[f, h, t * tile : (t + 1) * tile, :] = out.astype(jnp.bfloat16)

    def one_frame(f, h):
        score(h, f, 1)
        weigh(h, f, 0)
        score(h, jnp.minimum(f + 1, group - 1), 0)
        weigh(h, f, 1)

    for copy in copies(0):
        copy.start()
    for h in range(len(heads)):
        if h + 1 < len(heads):
            for copy in copies(h + 1):
                copy.start()
        for copy in copies(h):
            copy.wait()
        score(h, 0, 0)
        lax.fori_loop(0, group, lambda f, c, h=h: (one_frame(f, h), c)[1], 0)
    made = []
    for j in range(group):
        made.append(pltpu.make_async_copy(obuf.at[lane ^ j], outs[j], out_sem.at[j]))
    for copy in made:
        copy.start()
    for copy in made:
        copy.wait()


def attend(plan, room, place, pos, heads, wait):
    nfar, count = len(plan.slots), len(heads)
    any_spec = pl.BlockSpec(memory_space=pl.ANY)
    smem = pl.BlockSpec(memory_space=pltpu.SMEM)
    args, items = [], []
    for q, at_q, *kv in heads:
        args += q
        items.append((at_q, *((item, of_set) for _, item, _, of_set in kv)))
        for xs, _, recv, _ in kv:
            args += [*xs, *recv]
    shape = jax.ShapeDtypeStruct((count, plan.rows, HEAD_DIM), jnp.bfloat16)
    return pl.pallas_call(
        functools.partial(attend_body, plan, room, items, len(wait)),
        in_specs=[smem, smem] + [any_spec] * (len(args) + len(wait)),
        out_specs=[any_spec] * plan.group,
        out_shape=[shape] * plan.group,
        scratch_shapes=[
            pltpu.VMEM((2, plan.group, plan.rows, HEAD_DIM), jnp.bfloat16),
            pltpu.VMEM((2, 2, plan.total(room) * BLOCK, HEAD_DIM), jnp.bfloat16),
            pltpu.VMEM((plan.group, count, plan.rows, HEAD_DIM), jnp.bfloat16),
            pltpu.VMEM((plan.blocks, nfar * BLOCK, HEAD_DIM), jnp.bfloat16),
            pltpu.VMEM((plan.blocks, nfar * BLOCK, HEAD_DIM), jnp.bfloat16),
            pltpu.VMEM((plan.rows // 2, 3 * plan.rows + nfar * BLOCK), jnp.float32),
            pltpu.VMEM((plan.rows // 2, 3 * plan.rows + nfar * BLOCK), jnp.float32),
            pltpu.VMEM((plan.rows // 2, HEAD_DIM), jnp.float32),
            pltpu.VMEM((plan.rows // 2, HEAD_DIM), jnp.float32),
            pltpu.SemaphoreType.DMA((2, 3 * plan.group + 2 * (2 + plan.planes))),
            pltpu.SemaphoreType.DMA((plan.group,)),
        ],
        name="attend",
        **params(),
    )(place, pos, *args, *wait)


def merge_body(plan, first, place_ref, *refs):
    xs, (out, sem) = refs[: plan.group], refs[-2:]
    copies = []
    for j, x in enumerate(xs):
        for h in range(x.shape[0]):
            start = ((place_ref[1] ^ j) * plan.heads + first + h) * HEAD_DIM
            dst = out.at[:, pl.ds(pl.multiple_of(start, HEAD_DIM), HEAD_DIM)]
            copies.append(pltpu.make_async_copy(x.at[h], dst, sem.at[len(copies)]))
    for copy in copies:
        copy.start()
    for copy in copies:
        copy.wait()


def merge(plan, place, xs, first, out):
    width = plan.group * plan.heads * HEAD_DIM
    any_spec = pl.BlockSpec(memory_space=pl.ANY)
    vmem = pl.BlockSpec(memory_space=pltpu.VMEM)
    return pl.pallas_call(
        functools.partial(merge_body, plan, first),
        in_specs=[pl.BlockSpec(memory_space=pltpu.SMEM)]
        + [vmem] * plan.group
        + [any_spec] * len(out),
        out_specs=any_spec,
        out_shape=jax.ShapeDtypeStruct((plan.rows, width), jnp.bfloat16),
        input_output_aliases={1 + plan.group: 0} if out else {},
        scratch_shapes=[pltpu.SemaphoreType.DMA((plan.group * xs[0].shape[0],))],
        name="merge",
        **params(),
    )(place, *xs, *out)


def far_plan(plan, plane, far_frames, far_pick):
    group, blocks, frames, planes = plan.group, plan.blocks, plan.frames, plan.planes
    own = group * blocks
    lists = jnp.concatenate([far_frames[:, s : s + 1] for s in plan.slots], axis=1)
    every = jnp.arange(frames, dtype=jnp.int32)
    used = jnp.any(lists.reshape(frames, -1)[:, :, None] == every, axis=1)
    away = every[None, :] - (every // group * group)[:, None]
    used = used & ((away < -1) | (away > group))
    picked = far_pick[:, :, None] == jnp.arange(blocks, dtype=jnp.int32)
    needed = jnp.any((used[:, :, None] & picked).reshape(planes, group, frames, blocks), axis=1)
    needed = needed.reshape(planes * planes, own)
    before = (jnp.arange(own)[:, None] < jnp.arange(own)[None, :]).astype(jnp.float32)
    slot = jnp.dot(needed.astype(jnp.float32), before, precision=lax.Precision.HIGHEST)
    slot = jnp.where(needed, slot.astype(jnp.int32), -1)
    most = jnp.max(slot) + 1

    mine = lax.dynamic_slice_in_dim(lists, plane * own, own, 0)
    g = jnp.maximum(mine, 0)
    rows = lax.dynamic_slice_in_dim(far_pick, plane * group, group, 0)
    rows = jnp.repeat(rows, blocks, axis=0)
    pick = jnp.sum(jnp.where(g[:, :, None] == every, rows[:, None, :], 0), axis=2)
    come = lax.dynamic_slice_in_dim(slot, plane * planes, planes, 0).reshape(-1)
    hit = (g * blocks + pick)[:, :, None] == jnp.arange(frames * blocks, dtype=jnp.int32)
    come = jnp.sum(jnp.where(hit, come, 0), axis=2)
    away = g - plane * group
    near = jnp.where((away >= -1) & (away <= group), plan.near0 + away * blocks + pick, -2)
    near = jnp.where(mine >= 0, near, -1)
    if planes > 8:
        slot = slot.reshape(planes, planes, own)
        slot = lax.dynamic_slice_in_dim(slot, plane, 1, 1).reshape(planes, own)
    return most, slot, g // group, come, near


def local(query, key, value, q_gain, k_gain, far_frames, far_pick):
    rows, width = query.shape
    full_width = width * lax.axis_size("head")
    plan = Plan(lax.axis_size("tm"), rows, width // HEAD_DIM)
    frame = lax.axis_index("tm").astype(jnp.int32)
    plane = frame // plan.group
    place = jnp.stack([plane, frame % plan.group])

    def share(xs):
        return [xs[0]] + [lax.ppermute(xs[j], "tm", plan.swap(j)) for j in range(1, plan.group)]

    sums = jnp.stack([jnp.sum(jnp.square(x.astype(jnp.float32)), axis=1) for x in (query, key)])
    q_rs, k_rs = lax.rsqrt(lax.psum(sums, "head") / full_width + EPSILON)[:, :, None]
    q_gain, k_gain = q_gain[None, :], k_gain[None, :]

    def item(name):
        kind, h = name
        if kind == "k":
            return key, h, k_rs, k_gain
        return (value, h, None, None) if kind == "v" else (query, h, q_rs, q_gain)

    heads = plan.heads
    early = min(2, heads)
    opening = [("v", h) for h in range(early)]
    second = [("k", h) for h in range(early)] + [(n, h) for h in range(2, heads)[:1] for n in "kv"]
    sets = [opening, second] + [[("k", h), ("v", h)] for h in range(3, heads)]
    rounds = [[0], [1]] + [list(range(n, min(n + 2, len(sets)))) for n in range(2, len(sets), 2)]
    opened = share(select(plan, place, [item(name) for name in opening], []))
    most, slots, source, come, near = far_plan(plan, plane, far_frames, far_pick)

    def with_room(room, x):
        far = plan.far0 + source * room + come
        pos = jnp.where(near == -2, far, near).reshape(-1)
        packs, where = [], {}
        for index, chosen in enumerate(rounds):
            names = [name for n in chosen for name in sets[n]]
            if index:
                wait = packs[rounds[index - 1][0]][1:2]
                x = share(select(plan, place, [item(name) for name in names], wait))
            for n in chosen:
                packs.append(pack(plan, room, place, slots, x, names.index(sets[n][0]), len(sets[n])))
                for at, name in enumerate(sets[n]):
                    where[name] = (x, names.index(name), n, at)
        queries = [item(("q", h)) for h in range(heads)]
        q = share(select(plan, place, queries, packs[min(2, len(sets) - 1)][1:2]))
        halos = [
            [lax.ppermute(to_next, "tm", plan.halo(1)), lax.ppermute(to_prev, "tm", plan.halo(-1))]
            for _, to_next, to_prev in packs
        ]

        def send(n, after):
            x = hold(packs[n][0], after) if after else packs[n][0]
            x = lax.all_to_all(x, "tm", 0, 0, axis_index_groups=plan.lines(), tiled=True)
            return (x, *halos[n])

        def run(chosen, wait):
            args = []
            for h in chosen:
                kv = [where[name] for name in (("k", h), ("v", h))]
                args.append((q, h, *((x, at, recvs[n], of) for x, at, n, of in kv)))
            return list(attend(plan, room, place, pos, args, wait))

        recvs, out, first, begun = [], [], [], min(2, heads - 1)
        for n in range(len(sets)):
            after = halos[n - 1] if n else []
            if len(sets) > 2 and n == len(sets) - 2:
                after = after + q
            if len(sets) > 2 and n == len(sets) - 1:
                first = run(range(begun), [])
                after = after + halos[n] + first
            recvs.append(send(n, after))
        wait = []
        if begun:
            wait = share(first or run(range(begun), []))
            out = [merge(plan, place, wait, 0, out)]
        for h in range(begun, heads - 1, 2):
            chosen = range(h, min(h + 2, heads - 1))
            wait = share(run(chosen, []))
            out = [merge(plan, place, wait, h, out)]
        return merge(plan, place, share(run([heads - 1], wait)), heads - 1, out)

    forms = [functools.partial(with_room, room) for room in plan.rooms]
    if len(forms) == 1:
        return forms[0](opened)
    return lax.cond(most > plan.rooms[0], forms[1], forms[0], opened)


def solution(mesh):
    placed = (P("tm", "head"), P("tm", "head"), P("tm", "head"), P("head"), P("head"), P(), P())
    return jax.shard_map(
        local, mesh=mesh, in_specs=placed, out_specs=P("tm", "head"), check_vma=False
    )
```
